32 devices in a mesh: clip: 2 (over x), gz: 16 (over z, y, core).
Axes of the slice: x: 2, y: 2, z: 4, core: 2. Of those that a mesh axis runs over, the one named last changes fastest.
Arguments:
- source_term: float32 [2, 128, 64, 128], P(None, ('clip', 'gz')), parts along dimension 1, may hold values from -24 to 24
- material: int32 [128, 64, 128], P(('clip', 'gz')), parts along dimension 0, may hold values from 0 to 2
- orders: int32 [2, 1024], P(None, 'gz'), may hold values from -22 to 22
Outputs:
- solution: float32 [2, 128, 64, 128], P(None, ('clip', 'gz')), parts along dimension 1
- residual: float32 [2, 128, 64, 128], P(None, ('clip', 'gz')), parts along dimension 1
- pupil_orders: float32 [2, 2048], P(None, ('clip', 'gz')), parts along dimension 1
The draws below stay inside these ranges and needn't reach their ends.
There are 2 independent parts, one for each index of `clip`. The reference program is written for one: setup_inputs(seed, part) draws one part's arguments, and reference() takes and returns one part's arrays. A program takes and returns all parts, laid end to end along the dimension named above; an argument that names none is the same for every part. Nothing has to cross between parts.
All inputs are finite; a program needn't handle non-finite values.
Results may differ from the reference program's by a relative error of at most 0.0003.
Values sent between devices are 32-bit elements; how exact they have to be, the bound alone decides.
A program may use at most 128 MiB of HBM per device.

```python
import math
import jax
import jax.numpy as jnp
from jax import lax

NX = 64
NY = 128
LEVELS = 3
SWEEPS = 2
COARSE_SWEEPS = 4
ORD_HALF = 22
ORDERS = 1024
NZ = 64


def draw_source_term(key, part):
    planes = jnp.arange(NZ, dtype=jnp.float32)
    profile = 1.0 + 2.0 * planes / max(NZ - 1, 1)
    profile = profile[None, :, None, None]
    base = 2.0 * jnp.clip(jax.random.normal(key, (2, NZ, NX, NY), jnp.float32), -4.0, 4.0)
    return base * profile


def touch_ends(entries, key, smallest, high):
    longest = entries.shape.index(max(entries.shape))
    spots = []
    for shift in (0, 1):
        where = [jax.random.randint(jax.random.fold_in(key, axis), (), 0, length) for axis, length in enumerate(entries.shape)]
        where[longest] = (where[longest] + shift) % entries.shape[longest]
        spots.append(tuple(where))
    return entries.at[spots[0]].set(smallest).at[spots[1]].set(high)


def setup_inputs(seed: int = 0, part: int = 0) -> dict:
    streams_of = jax.random.split(jax.random.key(seed), 4)
    own_keys = jax.random.split(jax.random.fold_in(streams_of[3], part), 4)
    return {
        "source_term": draw_source_term(jax.random.fold_in(jax.random.fold_in(streams_of[3], part), 71), part),
        "material": touch_ends(jax.random.randint(own_keys[1], (NZ, NX, NY), 0, 3), jax.random.fold_in(own_keys[1], 1), 0, 2).astype(jnp.int32),
        "orders": touch_ends(jax.random.randint(streams_of[2], (2, ORDERS), 0 - ORD_HALF, ORD_HALF + 1), jax.random.fold_in(streams_of[2], 1), 0 - ORD_HALF, ORD_HALF).astype(jnp.int32),
    }


HELM_TABLE = ((-0.5, 0.0), (1.0, -1.4), (-1.2, 0.0))
SHIFT_TABLE = ((-0.5, -0.25), (1.0, -0.25 * math.sqrt(11.84)), (-1.2, -0.6))
RELAX_WEIGHT = 0.8

def lookup(material, lookup_table):
    columns = []
    for member in range(2):
        chosen = jnp.where(material == 1, lookup_table[1][member], jnp.where(material == 2, lookup_table[2][member], lookup_table[0][member]))
        columns.append(chosen.astype(jnp.float32))
    return jnp.stack(columns)

def complex_mul(left_side, right_side):
    return jnp.stack([left_side[0] * right_side[0] - left_side[1] * right_side[1], left_side[0] * right_side[1] + left_side[1] * right_side[0]])

def divide_by(numer_real, numer_imag, denom_real, denom_imag):
    modulus = denom_real * denom_real + denom_imag * denom_imag
    return jnp.stack([(numer_real * denom_real + numer_imag * denom_imag) / modulus, (numer_imag * denom_real - numer_real * denom_imag) / modulus])

def neighbours(padded):
    middle = padded[:, 1:-1]
    summed = padded[:, 2:] + padded[:, :-2]
    summed = summed + jnp.roll(middle, 1, axis=2) + jnp.roll(middle, -1, axis=2)
    summed = summed + jnp.roll(middle, 1, axis=3) + jnp.roll(middle, -1, axis=3)
    return summed

def operate(padded, coefficient, factor):
    middle = padded[:, 1:-1]
    return (6.0 * middle - neighbours(padded)) * factor + complex_mul(coefficient, middle)

def inverse_diagonal(shift_field, factor):
    diag_real = 6.0 * factor + shift_field[0]
    diag_imag = shift_field[1]
    modulus = diag_real * diag_real + diag_imag * diag_imag
    return jnp.stack([diag_real / modulus, -diag_imag / modulus])

def pad_planes(values):
    return jnp.pad(values, ((0, 0), (1, 1), (0, 0), (0, 0)))

def restrict(values):
    planes, height, breadth = (values.shape[1], values.shape[2], values.shape[3])
    blocks = values.reshape(2, planes // 2, 2, height // 2, 2, breadth // 2, 2)
    return lax.optimization_barrier(jnp.mean(blocks, axis=(2, 4, 6)))

def prolong(values):
    for which_axis in (1, 2, 3):
        values = jnp.repeat(values, 2, axis=which_axis)
    return values

def relax_once(values, source, shift_field, inverse, factor, padded):
    remainder = source - operate(padded, shift_field, factor)
    return values + RELAX_WEIGHT * complex_mul(inverse, remainder)

def multigrid_cycle(source, shifts, inverses, grid_level):
    factor = 0.25 ** grid_level
    shift_field = shifts[grid_level]
    inverse = inverses[grid_level]
    values = RELAX_WEIGHT * complex_mul(inverse, source)
    if grid_level == LEVELS - 1:
        for sweep_index in range(COARSE_SWEEPS - 1):
            values = relax_once(values, source, shift_field, inverse, factor, pad_planes(values))
        return values
    for sweep_index in range(SWEEPS - 1):
        values = relax_once(values, source, shift_field, inverse, factor, pad_planes(values))
    remainder = source - operate(pad_planes(values), shift_field, factor)
    coarse = multigrid_cycle(restrict(remainder), shifts, inverses, grid_level + 1)
    values = values + prolong(coarse)
    for sweep_index in range(SWEEPS):
        values = relax_once(values, source, shift_field, inverse, factor, pad_planes(values))
    return values

def precise_dot(left_side, right_side):
    return jnp.dot(left_side, right_side, precision=lax.Precision.HIGHEST, preferred_element_type=jnp.float32)

def phase_table(length):
    positions = jnp.arange(length, dtype=jnp.int32)
    harmonics = jnp.arange(2 * ORD_HALF + 1, dtype=jnp.int32) - ORD_HALF
    phase_index = positions[:, None] * harmonics[None, :] % length
    angles = phase_index.astype(jnp.float32) * (2.0 * math.pi / length)
    return (jnp.cos(angles), -jnp.sin(angles))

def spectrum_of(plane):
    height = plane.shape[1]
    breadth = plane.shape[2]
    cos_x, sin_x = phase_table(height)
    cos_y, sin_y = phase_table(breadth)
    inner_real = precise_dot(plane[0], cos_y) - precise_dot(plane[1], sin_y)
    inner_imag = precise_dot(plane[0], sin_y) + precise_dot(plane[1], cos_y)
    outer_real = precise_dot(cos_x.T, inner_real) - precise_dot(sin_x.T, inner_imag)
    outer_imag = precise_dot(cos_x.T, inner_imag) + precise_dot(sin_x.T, inner_real)
    return jnp.stack([outer_real, outer_imag]) * (1.0 / math.sqrt(height * breadth))

def reference(source_term, material, orders):
    helm_coef = lookup(material, HELM_TABLE)
    shifts = [lookup(material, SHIFT_TABLE)]
    for grid_level in range(1, LEVELS):
        shifts.append(restrict(shifts[-1]))
    inverses = [inverse_diagonal(shifts[grid_level], 0.25 ** grid_level) for grid_level in range(LEVELS)]
    norm_sum = jnp.sum(source_term * source_term)
    direction = multigrid_cycle(source_term, shifts, inverses, 0)
    image_field = operate(pad_planes(direction), helm_coef, 1.0)
    cross_real = jnp.sum(source_term[0] * image_field[0] + source_term[1] * image_field[1])
    cross_imag = jnp.sum(source_term[0] * image_field[1] - source_term[1] * image_field[0])
    step_alpha = divide_by(norm_sum, 0.0, cross_real, cross_imag)
    halfway = source_term - complex_mul(step_alpha, image_field)
    corrected = multigrid_cycle(halfway, shifts, inverses, 0)
    last_image = operate(pad_planes(corrected), helm_coef, 1.0)
    along_real = jnp.sum(last_image[0] * halfway[0] + last_image[1] * halfway[1])
    along_imag = jnp.sum(last_image[0] * halfway[1] - last_image[1] * halfway[0])
    image_norm = jnp.sum(last_image * last_image)
    step_omega = divide_by(along_real, along_imag, image_norm, 0.0)
    solution = complex_mul(step_alpha, direction) + complex_mul(step_omega, corrected)
    residual = halfway - complex_mul(step_omega, last_image)
    spectrum = spectrum_of(solution[:, -1])
    pupil_orders = spectrum[:, orders[0] + ORD_HALF, orders[1] + ORD_HALF]
    return (solution, residual, pupil_orders)
```

```python
import functools
import math

import jax
import jax.numpy as jnp
import numpy as np
from jax import lax
from jax.experimental import pallas as pl
from jax.experimental.pallas import tpu as pltpu
from jax.sharding import PartitionSpec as P

ORD_HALF = 22
HELM_TABLE = ((-0.5, 0.0), (1.0, -1.4), (-1.2, 0.0))
SHIFT_TABLE = ((-0.5, -0.25), (1.0, -0.25 * math.sqrt(11.84)), (-1.2, -0.6))
RELAX = 0.8
REACH1 = 3
REACH2 = 5
HALF = 64
HARM = 48
F32 = jnp.float32


def weight_of(shift):
    bottom = complex(6.0 + shift[0], shift[1])
    value = RELAX / bottom
    return (value.real, value.imag)


WEIGHT_TABLE = tuple(weight_of(entry) for entry in SHIFT_TABLE)
DIAG_TABLE = tuple((6.0 + entry[0], entry[1]) for entry in SHIFT_TABLE)
IMAGE_TABLE = tuple((6.0 + entry[0], entry[1]) for entry in HELM_TABLE)


def pick(material, table):
    one = material == 1
    two = material == 2
    return tuple(
        jnp.where(one, table[1][k], jnp.where(two, table[2][k], table[0][k])).astype(F32)
        for k in range(2)
    )


def mul(ar, ai, br, bi):
    return ar * br - ai * bi, ar * bi + ai * br


def loop(lo, hi, body):
    def step(p, carry):
        body(p)
        return carry

    lax.fori_loop(lo, hi, step, 0)


def around(ref, k, p, lane_step):
    x = ref[k, p]
    rows = x.shape[0]
    lanes = x.shape[1]
    total = ref[k, p - 1] + ref[k, p + 1]
    total = total + (pltpu.roll(x, 1, 0) + pltpu.roll(x, rows - 1, 0))
    return total + (pltpu.roll(x, lane_step, 1) + pltpu.roll(x, lanes - lane_step, 1))


def first_sweep(dst, rhs, weight, p):
    r, i = mul(weight[0, p], weight[1, p], rhs[0, p], rhs[1, p])
    dst[0, p] = r
    dst[1, p] = i


def sweep(dst, old, rhs, weight, p, lane_step, h2):
    nr = around(old, 0, p, lane_step)
    ni = around(old, 1, p, lane_step)
    if h2 != 1.0:
        nr, ni = nr * h2, ni * h2
    r, i = mul(weight[0, p], weight[1, p], rhs[0, p] + nr, rhs[1, p] + ni)
    dst[0, p] = (1.0 - RELAX) * old[0, p] + r
    dst[1, p] = (1.0 - RELAX) * old[1, p] + i


def lane_iota(shape):
    return lax.broadcasted_iota(jnp.int32, shape, 1)


def pair_lanes(x, step):
    lanes = x.shape[1]
    low = (lane_iota(x.shape) & step) == 0
    return x + jnp.where(low, pltpu.roll(x, lanes - step, 1), pltpu.roll(x, step, 1))


def pair_rows(x, tmp):
    rows = x.shape[0]
    tmp[0:rows] = x
    return tmp[pl.ds(0, rows // 2, stride=2)] + tmp[pl.ds(1, rows // 2, stride=2)]


def spread_rows(x, tmp):
    rows = x.shape[0]
    tmp[pl.ds(0, rows, stride=2)] = x
    tmp[pl.ds(1, rows, stride=2)] = x
    return tmp[0 : 2 * rows]


def pack_two(r, i):
    return jnp.where((lane_iota(r.shape) & 1) == 0, r, i)


def unpack_two(x):
    lanes = x.shape[1]
    even = (lane_iota(x.shape) & 1) == 0
    return jnp.where(even, x, pltpu.roll(x, 1, 1)), jnp.where(even, pltpu.roll(x, lanes - 1, 1), x)


def pack_four(r, i):
    rows = r.shape[0] // 2
    top = pack_two(r[:rows], i[:rows])
    low = pack_two(r[rows:], i[rows:])
    return jnp.where((lane_iota(top.shape) & 2) == 0, top, low)


def unpack_four(x):
    lanes = x.shape[1]
    first = (lane_iota(x.shape) & 2) == 0
    halves = []
    for y in unpack_two(x):
        halves.append(
            (jnp.where(first, y, pltpu.roll(y, 2, 1)), jnp.where(first, pltpu.roll(y, lanes - 2, 1), y))
        )
    return halves


def invert(r, i):
    bottom = 1.0 / (r * r + i * i)
    return RELAX * r * bottom, -RELAX * i * bottom


def precise(a, b, dims):
    return lax.dot_general(
        a, b, (dims, ((), ())), precision=lax.Precision.HIGHEST, preferred_element_type=F32
    )


def spectrum_of(r, i, ty, tx):
    gr = precise(ty, r, ((1,), (1,)))
    gi = precise(ty, i, ((1,), (1,)))
    inner = jnp.concatenate([gr[:HALF] - gi[HALF:], gr[HALF:] + gi[:HALF]], axis=0)
    outer = precise(inner, tx, ((1,), (0,)))
    turned = pltpu.roll(outer[HALF:], HALF, 1)
    left = lane_iota(turned.shape) < HALF
    return (outer[:HALF] + jnp.where(left, -turned, turned))[:HARM]


def tables(nx, ny):
    harmonics = np.arange(2 * ORD_HALF + 1) - ORD_HALF
    count = harmonics.size
    ty = np.zeros((2 * HALF, ny), np.float32)
    angle = 2.0 * np.pi * ((harmonics[:, None] * np.arange(ny)[None, :]) % ny) / ny
    ty[:count] = np.cos(angle)
    ty[HALF : HALF + count] = -np.sin(angle)
    tx = np.zeros((nx, 2 * HALF), np.float32)
    angle = 2.0 * np.pi * ((np.arange(nx)[:, None] * harmonics[None, :]) % nx) / nx
    scale = 1.0 / math.sqrt(nx * ny)
    tx[:, :count] = np.cos(angle) * scale
    tx[:, HALF : HALF + count] = -np.sin(angle) * scale
    return ty, tx


def kernel(
    n, src, mat, ords, ty, tx, sol, res, pup,
    fx, gx, mx, w0, va, vb, d1, w1, f1, v1a, v1b, w2, f2, v2a, v2b, d2,
    pk1, pk2, tmp, red, spec,
    fine_send, fine_recv, k1_send, k1_recv, k2_send, k2_recv,
    red_send, red_recv, spec_send, spec_recv,
):
    me = lax.axis_index("gz")
    own = src.shape[1]
    depth = own
    half = own // 2
    mid1 = REACH1 * half
    sent = []

    def other(k):
        return {"gz": lax.rem(me + k + n, n)}

    def start(source, target, ssem, rsem, k):
        copy = pltpu.make_async_remote_copy(
            src_ref=source, dst_ref=target, send_sem=ssem, recv_sem=rsem,
            device_id=other(k), device_id_type=pl.DeviceIdType.MESH,
        )
        copy.start()
        sent.append(copy)
        return copy

    barrier = pltpu.get_barrier_semaphore()

    def greet(k):
        pl.semaphore_signal(
            barrier, inc=1, device_id={"gz": lax.rem(me + k, n)},
            device_id_type=pl.DeviceIdType.MESH,
        )

    loop(1, n, greet)

    def take(p):
        m = mat[p]
        mx[depth + p] = m
        fx[0, depth + p] = src[0, p]
        fx[1, depth + p] = src[1, p]

    loop(0, own, take)

    for p in range(half):
        a = pick(mat[2 * p], SHIFT_TABLE)
        b = pick(mat[2 * p + 1], SHIFT_TABLE)
        for k in range(2):
            d1[k, p] = 0.125 * pair_rows(pair_lanes(a[k] + b[k], 1), tmp)
        pk1[0, REACH1, p] = pack_two(d1[0, p], d1[1, p])
    for k in range(2):
        d2[k] = 0.125 * pair_rows(pair_lanes(d1[k, 0] + d1[k, 1], 2), tmp)
    pk2[0, REACH2] = pack_four(d2[0], d2[1])

    pl.semaphore_wait(barrier, n - 1)

    def send_planes(source, base, target, slot, near, dims):
        up_from = half if near else 0
        up_to = half if near else 0
        down_from = 0 if near else half
        down_to = depth + own + (0 if near else half)
        copies = []
        for which, (k, a, b) in enumerate(((1, up_from, up_to), (-1, down_from, down_to))):
            s = pl.ds(base + a, half)
            t = pl.ds(b, half)
            one = source.at[:, s] if dims else source.at[s]
            two = target.at[:, t] if dims else target.at[t]
            copies.append(
                start(one, two, fine_send.at[slot + which], fine_recv.at[slot + which], k)
            )
        return copies

    def send_one(which):
        copies = {}
        for k in range(1, REACH1 + 1):
            for d in (k, -k):
                at = which * (2 * REACH1 + 1) + REACH1 - d
                copies[-d] = start(
                    pk1.at[which, REACH1], pk1.at[which, REACH1 - d],
                    k1_send.at[at], k1_recv.at[at], d,
                )
        return copies

    def send_two(which):
        copies = {}
        for k in range(1, REACH2 + 1):
            for d in (k, -k):
                at = which * (2 * REACH2 + 1) + REACH2 - d
                copies[-d] = start(
                    pk2.at[which, REACH2], pk2.at[which, REACH2 - d],
                    k2_send.at[at], k2_recv.at[at], d,
                )
        return copies

    near_mat = send_planes(mat, 0, mx, 0, True, False)
    near_src = send_planes(src, 0, fx, 2, True, True)
    shifts1 = send_one(0)
    shifts2 = send_two(0)
    far_mat = send_planes(mat, 0, mx, 4, False, False)
    far_src = send_planes(src, 0, fx, 6, False, True)

    def inside(plane, count):
        return jnp.where(jnp.logical_and(plane >= 0, plane < count), 1.0, 0.0).astype(F32)

    def weight0(p):
        m = inside(me * own + p - depth, n * own)
        r, i = pick(mx[p], WEIGHT_TABLE)
        w0[0, p] = r * m
        w0[1, p] = i * m

    def weight1(p):
        r, i = unpack_two(pk1[0, p // half, p % half])
        r, i = invert(r + 1.5, i)
        m = inside(me * half + p - mid1, n * half)
        w1[0, p] = r * m
        w1[1, p] = i * m

    def weight2(p):
        (rt, rb), (it, ib) = unpack_four(pk2[0, p])
        rows = rt.shape[0]
        m = inside(me + p - REACH2, n)
        for at, (r, i) in enumerate(((rt, it), (rb, ib))):
            r, i = invert(r + 0.375, i)
            w2[0, p, at * rows : (at + 1) * rows] = r * m
            w2[1, p, at * rows : (at + 1) * rows] = i * m

    def take1(which):
        def body(p):
            r, i = unpack_two(pk1[which, p // half, p % half])
            f1[0, p] = r
            f1[1, p] = i

        return body

    def take2(which):
        def body(p):
            (rt, rb), (it, ib) = unpack_four(pk2[which, p])
            rows = rt.shape[0]
            f2[0, p, 0:rows] = rt
            f2[0, p, rows : 2 * rows] = rb
            f2[1, p, 0:rows] = it
            f2[1, p, rows : 2 * rows] = ib

        return body

    def cycle(which, f, near, far):
        begin, end = depth, depth + own
        if which == 1:
            for copy in near_mat:
                copy.wait_recv()
            loop(begin - 2, end + 2, weight0)
        for copy in near:
            copy.wait_recv()
        loop(begin - 2, end + 2, lambda p: first_sweep(va, f, w0, p))
        loop(begin - 1, end + 1, lambda p: sweep(vb, va, f, w0, p, 1, 1.0))

        def down(q):
            total = [None, None]
            for s in range(2):
                p = depth + 2 * q + s
                c = pick(mx[p], DIAG_TABLE)
                dr, di = mul(c[0], c[1], vb[0, p], vb[1, p])
                for k, d in enumerate((dr, di)):
                    e = (f[k, p] - d) + around(vb, k, p, 1)
                    total[k] = e if s == 0 else total[k] + e
            parts = [0.125 * pair_rows(pair_lanes(t, 1), tmp) for t in total]
            f1[0, mid1 + q] = parts[0]
            f1[1, mid1 + q] = parts[1]
            pk1[which, REACH1, q] = pack_two(parts[0], parts[1])

        for q in range(half):
            down(q)
        ones = send_one(which)

        if which == 1:
            for d in (-1, 1):
                shifts1[d].wait_recv()
            loop(mid1 - half, mid1 + 2 * half, weight1)

        for d in (-1, 1):
            ones[d].wait_recv()
        loop(mid1 - half, mid1, take1(which))
        loop(mid1 + half, mid1 + 2 * half, take1(which))
        loop(mid1 - 2, mid1 + half + 2, lambda p: first_sweep(v1a, f1, w1, p))
        loop(mid1 - 1, mid1 + half + 1, lambda p: sweep(v1b, v1a, f1, w1, p, 2, 0.25))

        parts = []
        total = [None, None]
        for q in range(half):
            p = mid1 + q
            dr, di = mul(d1[0, q] + 1.5, d1[1, q], v1b[0, p], v1b[1, p])
            for k, d in enumerate((dr, di)):
                e = (f1[k, p] - d) + 0.25 * around(v1b, k, p, 2)
                total[k] = e if q == 0 else total[k] + e
        parts = [0.125 * pair_rows(pair_lanes(t, 2), tmp) for t in total]
        pk2[which, REACH2] = pack_four(parts[0], parts[1])
        twos = send_two(which)

        if which == 1:
            for copy in far_mat:
                copy.wait_recv()
            loop(0, begin - 2, weight0)
            loop(end + 2, end + depth, weight0)
            for d in range(2, REACH1 + 1):
                shifts1[d].wait_recv()
                shifts1[-d].wait_recv()
            loop(1, mid1 - half, weight1)
            loop(mid1 + 2 * half, 2 * mid1 + half - 1, weight1)
        for d in range(2, REACH1 + 1):
            ones[d].wait_recv()
            ones[-d].wait_recv()
        loop(1, mid1 - half, take1(which))
        loop(mid1 + 2 * half, 2 * mid1 + half - 1, take1(which))
        loop(1, mid1 - 2, lambda p: first_sweep(v1a, f1, w1, p))
        loop(mid1 + half + 2, 2 * mid1 + half - 1, lambda p: first_sweep(v1a, f1, w1, p))
        loop(2, mid1 - 1, lambda p: sweep(v1b, v1a, f1, w1, p, 2, 0.25))
        loop(mid1 + half + 1, 2 * mid1 + half - 2, lambda p: sweep(v1b, v1a, f1, w1, p, 2, 0.25))
        for copy in far:
            copy.wait_recv()
        loop(0, begin - 2, lambda p: first_sweep(va, f, w0, p))
        loop(end + 2, end + depth, lambda p: first_sweep(va, f, w0, p))
        loop(1, begin - 1, lambda p: sweep(vb, va, f, w0, p, 1, 1.0))
        loop(end + 1, end + depth - 1, lambda p: sweep(vb, va, f, w0, p, 1, 1.0))
        if which == 1:
            for d in range(1, REACH2 + 1):
                shifts2[d].wait_recv()
                shifts2[-d].wait_recv()
            loop(0, 2 * REACH2 + 1, weight2)

        for d in range(1, REACH2 + 1):
            twos[d].wait_recv()
            twos[-d].wait_recv()
        loop(0, 2 * REACH2 + 1, take2(which))
        loop(0, 2 * REACH2 + 1, lambda p: first_sweep(v2a, f2, w2, p))
        loop(1, 2 * REACH2, lambda p: sweep(v2b, v2a, f2, w2, p, 4, 0.0625))
        loop(2, 2 * REACH2 - 1, lambda p: sweep(v2a, v2b, f2, w2, p, 4, 0.0625))
        loop(3, 2 * REACH2 - 2, lambda p: sweep(v2b, v2a, f2, w2, p, 4, 0.0625))

        def raise1(c):
            p = (c - REACH2 + REACH1) * half
            for k in range(2):
                x = spread_rows(v2b[k, c], tmp)
                v1b[k, p] = v1b[k, p] + x
                v1b[k, p + 1] = v1b[k, p + 1] + x

        loop(REACH2 - 2, REACH2 + 3, raise1)
        loop(mid1 - 3, mid1 + half + 3, lambda p: sweep(v1a, v1b, f1, w1, p, 2, 0.25))
        loop(mid1 - 2, mid1 + half + 2, lambda p: sweep(v1b, v1a, f1, w1, p, 2, 0.25))

        def raise0(c):
            p = depth + 2 * (c - mid1)
            for k in range(2):
                x = spread_rows(v1b[k, c], tmp)
                vb[k, p] = vb[k, p] + x
                vb[k, p + 1] = vb[k, p + 1] + x

        loop(mid1 - 2, mid1 + half + 2, raise0)
        loop(begin - 2, end + 2, lambda p: sweep(va, vb, f, w0, p, 1, 1.0))
        loop(begin - 1, end + 1, lambda p: sweep(vb, va, f, w0, p, 1, 1.0))

    def image_of(p):
        c = pick(mx[p], IMAGE_TABLE)
        r, i = mul(c[0], c[1], vb[0, p], vb[1, p])
        return r - around(vb, 0, p, 1), i - around(vb, 1, p, 1)

    def fold(x):
        rows, lanes = x.shape
        return jnp.sum(x.reshape(rows // 8, 8, lanes), axis=0)

    def share(which, sums):
        rows = [jnp.sum(s, axis=0, keepdims=True) for s in sums]
        rows.append(jnp.zeros((8 - len(rows), rows[0].shape[1]), F32))
        red[which, me] = jnp.concatenate(rows, axis=0)

        def post(k):
            pltpu.make_async_remote_copy(
                src_ref=red.at[which, me], dst_ref=red.at[which, me],
                send_sem=red_send.at[which, k], recv_sem=red_recv.at[which, k],
                device_id={"gz": lax.rem(me + k, n)}, device_id_type=pl.DeviceIdType.MESH,
            ).start()

        loop(1, n, post)

    def collect(which):
        def await_one(k):
            one = pltpu.make_async_remote_copy(
                src_ref=red.at[which, me], dst_ref=red.at[which, lax.rem(me + n - k, n)],
                send_sem=red_send.at[which, k], recv_sem=red_recv.at[which, k],
                device_id={"gz": lax.rem(me + k, n)}, device_id_type=pl.DeviceIdType.MESH,
            )
            one.wait_recv()
            one.wait_send()

        loop(1, n, await_one)
        total = red[which, 0]
        for j in range(1, n):
            total = total + red[which, j]
        total = jnp.sum(total, axis=1, keepdims=True)
        return total[0:1], total[1:2], total[2:3]

    def spectrum(which):
        def post(k):
            pltpu.make_async_remote_copy(
                src_ref=spec.at[which], dst_ref=spec.at[which],
                send_sem=spec_send.at[which, k], recv_sem=spec_recv.at[which],
                device_id={"gz": lax.rem(me + k, n)}, device_id_type=pl.DeviceIdType.MESH,
            ).start()

        @pl.when(me == n - 1)
        def _():
            last = depth + own - 1
            spec[which] = spectrum_of(vb[0, last], vb[1, last], ty[...], tx[...])
            loop(1, n, post)

    def orders_of(which):
        def settle(k):
            pltpu.make_async_remote_copy(
                src_ref=spec.at[which], dst_ref=spec.at[which],
                send_sem=spec_send.at[which, k], recv_sem=spec_recv.at[which],
                device_id={"gz": lax.rem(me + k, n)}, device_id_type=pl.DeviceIdType.MESH,
            ).wait_send()

        @pl.when(me == n - 1)
        def _():
            loop(1, n, settle)

        @pl.when(me != n - 1)
        def _():
            pltpu.make_async_remote_copy(
                src_ref=spec.at[which], dst_ref=spec.at[which],
                send_sem=spec_send.at[which, 0], recv_sem=spec_recv.at[which],
                device_id={"gz": lax.rem(me + 1, n)}, device_id_type=pl.DeviceIdType.MESH,
            ).wait_recv()

        count = ords.shape[1]
        x = ords[0:1] + ORD_HALF
        y = ords[1:2] + ORD_HALF
        row = lax.broadcasted_iota(jnp.int32, (2 * HALF, count), 0)
        pick_y = lax.broadcasted_iota(jnp.int32, (HARM, count), 0) == y
        out = []
        for k in range(2):
            pick_x = jnp.where(row == x + k * HALF, 1.0, 0.0).astype(F32)
            chosen = precise(spec[which], pick_x, ((1,), (0,)))
            out.append(jnp.sum(jnp.where(pick_y, chosen, 0.0), axis=0, keepdims=True))
        return out

    cycle(1, fx, near_src, far_src)

    zero = jnp.zeros((8, src.shape[3]), F32)
    sums = [zero, zero, zero]
    for p in range(own):
        r, i = image_of(depth + p)
        gx[0, depth + p] = r
        gx[1, depth + p] = i
        a, b = src[0, p], src[1, p]
        sums[0] = sums[0] + fold(a * a + b * b)
        sums[1] = sums[1] + fold(a * r + b * i)
        sums[2] = sums[2] + fold(a * i - b * r)
    near_img = send_planes(gx, depth, gx, 8, True, True)
    share(0, sums)
    far_img = send_planes(gx, depth, gx, 10, False, True)

    def keep(p):
        sol[0, p] = vb[0, depth + p]
        sol[1, p] = vb[1, depth + p]

    loop(0, own, keep)
    spectrum(0)

    cycle(2, gx, near_img, far_img)

    rho, cr, ci = collect(0)
    scale = rho / (cr * cr + ci * ci)
    ar, ai = cr * scale, -(ci * scale)

    sums = [zero, zero, zero]
    for p in range(own):
        e = depth + p
        r, i = image_of(e)
        gr, gi = gx[0, e], gx[1, e]
        tr, ti = mul(ar, ai, gr, gi)
        hr, hi = src[0, p] - tr, src[1, p] - ti
        tr, ti = mul(ar, ai, r, i)
        lr, li = gr - tr, gi - ti
        va[0, e], va[1, e] = lr, li
        res[0, p], res[1, p] = hr, hi
        sums[0] = sums[0] + fold(lr * hr + li * hi)
        sums[1] = sums[1] + fold(lr * hi - li * hr)
        sums[2] = sums[2] + fold(lr * lr + li * li)
    share(1, sums)
    spectrum(1)
    sdr, sdi = orders_of(0)

    along_r, along_i, norm = collect(1)
    wr, wi = along_r / norm, along_i / norm

    def finish(p):
        e = depth + p
        dr, di = sol[0, p], sol[1, p]
        tr, ti = mul(ar, ai, vb[0, e], vb[1, e])
        cr_, ci_ = mul(wr, wi, dr - tr, di - ti)
        xr, xi = mul(ar, ai, dr, di)
        sol[0, p], sol[1, p] = xr + cr_, xi + ci_
        tr, ti = mul(wr, wi, va[0, e], va[1, e])
        res[0, p], res[1, p] = res[0, p] - tr, res[1, p] - ti

    loop(0, own, finish)

    sqr, sqi = orders_of(1)
    tr, ti = mul(ar, ai, sqr, sqi)
    cr_, ci_ = mul(wr, wi, sdr - tr, sdi - ti)
    xr, xi = mul(ar, ai, sdr, sdi)
    pup[0:1] = xr + cr_
    pup[1:2] = xi + ci_

    for copy in sent:
        copy.wait_send()


def on_device(n, source_term, material, orders):
    own, nx, ny = material.shape
    half = own // 2
    ty, tx = tables(nx, ny)
    vm = pltpu.VMEM
    fine = vm((2, 3 * own, nx, ny), F32)
    planes1 = (2 * REACH1 + 1) * half
    one = vm((2, planes1, nx // 2, ny), F32)
    planes2 = 2 * REACH2 + 1
    two = vm((2, planes2, nx // 4, ny), F32)
    dma = pltpu.SemaphoreType.DMA
    ext1 = 3 * (2 * REACH1 + 1)
    ext2 = 3 * planes2
    whole = pl.BlockSpec(memory_space=pltpu.VMEM)
    return pl.pallas_call(
        functools.partial(kernel, n),
        out_shape=(
            jax.ShapeDtypeStruct(source_term.shape, F32),
            jax.ShapeDtypeStruct(source_term.shape, F32),
            jax.ShapeDtypeStruct(orders.shape, F32),
        ),
        in_specs=[whole] * 5,
        out_specs=(whole,) * 3,
        scratch_shapes=[
            fine, fine, vm((3 * own, nx, ny), jnp.int32), fine, fine, fine,
            vm((2, half, nx // 2, ny), F32), one, one, one, one,
            two, two, two, two, vm((2, nx // 4, ny), F32),
            vm((3, 2 * REACH1 + 1, half, nx // 2, ny), F32),
            vm((3, planes2, nx // 8, ny), F32),
            vm((nx, ny), F32),
            vm((2, n, 8, ny), F32),
            vm((2, HARM, 2 * HALF), F32),
            dma((12,)), dma((12,)), dma((ext1,)), dma((ext1,)), dma((ext2,)), dma((ext2,)),
            dma((2, n)), dma((2, n)), dma((2, n)), dma((2,)),
        ],
        compiler_params=pltpu.CompilerParams(
            collective_id=0, has_side_effects=True, vmem_limit_bytes=40 * 1024 * 1024
        ),
    )(source_term, material, orders, jnp.asarray(ty), jnp.asarray(tx))


def solution(mesh):
    return jax.shard_map(
        functools.partial(on_device, mesh.shape["gz"]),
        mesh=mesh,
        in_specs=(
            P(None, ("clip", "gz"), None, None),
            P(("clip", "gz"), None, None),
            P(None, "gz"),
        ),
        out_specs=(
            P(None, ("clip", "gz"), None, None),
            P(None, ("clip", "gz"), None, None),
            P(None, ("clip", "gz")),
        ),
        check_vma=False,
    )
```

```python
import functools
import math

import jax
import jax.numpy as jnp
import numpy as np
from jax import lax
from jax.experimental import pallas as pl
from jax.experimental.pallas import tpu as pltpu
from jax.sharding import PartitionSpec as P

ORD_HALF = 22
HELM_TABLE = ((-0.5, 0.0), (1.0, -1.4), (-1.2, 0.0))
SHIFT_TABLE = ((-0.5, -0.25), (1.0, -0.25 * math.sqrt(11.84)), (-1.2, -0.6))
RELAX = 0.8
REACH1 = 3
REACH2 = 5
HALF = 64
HARM = 48
F32 = jnp.float32


def weight_of(shift):
    bottom = complex(6.0 + shift[0], shift[1])
    value = RELAX / bottom
    return (value.real, value.imag)


WEIGHT_TABLE = tuple(weight_of(entry) for entry in SHIFT_TABLE)
DIAG_TABLE = tuple((6.0 + entry[0], entry[1]) for entry in SHIFT_TABLE)
IMAGE_TABLE = tuple((6.0 + entry[0], entry[1]) for entry in HELM_TABLE)


def pick(material, table):
    one = material == 1
    two = material == 2
    return tuple(
        jnp.where(one, table[1][k], jnp.where(two, table[2][k], table[0][k])).astype(F32)
        for k in range(2)
    )


def mul(ar, ai, br, bi):
    return ar * br - ai * bi, ar * bi + ai * br


def loop(lo, hi, body):
    def step(p, carry):
        body(p)
        return carry

    lax.fori_loop(lo, hi, step, 0)


def planes(lo, hi, group, dst, body):
    def some(first, count):
        values = [body(first + j) for j in range(count)]
        for j, (r, i) in enumerate(values):
            dst[0, first + j] = r
            dst[1, first + j] = i

    steps = (hi - lo) // group
    if steps == 1:
        some(lo, group)
    elif steps > 1:
        loop(0, steps, lambda t: some(lo + t * group, group))
    if (hi - lo) % group:
        some(lo + steps * group, (hi - lo) % group)


FINE, MIDDLE, COARSE = 2, 4, 6


def around(ref, k, p, lane_step):
    x = ref[k, p]
    rows = x.shape[0]
    lanes = x.shape[1]
    total = ref[k, p - 1] + ref[k, p + 1]
    total = total + (pltpu.roll(x, 1, 0) + pltpu.roll(x, rows - 1, 0))
    return total + (pltpu.roll(x, lane_step, 1) + pltpu.roll(x, lanes - lane_step, 1))


def first_sweep(lo, hi, group, dst, rhs, weight):
    planes(lo, hi, group, dst, lambda p: mul(weight[0, p], weight[1, p], rhs[0, p], rhs[1, p]))


def sweep(lo, hi, group, dst, old, rhs, weight, lane_step, h2):
    def body(p):
        nr = around(old, 0, p, lane_step)
        ni = around(old, 1, p, lane_step)
        if h2 != 1.0:
            nr, ni = nr * h2, ni * h2
        r, i = mul(weight[0, p], weight[1, p], rhs[0, p] + nr, rhs[1, p] + ni)
        return (1.0 - RELAX) * old[0, p] + r, (1.0 - RELAX) * old[1, p] + i

    planes(lo, hi, group, dst, body)


def lane_iota(shape):
    return lax.broadcasted_iota(jnp.int32, shape, 1)


def pair_lanes(x, step):
    lanes = x.shape[1]
    low = (lane_iota(x.shape) & step) == 0
    return x + jnp.where(low, pltpu.roll(x, lanes - step, 1), pltpu.roll(x, step, 1))


def pair_rows(x, tmp):
    rows = x.shape[0]
    tmp[0:rows] = x
    return tmp[pl.ds(0, rows // 2, stride=2)] + tmp[pl.ds(1, rows // 2, stride=2)]


def spread_rows(x, tmp):
    rows = x.shape[0]
    tmp[pl.ds(0, rows, stride=2)] = x
    tmp[pl.ds(1, rows, stride=2)] = x
    return tmp[0 : 2 * rows]


def pack_two(r, i):
    return jnp.where((lane_iota(r.shape) & 1) == 0, r, i)


def unpack_two(x):
    lanes = x.shape[1]
    even = (lane_iota(x.shape) & 1) == 0
    return jnp.where(even, x, pltpu.roll(x, 1, 1)), jnp.where(even, pltpu.roll(x, lanes - 1, 1), x)


def pack_four(r, i):
    rows = r.shape[0] // 2
    top = pack_two(r[:rows], i[:rows])
    low = pack_two(r[rows:], i[rows:])
    return jnp.where((lane_iota(top.shape) & 2) == 0, top, low)


def unpack_four(x):
    lanes = x.shape[1]
    first = (lane_iota(x.shape) & 2) == 0
    halves = []
    for y in unpack_two(x):
        halves.append(
            (jnp.where(first, y, pltpu.roll(y, 2, 1)), jnp.where(first, pltpu.roll(y, lanes - 2, 1), y))
        )
    return halves


def invert(r, i):
    bottom = 1.0 / (r * r + i * i)
    return RELAX * r * bottom, -RELAX * i * bottom


def precise(a, b, dims):
    return lax.dot_general(
        a, b, (dims, ((), ())), precision=lax.Precision.HIGHEST, preferred_element_type=F32
    )


def spectrum_of(r, i, ty, tx):
    gr = precise(ty, r, ((1,), (1,)))
    gi = precise(ty, i, ((1,), (1,)))
    inner = jnp.concatenate([gr[:HALF] - gi[HALF:], gr[HALF:] + gi[:HALF]], axis=0)
    outer = precise(inner, tx, ((1,), (0,)))
    turned = pltpu.roll(outer[HALF:], HALF, 1)
    left = lane_iota(turned.shape) < HALF
    return (outer[:HALF] + jnp.where(left, -turned, turned))[:HARM]


def tables(nx, ny):
    harmonics = np.arange(2 * ORD_HALF + 1) - ORD_HALF
    count = harmonics.size
    ty = np.zeros((2 * HALF, ny), np.float32)
    angle = 2.0 * np.pi * ((harmonics[:, None] * np.arange(ny)[None, :]) % ny) / ny
    ty[:count] = np.cos(angle)
    ty[HALF : HALF + count] = -np.sin(angle)
    tx = np.zeros((nx, 2 * HALF), np.float32)
    angle = 2.0 * np.pi * ((np.arange(nx)[:, None] * harmonics[None, :]) % nx) / nx
    scale = 1.0 / math.sqrt(nx * ny)
    tx[:, :count] = np.cos(angle) * scale
    tx[:, HALF : HALF + count] = -np.sin(angle) * scale
    return ty, tx


def kernel(
    n, src_in, mat_in, ords_in, ty_in, tx_in, sol, res, pup,
    ords, ty, tx, in_sem, fx, gx, mx, w0, va, vb, d1, w1, f1, v1a, v1b, w2, f2, v2a, v2b, d2,
    pk1, pk2, tmp, red, spec,
    fine_send, fine_recv, k1_send, k1_recv, k2_send, k2_recv,
    red_send, red_recv, spec_send, spec_recv,
):
    me = lax.axis_index("gz")
    own = mat_in.shape[0]
    depth = own
    half = own // 2
    mid1 = REACH1 * half
    sent = []

    def other(k):
        return {"gz": lax.rem(me + k + n, n)}

    def start(source, target, ssem, rsem, k):
        copy = pltpu.make_async_remote_copy(
            src_ref=source, dst_ref=target, send_sem=ssem, recv_sem=rsem,
            device_id=other(k), device_id_type=pl.DeviceIdType.MESH,
        )
        copy.start()
        sent.append(copy)
        return copy

    barrier = pltpu.get_barrier_semaphore()

    def greet(k):
        pl.semaphore_signal(
            barrier, inc=1, device_id={"gz": lax.rem(me + k, n)},
            device_id_type=pl.DeviceIdType.MESH,
        )

    loop(1, n, greet)

    src = fx.at[:, pl.ds(depth, own)]
    mat = mx.at[pl.ds(depth, own)]
    fetches = [
        pltpu.make_async_copy(a, b, in_sem.at[k])
        for k, (a, b) in enumerate(
            ((mat_in, mat), (src_in, src), (ords_in, ords), (ty_in, ty), (tx_in, tx))
        )
    ]
    for fetch in fetches:
        fetch.start()
    fetches[0].wait()

    for p in range(half):
        a = pick(mat[2 * p], SHIFT_TABLE)
        b = pick(mat[2 * p + 1], SHIFT_TABLE)
        for k in range(2):
            d1[k, p] = 0.125 * pair_rows(pair_lanes(a[k] + b[k], 1), tmp.at[2 * p + k])
        pk1[0, REACH1, p] = pack_two(d1[0, p], d1[1, p])
    for k in range(2):
        d2[k] = 0.125 * pair_rows(pair_lanes(d1[k, 0] + d1[k, 1], 2), tmp.at[k])
    pk2[0, REACH2] = pack_four(d2[0], d2[1])

    for fetch in fetches[1:]:
        fetch.wait()
    pl.semaphore_wait(barrier, n - 1)

    def send_planes(source, base, target, slot, near, dims):
        up_from = half if near else 0
        up_to = half if near else 0
        down_from = 0 if near else half
        down_to = depth + own + (0 if near else half)
        copies = []
        for which, (k, a, b) in enumerate(((1, up_from, up_to), (-1, down_from, down_to))):
            s = pl.ds(base + a, half)
            t = pl.ds(b, half)
            one = source.at[:, s] if dims else source.at[s]
            two = target.at[:, t] if dims else target.at[t]
            copies.append(
                start(one, two, fine_send.at[slot + which], fine_recv.at[slot + which], k)
            )
        return copies

    def send_one(which):
        copies = {}
        for k in range(1, REACH1 + 1):
            for d in (k, -k):
                at = which * (2 * REACH1 + 1) + REACH1 - d
                part = pl.ds(0, half)
                if k == REACH1:
                    part = pl.ds(half - 1 if d > 0 else 0, 1)
                copies[-d] = start(
                    pk1.at[which, REACH1, part], pk1.at[which, REACH1 - d, part],
                    k1_send.at[at], k1_recv.at[at], d,
                )
        return copies

    def send_two(which):
        copies = {}
        for k in range(1, REACH2 + 1):
            for d in (k, -k):
                at = which * (2 * REACH2 + 1) + REACH2 - d
                copies[-d] = start(
                    pk2.at[which, REACH2], pk2.at[which, REACH2 - d],
                    k2_send.at[at], k2_recv.at[at], d,
                )
        return copies

    near_mat = send_planes(mx, depth, mx, 0, True, False)
    near_src = send_planes(fx, depth, fx, 2, True, True)
    shifts1 = send_one(0)
    shifts2 = send_two(0)
    far_mat = send_planes(mx, depth, mx, 4, False, False)
    far_src = send_planes(fx, depth, fx, 6, False, True)

    def inside(plane, count):
        return jnp.where(jnp.logical_and(plane >= 0, plane < count), 1.0, 0.0).astype(F32)

    def weight0(p):
        m = inside(me * own + p - depth, n * own)
        r, i = pick(mx[p], WEIGHT_TABLE)
        return r * m, i * m

    def weight1(p):
        r, i = unpack_two(pk1[0, p // half, p % half])
        r, i = invert(r + 1.5, i)
        m = inside(me * half + p - mid1, n * half)
        return r * m, i * m

    def weight2(p):
        (rt, rb), (it, ib) = unpack_four(pk2[0, p])
        m = inside(me + p - REACH2, n)
        r, i = invert(jnp.concatenate([rt, rb]) + 0.375, jnp.concatenate([it, ib]))
        return r * m, i * m

    def take1(which):
        def body(p):
            return unpack_two(pk1[which, p // half, p % half])

        return body

    def take2(which):
        def body(p):
            (rt, rb), (it, ib) = unpack_four(pk2[which, p])
            return jnp.concatenate([rt, rb]), jnp.concatenate([it, ib])

        return body

    def cycle(which, f, near, far):
        begin, end = depth, depth + own
        if which == 1:
            for copy in near_mat:
                copy.wait_recv()
            planes(begin - 2, end + 2, FINE, w0, weight0)
        for copy in near:
            copy.wait_recv()
        first_sweep(begin - 2, end + 2, FINE, va, f, w0)
        sweep(begin - 1, end + 1, FINE, vb, va, f, w0, 1, 1.0)

        def down(q):
            total = [None, None]
            for s in range(2):
                p = depth + 2 * q + s
                c = pick(mx[p], DIAG_TABLE)
                dr, di = mul(c[0], c[1], vb[0, p], vb[1, p])
                for k, d in enumerate((dr, di)):
                    e = (f[k, p] - d) + around(vb, k, p, 1)
                    total[k] = e if s == 0 else total[k] + e
            parts = [
                0.125 * pair_rows(pair_lanes(t, 1), tmp.at[2 * q + k]) for k, t in enumerate(total)
            ]
            f1[0, mid1 + q] = parts[0]
            f1[1, mid1 + q] = parts[1]
            pk1[which, REACH1, q] = pack_two(parts[0], parts[1])

        for q in range(half):
            down(q)
        ones = send_one(which)

        if which == 1:
            for d in (-1, 1):
                shifts1[d].wait_recv()
            planes(mid1 - half, mid1 + 2 * half, MIDDLE, w1, weight1)

        for d in (-1, 1):
            ones[d].wait_recv()
        planes(mid1 - half, mid1, MIDDLE, f1, take1(which))
        planes(mid1 + half, mid1 + 2 * half, MIDDLE, f1, take1(which))
        first_sweep(mid1 - 2, mid1 + half + 2, MIDDLE, v1a, f1, w1)
        sweep(mid1 - 1, mid1 + half + 1, MIDDLE, v1b, v1a, f1, w1, 2, 0.25)

        parts = []
        total = [None, None]
        for q in range(half):
            p = mid1 + q
            dr, di = mul(d1[0, q] + 1.5, d1[1, q], v1b[0, p], v1b[1, p])
            for k, d in enumerate((dr, di)):
                e = (f1[k, p] - d) + 0.25 * around(v1b, k, p, 2)
                total[k] = e if q == 0 else total[k] + e
        parts = [0.125 * pair_rows(pair_lanes(t, 2), tmp.at[k]) for k, t in enumerate(total)]
        pk2[which, REACH2] = pack_four(parts[0], parts[1])
        twos = send_two(which)

        if which == 1:
            for copy in far_mat:
                copy.wait_recv()
            planes(0, begin - 2, FINE, w0, weight0)
            planes(end + 2, end + depth, FINE, w0, weight0)
            for d in range(2, REACH1 + 1):
                shifts1[d].wait_recv()
                shifts1[-d].wait_recv()
            planes(1, mid1 - half, MIDDLE, w1, weight1)
            planes(mid1 + 2 * half, 2 * mid1 + half - 1, MIDDLE, w1, weight1)
        for d in range(2, REACH1 + 1):
            ones[d].wait_recv()
            ones[-d].wait_recv()
        planes(1, mid1 - half, MIDDLE, f1, take1(which))
        planes(mid1 + 2 * half, 2 * mid1 + half - 1, MIDDLE, f1, take1(which))
        first_sweep(1, mid1 - 2, MIDDLE, v1a, f1, w1)
        first_sweep(mid1 + half + 2, 2 * mid1 + half - 1, MIDDLE, v1a, f1, w1)
        sweep(2, mid1 - 1, MIDDLE, v1b, v1a, f1, w1, 2, 0.25)
        sweep(mid1 + half + 1, 2 * mid1 + half - 2, MIDDLE, v1b, v1a, f1, w1, 2, 0.25)
        for copy in far:
            copy.wait_recv()
        first_sweep(0, begin - 2, FINE, va, f, w0)
        first_sweep(end + 2, end + depth, FINE, va, f, w0)
        sweep(1, begin - 1, FINE, vb, va, f, w0, 1, 1.0)
        sweep(end + 1, end + depth - 1, FINE, vb, va, f, w0, 1, 1.0)
        if which == 1:
            for d in range(1, REACH2 + 1):
                shifts2[d].wait_recv()
                shifts2[-d].wait_recv()
            planes(0, 2 * REACH2 + 1, COARSE, w2, weight2)

        for d in range(1, REACH2 + 1):
            twos[d].wait_recv()
            twos[-d].wait_recv()
        planes(0, 2 * REACH2 + 1, COARSE, f2, take2(which))
        first_sweep(0, 2 * REACH2 + 1, COARSE, v2a, f2, w2)
        sweep(1, 2 * REACH2, COARSE, v2b, v2a, f2, w2, 4, 0.0625)
        sweep(2, 2 * REACH2 - 1, COARSE, v2a, v2b, f2, w2, 4, 0.0625)
        sweep(3, 2 * REACH2 - 2, COARSE, v2b, v2a, f2, w2, 4, 0.0625)

        def raise1(c):
            p = (c - REACH2 + REACH1) * half
            for k in range(2):
                x = spread_rows(v2b[k, c], tmp.at[2 * (c % 2) + k])
                v1b[k, p] = v1b[k, p] + x
                v1b[k, p + 1] = v1b[k, p + 1] + x

        for c in range(REACH2 - 2, REACH2 + 3):
            raise1(c)
        sweep(mid1 - 3, mid1 + half + 3, MIDDLE, v1a, v1b, f1, w1, 2, 0.25)
        sweep(mid1 - 2, mid1 + half + 2, MIDDLE, v1b, v1a, f1, w1, 2, 0.25)

        def raise0(c):
            p = depth + 2 * (c - mid1)
            for k in range(2):
                x = spread_rows(v1b[k, c], tmp.at[2 * (c % 2) + k])
                vb[k, p] = vb[k, p] + x
                vb[k, p + 1] = vb[k, p + 1] + x

        for c in range(mid1 - 2, mid1 + half + 2):
            raise0(c)
        sweep(begin - 2, end + 2, FINE, va, vb, f, w0, 1, 1.0)
        sweep(begin - 1, end + 1, FINE, vb, va, f, w0, 1, 1.0)

    def image_of(p):
        c = pick(mx[p], IMAGE_TABLE)
        r, i = mul(c[0], c[1], vb[0, p], vb[1, p])
        return r - around(vb, 0, p, 1), i - around(vb, 1, p, 1)

    def fold(x):
        rows, lanes = x.shape
        return jnp.sum(x.reshape(rows // 8, 8, lanes), axis=0)

    def share(which, sums):
        rows = [jnp.sum(s, axis=0, keepdims=True) for s in sums]
        rows.append(jnp.zeros((8 - len(rows), rows[0].shape[1]), F32))
        red[which, me] = jnp.concatenate(rows, axis=0)

        def post(k):
            pltpu.make_async_remote_copy(
                src_ref=red.at[which, me], dst_ref=red.at[which, me],
                send_sem=red_send.at[which, k], recv_sem=red_recv.at[which, k],
                device_id={"gz": lax.rem(me + k, n)}, device_id_type=pl.DeviceIdType.MESH,
            ).start()

        loop(1, n, post)

    def collect(which):
        def await_one(k):
            one = pltpu.make_async_remote_copy(
                src_ref=red.at[which, me], dst_ref=red.at[which, lax.rem(me + n - k, n)],
                send_sem=red_send.at[which, k], recv_sem=red_recv.at[which, k],
                device_id={"gz": lax.rem(me + k, n)}, device_id_type=pl.DeviceIdType.MESH,
            )
            one.wait_recv()
            one.wait_send()

        loop(1, n, await_one)
        total = red[which, 0]
        for j in range(1, n):
            total = total + red[which, j]
        total = jnp.sum(total, axis=1, keepdims=True)
        return total[0:1], total[1:2], total[2:3]

    def spectrum(which):
        def post(k):
            pltpu.make_async_remote_copy(
                src_ref=spec.at[which], dst_ref=spec.at[which],
                send_sem=spec_send.at[which, k], recv_sem=spec_recv.at[which],
                device_id={"gz": lax.rem(me + k, n)}, device_id_type=pl.DeviceIdType.MESH,
            ).start()

        @pl.when(me == n - 1)
        def _():
            last = depth + own - 1
            spec[which] = spectrum_of(vb[0, last], vb[1, last], ty[...], tx[...])
            loop(1, n, post)

    def orders_of(which):
        def settle(k):
            pltpu.make_async_remote_copy(
                src_ref=spec.at[which], dst_ref=spec.at[which],
                send_sem=spec_send.at[which, k], recv_sem=spec_recv.at[which],
                device_id={"gz": lax.rem(me + k, n)}, device_id_type=pl.DeviceIdType.MESH,
            ).wait_send()

        @pl.when(me == n - 1)
        def _():
            loop(1, n, settle)

        @pl.when(me != n - 1)
        def _():
            pltpu.make_async_remote_copy(
                src_ref=spec.at[which], dst_ref=spec.at[which],
                send_sem=spec_send.at[which, 0], recv_sem=spec_recv.at[which],
                device_id={"gz": lax.rem(me + 1, n)}, device_id_type=pl.DeviceIdType.MESH,
            ).wait_recv()

        count = ords.shape[1]
        x = ords[0:1] + ORD_HALF
        y = ords[1:2] + ORD_HALF
        row = lax.broadcasted_iota(jnp.int32, (2 * HALF, count), 0)
        pick_y = lax.broadcasted_iota(jnp.int32, (HARM, count), 0) == y
        out = []
        for k in range(2):
            pick_x = jnp.where(row == x + k * HALF, 1.0, 0.0).astype(F32)
            chosen = precise(spec[which], pick_x, ((1,), (0,)))
            out.append(jnp.sum(jnp.where(pick_y, chosen, 0.0), axis=0, keepdims=True))
        return out

    cycle(1, fx, near_src, far_src)

    zero = jnp.zeros((8, fx.shape[3]), F32)
    sums = [zero, zero, zero]
    for p in range(own):
        r, i = image_of(depth + p)
        gx[0, depth + p] = r
        gx[1, depth + p] = i
        a, b = src[0, p], src[1, p]
        sums[0] = sums[0] + fold(a * a + b * b)
        sums[1] = sums[1] + fold(a * r + b * i)
        sums[2] = sums[2] + fold(a * i - b * r)
    near_img = send_planes(gx, depth, gx, 8, True, True)
    share(0, sums)
    far_img = send_planes(gx, depth, gx, 10, False, True)

    def keep(p):
        sol[0, p] = vb[0, depth + p]
        sol[1, p] = vb[1, depth + p]

    loop(0, own, keep)
    spectrum(0)

    cycle(2, gx, near_img, far_img)

    rho, cr, ci = collect(0)
    scale = rho / (cr * cr + ci * ci)
    ar, ai = cr * scale, -(ci * scale)

    sums = [zero, zero, zero]
    for p in range(own):
        e = depth + p
        r, i = image_of(e)
        gr, gi = gx[0, e], gx[1, e]
        tr, ti = mul(ar, ai, gr, gi)
        hr, hi = src[0, p] - tr, src[1, p] - ti
        tr, ti = mul(ar, ai, r, i)
        lr, li = gr - tr, gi - ti
        va[0, e], va[1, e] = lr, li
        res[0, p], res[1, p] = hr, hi
        sums[0] = sums[0] + fold(lr * hr + li * hi)
        sums[1] = sums[1] + fold(lr * hi - li * hr)
        sums[2] = sums[2] + fold(lr * lr + li * li)
    share(1, sums)
    spectrum(1)
    sdr, sdi = orders_of(0)

    along_r, along_i, norm = collect(1)
    wr, wi = along_r / norm, along_i / norm

    def finish(p):
        e = depth + p
        dr, di = sol[0, p], sol[1, p]
        tr, ti = mul(ar, ai, vb[0, e], vb[1, e])
        cr_, ci_ = mul(wr, wi, dr - tr, di - ti)
        xr, xi = mul(ar, ai, dr, di)
        sol[0, p], sol[1, p] = xr + cr_, xi + ci_
        tr, ti = mul(wr, wi, va[0, e], va[1, e])
        res[0, p], res[1, p] = res[0, p] - tr, res[1, p] - ti

    loop(0, own, finish)

    sqr, sqi = orders_of(1)
    tr, ti = mul(ar, ai, sqr, sqi)
    cr_, ci_ = mul(wr, wi, sdr - tr, sdi - ti)
    xr, xi = mul(ar, ai, sdr, sdi)
    pup[0:1] = xr + cr_
    pup[1:2] = xi + ci_

    for copy in sent:
        copy.wait_send()


def on_device(n, source_term, material, orders):
    own, nx, ny = material.shape
    half = own // 2
    ty, tx = tables(nx, ny)
    vm = pltpu.VMEM
    fine = vm((2, 3 * own, nx, ny), F32)
    planes1 = (2 * REACH1 + 1) * half
    one = vm((2, planes1, nx // 2, ny), F32)
    planes2 = 2 * REACH2 + 1
    two = vm((2, planes2, nx // 4, ny), F32)
    dma = pltpu.SemaphoreType.DMA
    ext1 = 3 * (2 * REACH1 + 1)
    ext2 = 3 * planes2
    whole = pl.BlockSpec(memory_space=pltpu.VMEM)
    return pl.pallas_call(
        functools.partial(kernel, n),
        out_shape=(
            jax.ShapeDtypeStruct(source_term.shape, F32),
            jax.ShapeDtypeStruct(source_term.shape, F32),
            jax.ShapeDtypeStruct(orders.shape, F32),
        ),
        in_specs=[pl.BlockSpec(memory_space=pl.ANY)] * 5,
        out_specs=(whole,) * 3,
        scratch_shapes=[
            vm(orders.shape, jnp.int32), vm(ty.shape, F32), vm(tx.shape, F32), dma((5,)),
            fine, fine, vm((3 * own, nx, ny), jnp.int32), fine, fine, fine,
            vm((2, half, nx // 2, ny), F32), one, one, one, one,
            two, two, two, two, vm((2, nx // 4, ny), F32),
            vm((3, 2 * REACH1 + 1, half, nx // 2, ny), F32),
            vm((3, planes2, nx // 8, ny), F32),
            vm((2 * half, nx, ny), F32),
            vm((2, n, 8, ny), F32),
            vm((2, HARM, 2 * HALF), F32),
            dma((12,)), dma((12,)), dma((ext1,)), dma((ext1,)), dma((ext2,)), dma((ext2,)),
            dma((2, n)), dma((2, n)), dma((2, n)), dma((2,)),
        ],
        compiler_params=pltpu.CompilerParams(
            collective_id=0, has_side_effects=True, vmem_limit_bytes=40 * 1024 * 1024
        ),
    )(source_term, material, orders, jnp.asarray(ty), jnp.asarray(tx))


def solution(mesh):
    return jax.shard_map(
        functools.partial(on_device, mesh.shape["gz"]),
        mesh=mesh,
        in_specs=(
            P(None, ("clip", "gz"), None, None),
            P(("clip", "gz"), None, None),
            P(None, "gz"),
        ),
        out_specs=(
            P(None, ("clip", "gz"), None, None),
            P(None, ("clip", "gz"), None, None),
            P(None, ("clip", "gz")),
        ),
        check_vma=False,
    )
```

```python
import functools
import math

import jax
import jax.numpy as jnp
import numpy as np
from jax import lax
from jax.experimental import pallas as pl
from jax.experimental.pallas import tpu as pltpu
from jax.sharding import PartitionSpec as P

ORD_HALF = 22
HELM_TABLE = ((-0.5, 0.0), (1.0, -1.4), (-1.2, 0.0))
SHIFT_TABLE = ((-0.5, -0.25), (1.0, -0.25 * math.sqrt(11.84)), (-1.2, -0.6))
RELAX = 0.8
REACH1 = 3
REACH2 = 5
HALF = 64
HARM = 48
F32 = jnp.float32


def weight_of(shift):
    bottom = complex(6.0 + shift[0], shift[1])
    value = RELAX / bottom
    return (value.real, value.imag)


WEIGHT_TABLE = tuple(weight_of(entry) for entry in SHIFT_TABLE)
DIAG_TABLE = tuple((6.0 + entry[0], entry[1]) for entry in SHIFT_TABLE)
IMAGE_TABLE = tuple((6.0 + entry[0], entry[1]) for entry in HELM_TABLE)


def pick(material, table):
    one = material == 1
    two = material == 2
    return tuple(
        jnp.where(one, table[1][k], jnp.where(two, table[2][k], table[0][k])).astype(F32)
        for k in range(2)
    )


def mul(ar, ai, br, bi):
    return ar * br - ai * bi, ar * bi + ai * br


def loop(lo, hi, body):
    def step(p, carry):
        body(p)
        return carry

    lax.fori_loop(lo, hi, step, 0)


def planes(lo, hi, group, dst, body):
    def some(first, count):
        values = [body(first + j) for j in range(count)]
        for j, (r, i) in enumerate(values):
            dst[0, first + j] = r
            dst[1, first + j] = i

    steps = (hi - lo) // group
    if steps == 1:
        some(lo, group)
    elif steps > 1:
        loop(0, steps, lambda t: some(lo + t * group, group))
    if (hi - lo) % group:
        some(lo + steps * group, (hi - lo) % group)


FINE, MIDDLE, COARSE = 2, 4, 6


def row_neighbours(x, lane_step):
    if lane_step == 4:
        return pltpu.roll(x, 1, 0) + pltpu.roll(x, x.shape[0] - 1, 0)
    if lane_step == 2:
        h = x.shape[0] // 2
        even, odd = x[:h], x[h:]
        return jnp.concatenate([odd + pltpu.roll(odd, 1, 0), even + pltpu.roll(even, h - 1, 0)])
    q = x.shape[0] // 4
    a, b, c, d = (x[j * q : (j + 1) * q] for j in range(4))
    return jnp.concatenate([c + pltpu.roll(d, 1, 0), c + d, a + b, b + pltpu.roll(a, q - 1, 0)])


def split_rows(rows):
    q = rows // 4
    return [((2 * c + b) * q, 2 * b + c) for c in range(2) for b in range(2)]


def around(ref, k, p, lane_step):
    x = ref[k, p]
    lanes = x.shape[1]
    total = ref[k, p - 1] + ref[k, p + 1]
    total = total + row_neighbours(x, lane_step)
    return total + (pltpu.roll(x, lane_step, 1) + pltpu.roll(x, lanes - lane_step, 1))


def first_sweep(lo, hi, group, dst, rhs, weight):
    planes(lo, hi, group, dst, lambda p: mul(weight[0, p], weight[1, p], rhs[0, p], rhs[1, p]))


def sweep(lo, hi, group, dst, old, rhs, weight, lane_step, h2):
    def body(p):
        nr = around(old, 0, p, lane_step)
        ni = around(old, 1, p, lane_step)
        if h2 != 1.0:
            nr, ni = nr * h2, ni * h2
        r, i = mul(weight[0, p], weight[1, p], rhs[0, p] + nr, rhs[1, p] + ni)
        return (1.0 - RELAX) * old[0, p] + r, (1.0 - RELAX) * old[1, p] + i

    planes(lo, hi, group, dst, body)


def lane_iota(shape):
    return lax.broadcasted_iota(jnp.int32, shape, 1)


def pair_lanes(x, step):
    lanes = x.shape[1]
    low = (lane_iota(x.shape) & step) == 0
    return x + jnp.where(low, pltpu.roll(x, lanes - step, 1), pltpu.roll(x, step, 1))


def pair_rows(x):
    h = x.shape[0] // 2
    return x[:h] + x[h:]


def spread_rows(x):
    return jnp.concatenate([x, x])


def pack_two(r, i):
    return jnp.where((lane_iota(r.shape) & 1) == 0, r, i)


def unpack_two(x):
    lanes = x.shape[1]
    even = (lane_iota(x.shape) & 1) == 0
    return jnp.where(even, x, pltpu.roll(x, 1, 1)), jnp.where(even, pltpu.roll(x, lanes - 1, 1), x)


def pack_four(r, i):
    rows = r.shape[0] // 2
    top = pack_two(r[:rows], i[:rows])
    low = pack_two(r[rows:], i[rows:])
    return jnp.where((lane_iota(top.shape) & 2) == 0, top, low)


def unpack_four(x):
    lanes = x.shape[1]
    first = (lane_iota(x.shape) & 2) == 0
    halves = []
    for y in unpack_two(x):
        halves.append(
            (jnp.where(first, y, pltpu.roll(y, 2, 1)), jnp.where(first, pltpu.roll(y, lanes - 2, 1), y))
        )
    return halves


def invert(r, i):
    bottom = 1.0 / (r * r + i * i)
    return RELAX * r * bottom, -RELAX * i * bottom


def precise(a, b, dims):
    return lax.dot_general(
        a, b, (dims, ((), ())), precision=lax.Precision.HIGHEST, preferred_element_type=F32
    )


def spectrum_of(r, i, ty, tx):
    gr = precise(ty, r, ((1,), (1,)))
    gi = precise(ty, i, ((1,), (1,)))
    inner = jnp.concatenate([gr[:HALF] - gi[HALF:], gr[HALF:] + gi[:HALF]], axis=0)
    outer = precise(inner, tx, ((1,), (0,)))
    turned = pltpu.roll(outer[HALF:], HALF, 1)
    left = lane_iota(turned.shape) < HALF
    return (outer[:HALF] + jnp.where(left, -turned, turned))[:HARM]


def tables(nx, ny):
    harmonics = np.arange(2 * ORD_HALF + 1) - ORD_HALF
    count = harmonics.size
    ty = np.zeros((2 * HALF, ny), np.float32)
    angle = 2.0 * np.pi * ((harmonics[:, None] * np.arange(ny)[None, :]) % ny) / ny
    ty[:count] = np.cos(angle)
    ty[HALF : HALF + count] = -np.sin(angle)
    tx = np.zeros((nx, 2 * HALF), np.float32)
    angle = 2.0 * np.pi * ((np.arange(nx)[:, None] * harmonics[None, :]) % nx) / nx
    scale = 1.0 / math.sqrt(nx * ny)
    tx[:, :count] = np.cos(angle) * scale
    tx[:, HALF : HALF + count] = -np.sin(angle) * scale
    tx = np.concatenate([tx[row::4] for _, row in split_rows(nx)])
    return ty, tx


def kernel(
    n, src_in, mat_in, ords_in, ty_in, tx_in, sol, res, pup,
    ords, ty, tx, in_sem, fx, gx, mx, w0, va, vb, d1, w1, f1, v1a, v1b, w2, f2, v2a, v2b, d2,
    pk1, pk2, raw, raw_mat, red, spec,
    fine_send, fine_recv, k1_send, k1_recv, k2_send, k2_recv,
    red_send, red_recv, spec_send, spec_recv,
):
    me = lax.axis_index("gz")
    own = mat_in.shape[0]
    depth = own
    half = own // 2
    mid1 = REACH1 * half
    sent = []

    def other(k):
        return {"gz": lax.rem(me + k + n, n)}

    def start(source, target, ssem, rsem, k):
        copy = pltpu.make_async_remote_copy(
            src_ref=source, dst_ref=target, send_sem=ssem, recv_sem=rsem,
            device_id=other(k), device_id_type=pl.DeviceIdType.MESH,
        )
        copy.start()
        sent.append(copy)
        return copy

    barrier = pltpu.get_barrier_semaphore()

    def greet(k):
        pl.semaphore_signal(
            barrier, inc=1, device_id={"gz": lax.rem(me + k, n)},
            device_id_type=pl.DeviceIdType.MESH,
        )

    loop(1, n, greet)

    src = fx.at[:, pl.ds(depth, own)]
    mat = mx.at[pl.ds(depth, own)]
    fetches = [
        pltpu.make_async_copy(a, b, in_sem.at[k])
        for k, (a, b) in enumerate(
            ((mat_in, raw_mat), (src_in, raw), (ords_in, ords), (ty_in, ty), (tx_in, tx))
        )
    ]
    for fetch in fetches:
        fetch.start()
    quarter = mat_in.shape[1] // 4
    quarters = split_rows(mat_in.shape[1])
    fetches[0].wait()
    for p in range(own):
        for at, row in quarters:
            mat[p, at : at + quarter] = raw_mat[p, pl.ds(row, quarter, stride=4)]

    for p in range(half):
        a = pick(mat[2 * p], SHIFT_TABLE)
        b = pick(mat[2 * p + 1], SHIFT_TABLE)
        for k in range(2):
            d1[k, p] = 0.125 * pair_rows(pair_lanes(a[k] + b[k], 1))
        pk1[0, REACH1, p] = pack_two(d1[0, p], d1[1, p])
    for k in range(2):
        d2[k] = 0.125 * pair_rows(pair_lanes(d1[k, 0] + d1[k, 1], 2))
    pk2[0, REACH2] = pack_four(d2[0], d2[1])

    for fetch in fetches[1:]:
        fetch.wait()
    for p in range(own):
        for at, row in quarters:
            for k in range(2):
                src[k, p, at : at + quarter] = raw[k, p, pl.ds(row, quarter, stride=4)]
    pl.semaphore_wait(barrier, n - 1)

    def send_planes(source, base, target, slot, near, dims):
        up_from = half if near else 0
        up_to = half if near else 0
        down_from = 0 if near else half
        down_to = depth + own + (0 if near else half)
        copies = []
        for which, (k, a, b) in enumerate(((1, up_from, up_to), (-1, down_from, down_to))):
            s = pl.ds(base + a, half)
            t = pl.ds(b, half)
            one = source.at[:, s] if dims else source.at[s]
            two = target.at[:, t] if dims else target.at[t]
            copies.append(
                start(one, two, fine_send.at[slot + which], fine_recv.at[slot + which], k)
            )
        return copies

    def send_one(which):
        copies = {}
        for k in range(1, REACH1 + 1):
            for d in (k, -k):
                at = which * (2 * REACH1 + 1) + REACH1 - d
                part = pl.ds(0, half)
                if k == REACH1:
                    part = pl.ds(half - 1 if d > 0 else 0, 1)
                copies[-d] = start(
                    pk1.at[which, REACH1, part], pk1.at[which, REACH1 - d, part],
                    k1_send.at[at], k1_recv.at[at], d,
                )
        return copies

    def send_two(which):
        copies = {}
        for k in range(1, REACH2 + 1):
            for d in (k, -k):
                at = which * (2 * REACH2 + 1) + REACH2 - d
                copies[-d] = start(
                    pk2.at[which, REACH2], pk2.at[which, REACH2 - d],
                    k2_send.at[at], k2_recv.at[at], d,
                )
        return copies

    near_mat = send_planes(mx, depth, mx, 0, True, False)
    near_src = send_planes(fx, depth, fx, 2, True, True)
    shifts1 = send_one(0)
    shifts2 = send_two(0)
    far_mat = send_planes(mx, depth, mx, 4, False, False)
    far_src = send_planes(fx, depth, fx, 6, False, True)

    def inside(plane, count):
        return jnp.where(jnp.logical_and(plane >= 0, plane < count), 1.0, 0.0).astype(F32)

    def weight0(p):
        m = inside(me * own + p - depth, n * own)
        r, i = pick(mx[p], WEIGHT_TABLE)
        return r * m, i * m

    def weight1(p):
        r, i = unpack_two(pk1[0, p // half, p % half])
        r, i = invert(r + 1.5, i)
        m = inside(me * half + p - mid1, n * half)
        return r * m, i * m

    def weight2(p):
        (rt, rb), (it, ib) = unpack_four(pk2[0, p])
        m = inside(me + p - REACH2, n)
        r, i = invert(jnp.concatenate([rt, rb]) + 0.375, jnp.concatenate([it, ib]))
        return r * m, i * m

    def take1(which):
        def body(p):
            return unpack_two(pk1[which, p // half, p % half])

        return body

    def take2(which):
        def body(p):
            (rt, rb), (it, ib) = unpack_four(pk2[which, p])
            return jnp.concatenate([rt, rb]), jnp.concatenate([it, ib])

        return body

    def cycle(which, f, near, far):
        begin, end = depth, depth + own
        if which == 1:
            for copy in near_mat:
                copy.wait_recv()
            planes(begin - 2, end + 2, FINE, w0, weight0)
        for copy in near:
            copy.wait_recv()
        first_sweep(begin - 2, end + 2, FINE, va, f, w0)
        sweep(begin - 1, end + 1, FINE, vb, va, f, w0, 1, 1.0)

        def down(q):
            total = [None, None]
            for s in range(2):
                p = depth + 2 * q + s
                c = pick(mx[p], DIAG_TABLE)
                dr, di = mul(c[0], c[1], vb[0, p], vb[1, p])
                for k, d in enumerate((dr, di)):
                    e = (f[k, p] - d) + around(vb, k, p, 1)
                    total[k] = e if s == 0 else total[k] + e
            parts = [
                0.125 * pair_rows(pair_lanes(t, 1)) for k, t in enumerate(total)
            ]
            f1[0, mid1 + q] = parts[0]
            f1[1, mid1 + q] = parts[1]
            pk1[which, REACH1, q] = pack_two(parts[0], parts[1])

        for q in range(half):
            down(q)
        ones = send_one(which)

        if which == 1:
            for d in (-1, 1):
                shifts1[d].wait_recv()
            planes(mid1 - half, mid1 + 2 * half, MIDDLE, w1, weight1)

        for d in (-1, 1):
            ones[d].wait_recv()
        planes(mid1 - half, mid1, MIDDLE, f1, take1(which))
        planes(mid1 + half, mid1 + 2 * half, MIDDLE, f1, take1(which))
        first_sweep(mid1 - 2, mid1 + half + 2, MIDDLE, v1a, f1, w1)
        sweep(mid1 - 1, mid1 + half + 1, MIDDLE, v1b, v1a, f1, w1, 2, 0.25)

        parts = []
        total = [None, None]
        for q in range(half):
            p = mid1 + q
            dr, di = mul(d1[0, q] + 1.5, d1[1, q], v1b[0, p], v1b[1, p])
            for k, d in enumerate((dr, di)):
                e = (f1[k, p] - d) + 0.25 * around(v1b, k, p, 2)
                total[k] = e if q == 0 else total[k] + e
        parts = [0.125 * pair_rows(pair_lanes(t, 2)) for k, t in enumerate(total)]
        pk2[which, REACH2] = pack_four(parts[0], parts[1])
        twos = send_two(which)

        if which == 1:
            for copy in far_mat:
                copy.wait_recv()
            planes(0, begin - 2, FINE, w0, weight0)
            planes(end + 2, end + depth, FINE, w0, weight0)
            for d in range(2, REACH1 + 1):
                shifts1[d].wait_recv()
                shifts1[-d].wait_recv()
            planes(1, mid1 - half, MIDDLE, w1, weight1)
            planes(mid1 + 2 * half, 2 * mid1 + half - 1, MIDDLE, w1, weight1)
        for d in range(2, REACH1 + 1):
            ones[d].wait_recv()
            ones[-d].wait_recv()
        planes(1, mid1 - half, MIDDLE, f1, take1(which))
        planes(mid1 + 2 * half, 2 * mid1 + half - 1, MIDDLE, f1, take1(which))
        first_sweep(1, mid1 - 2, MIDDLE, v1a, f1, w1)
        first_sweep(mid1 + half + 2, 2 * mid1 + half - 1, MIDDLE, v1a, f1, w1)
        sweep(2, mid1 - 1, MIDDLE, v1b, v1a, f1, w1, 2, 0.25)
        sweep(mid1 + half + 1, 2 * mid1 + half - 2, MIDDLE, v1b, v1a, f1, w1, 2, 0.25)
        for copy in far:
            copy.wait_recv()
        first_sweep(0, begin - 2, FINE, va, f, w0)
        first_sweep(end + 2, end + depth, FINE, va, f, w0)
        sweep(1, begin - 1, FINE, vb, va, f, w0, 1, 1.0)
        sweep(end + 1, end + depth - 1, FINE, vb, va, f, w0, 1, 1.0)
        if which == 1:
            for d in range(1, REACH2 + 1):
                shifts2[d].wait_recv()
                shifts2[-d].wait_recv()
            planes(0, 2 * REACH2 + 1, COARSE, w2, weight2)

        for d in range(1, REACH2 + 1):
            twos[d].wait_recv()
            twos[-d].wait_recv()
        planes(0, 2 * REACH2 + 1, COARSE, f2, take2(which))
        first_sweep(0, 2 * REACH2 + 1, COARSE, v2a, f2, w2)
        sweep(1, 2 * REACH2, COARSE, v2b, v2a, f2, w2, 4, 0.0625)
        sweep(2, 2 * REACH2 - 1, COARSE, v2a, v2b, f2, w2, 4, 0.0625)
        sweep(3, 2 * REACH2 - 2, COARSE, v2b, v2a, f2, w2, 4, 0.0625)

        def raise1(c):
            p = (c - REACH2 + REACH1) * half
            for k in range(2):
                x = spread_rows(v2b[k, c])
                v1b[k, p] = v1b[k, p] + x
                v1b[k, p + 1] = v1b[k, p + 1] + x

        for c in range(REACH2 - 2, REACH2 + 3):
            raise1(c)
        sweep(mid1 - 3, mid1 + half + 3, MIDDLE, v1a, v1b, f1, w1, 2, 0.25)
        sweep(mid1 - 2, mid1 + half + 2, MIDDLE, v1b, v1a, f1, w1, 2, 0.25)

        def raise0(c):
            p = depth + 2 * (c - mid1)
            for k in range(2):
                x = spread_rows(v1b[k, c])
                vb[k, p] = vb[k, p] + x
                vb[k, p + 1] = vb[k, p + 1] + x

        for c in range(mid1 - 2, mid1 + half + 2):
            raise0(c)
        sweep(begin - 2, end + 2, FINE, va, vb, f, w0, 1, 1.0)
        sweep(begin - 1, end + 1, FINE, vb, va, f, w0, 1, 1.0)

    def image_of(p):
        c = pick(mx[p], IMAGE_TABLE)
        r, i = mul(c[0], c[1], vb[0, p], vb[1, p])
        return r - around(vb, 0, p, 1), i - around(vb, 1, p, 1)

    def fold(x):
        rows, lanes = x.shape
        return jnp.sum(x.reshape(rows // 8, 8, lanes), axis=0)

    def share(which, sums):
        rows = [jnp.sum(s, axis=0, keepdims=True) for s in sums]
        rows.append(jnp.zeros((8 - len(rows), rows[0].shape[1]), F32))
        red[which, me] = jnp.concatenate(rows, axis=0)

        def post(k):
            pltpu.make_async_remote_copy(
                src_ref=red.at[which, me], dst_ref=red.at[which, me],
                send_sem=red_send.at[which, k], recv_sem=red_recv.at[which, k],
                device_id={"gz": lax.rem(me + k, n)}, device_id_type=pl.DeviceIdType.MESH,
            ).start()

        loop(1, n, post)

    def collect(which):
        def await_one(k):
            one = pltpu.make_async_remote_copy(
                src_ref=red.at[which, me], dst_ref=red.at[which, lax.rem(me + n - k, n)],
                send_sem=red_send.at[which, k], recv_sem=red_recv.at[which, k],
                device_id={"gz": lax.rem(me + k, n)}, device_id_type=pl.DeviceIdType.MESH,
            )
            one.wait_recv()
            one.wait_send()

        loop(1, n, await_one)
        total = red[which, 0]
        for j in range(1, n):
            total = total + red[which, j]
        total = jnp.sum(total, axis=1, keepdims=True)
        return total[0:1], total[1:2], total[2:3]

    def spectrum(which):
        def post(k):
            pltpu.make_async_remote_copy(
                src_ref=spec.at[which], dst_ref=spec.at[which],
                send_sem=spec_send.at[which, k], recv_sem=spec_recv.at[which],
                device_id={"gz": lax.rem(me + k, n)}, device_id_type=pl.DeviceIdType.MESH,
            ).start()

        @pl.when(me == n - 1)
        def _():
            last = depth + own - 1
            spec[which] = spectrum_of(vb[0, last], vb[1, last], ty[...], tx[...])
            loop(1, n, post)

    def orders_of(which):
        def settle(k):
            pltpu.make_async_remote_copy(
                src_ref=spec.at[which], dst_ref=spec.at[which],
                send_sem=spec_send.at[which, k], recv_sem=spec_recv.at[which],
                device_id={"gz": lax.rem(me + k, n)}, device_id_type=pl.DeviceIdType.MESH,
            ).wait_send()

        @pl.when(me == n - 1)
        def _():
            loop(1, n, settle)

        @pl.when(me != n - 1)
        def _():
            pltpu.make_async_remote_copy(
                src_ref=spec.at[which], dst_ref=spec.at[which],
                send_sem=spec_send.at[which, 0], recv_sem=spec_recv.at[which],
                device_id={"gz": lax.rem(me + 1, n)}, device_id_type=pl.DeviceIdType.MESH,
            ).wait_recv()

        count = ords.shape[1]
        x = ords[0:1] + ORD_HALF
        y = ords[1:2] + ORD_HALF
        row = lax.broadcasted_iota(jnp.int32, (2 * HALF, count), 0)
        pick_y = lax.broadcasted_iota(jnp.int32, (HARM, count), 0) == y
        out = []
        for k in range(2):
            pick_x = jnp.where(row == x + k * HALF, 1.0, 0.0).astype(F32)
            chosen = precise(spec[which], pick_x, ((1,), (0,)))
            out.append(jnp.sum(jnp.where(pick_y, chosen, 0.0), axis=0, keepdims=True))
        return out

    cycle(1, fx, near_src, far_src)

    zero = jnp.zeros((8, fx.shape[3]), F32)
    sums = [zero, zero, zero]
    for p in range(own):
        r, i = image_of(depth + p)
        gx[0, depth + p] = r
        gx[1, depth + p] = i
        a, b = src[0, p], src[1, p]
        sums[0] = sums[0] + fold(a * a + b * b)
        sums[1] = sums[1] + fold(a * r + b * i)
        sums[2] = sums[2] + fold(a * i - b * r)
    near_img = send_planes(gx, depth, gx, 8, True, True)
    share(0, sums)
    far_img = send_planes(gx, depth, gx, 10, False, True)

    def keep(p):
        sol[0, p] = vb[0, depth + p]
        sol[1, p] = vb[1, depth + p]

    loop(0, own, keep)
    spectrum(0)

    cycle(2, gx, near_img, far_img)

    rho, cr, ci = collect(0)
    scale = rho / (cr * cr + ci * ci)
    ar, ai = cr * scale, -(ci * scale)

    sums = [zero, zero, zero]
    for p in range(own):
        e = depth + p
        r, i = image_of(e)
        gr, gi = gx[0, e], gx[1, e]
        tr, ti = mul(ar, ai, gr, gi)
        hr, hi = src[0, p] - tr, src[1, p] - ti
        tr, ti = mul(ar, ai, r, i)
        lr, li = gr - tr, gi - ti
        va[0, e], va[1, e] = lr, li
        raw[0, p], raw[1, p] = hr, hi
        sums[0] = sums[0] + fold(lr * hr + li * hi)
        sums[1] = sums[1] + fold(lr * hi - li * hr)
        sums[2] = sums[2] + fold(lr * lr + li * li)
    share(1, sums)
    spectrum(1)
    sdr, sdi = orders_of(0)

    along_r, along_i, norm = collect(1)
    wr, wi = along_r / norm, along_i / norm

    def finish(p):
        e = depth + p
        dr, di = sol[0, p], sol[1, p]
        tr, ti = mul(ar, ai, vb[0, e], vb[1, e])
        cr_, ci_ = mul(wr, wi, dr - tr, di - ti)
        xr, xi = mul(ar, ai, dr, di)
        solved = (xr + cr_, xi + ci_)
        tr, ti = mul(wr, wi, va[0, e], va[1, e])
        left = (raw[0, p] - tr, raw[1, p] - ti)
        for k in range(2):
            for at, row in quarters:
                sol[k, p, pl.ds(row, quarter, stride=4)] = solved[k][at : at + quarter]
                res[k, p, pl.ds(row, quarter, stride=4)] = left[k][at : at + quarter]

    for p in range(own):
        finish(p)

    sqr, sqi = orders_of(1)
    tr, ti = mul(ar, ai, sqr, sqi)
    cr_, ci_ = mul(wr, wi, sdr - tr, sdi - ti)
    xr, xi = mul(ar, ai, sdr, sdi)
    pup[0:1] = xr + cr_
    pup[1:2] = xi + ci_

    for copy in sent:
        copy.wait_send()


def on_device(n, source_term, material, orders):
    own, nx, ny = material.shape
    half = own // 2
    ty, tx = tables(nx, ny)
    vm = pltpu.VMEM
    fine = vm((2, 3 * own, nx, ny), F32)
    planes1 = (2 * REACH1 + 1) * half
    one = vm((2, planes1, nx // 2, ny), F32)
    planes2 = 2 * REACH2 + 1
    two = vm((2, planes2, nx // 4, ny), F32)
    dma = pltpu.SemaphoreType.DMA
    ext1 = 3 * (2 * REACH1 + 1)
    ext2 = 3 * planes2
    whole = pl.BlockSpec(memory_space=pltpu.VMEM)
    return pl.pallas_call(
        functools.partial(kernel, n),
        out_shape=(
            jax.ShapeDtypeStruct(source_term.shape, F32),
            jax.ShapeDtypeStruct(source_term.shape, F32),
            jax.ShapeDtypeStruct(orders.shape, F32),
        ),
        in_specs=[pl.BlockSpec(memory_space=pl.ANY)] * 5,
        out_specs=(whole,) * 3,
        scratch_shapes=[
            vm(orders.shape, jnp.int32), vm(ty.shape, F32), vm(tx.shape, F32), dma((5,)),
            fine, fine, vm((3 * own, nx, ny), jnp.int32), fine, fine, fine,
            vm((2, half, nx // 2, ny), F32), one, one, one, one,
            two, two, two, two, vm((2, nx // 4, ny), F32),
            vm((3, 2 * REACH1 + 1, half, nx // 2, ny), F32),
            vm((3, planes2, nx // 8, ny), F32),
            vm((2, own, nx, ny), F32),
            vm((own, nx, ny), jnp.int32),
            vm((2, n, 8, ny), F32),
            vm((2, HARM, 2 * HALF), F32),
            dma((12,)), dma((12,)), dma((ext1,)), dma((ext1,)), dma((ext2,)), dma((ext2,)),
            dma((2, n)), dma((2, n)), dma((2, n)), dma((2,)),
        ],
        compiler_params=pltpu.CompilerParams(
            collective_id=0, has_side_effects=True, vmem_limit_bytes=62 * 1024 * 1024
        ),
    )(source_term, material, orders, jnp.asarray(ty), jnp.asarray(tx))


def solution(mesh):
    return jax.shard_map(
        functools.partial(on_device, mesh.shape["gz"]),
        mesh=mesh,
        in_specs=(
            P(None, ("clip", "gz"), None, None),
            P(("clip", "gz"), None, None),
            P(None, "gz"),
        ),
        out_specs=(
            P(None, ("clip", "gz"), None, None),
            P(None, ("clip", "gz"), None, None),
            P(None, ("clip", "gz")),
        ),
        check_vma=False,
    )
```

```python
import functools
import math

import jax
import jax.numpy as jnp
import numpy as np
from jax import lax
from jax.experimental import pallas as pl
from jax.experimental.pallas import tpu as pltpu
from jax.sharding import PartitionSpec as P

ORD_HALF = 22
HELM_TABLE = ((-0.5, 0.0), (1.0, -1.4), (-1.2, 0.0))
SHIFT_TABLE = ((-0.5, -0.25), (1.0, -0.25 * math.sqrt(11.84)), (-1.2, -0.6))
RELAX = 0.8
REACH1 = 3
REACH2 = 5
HALF = 64
HARM = 48
F32 = jnp.float32


def weight_of(shift):
    bottom = complex(6.0 + shift[0], shift[1])
    value = RELAX / bottom
    return (value.real, value.imag)


WEIGHT_TABLE = tuple(weight_of(entry) for entry in SHIFT_TABLE)
DIAG_TABLE = tuple((6.0 + entry[0], entry[1]) for entry in SHIFT_TABLE)
IMAGE_TABLE = tuple((6.0 + entry[0], entry[1]) for entry in HELM_TABLE)


def pick(material, table):
    one = material == 1
    two = material == 2
    return tuple(
        jnp.where(one, table[1][k], jnp.where(two, table[2][k], table[0][k])).astype(F32)
        for k in range(2)
    )


def mul(ar, ai, br, bi):
    return ar * br - ai * bi, ar * bi + ai * br


class Message:
    def __init__(self, copy, sends, receives):
        self.copy, self.sends, self.receives = copy, sends, receives

    def start(self):
        pl.when(self.sends)(lambda: self.copy.start())

    def wait_send(self):
        pl.when(self.sends)(lambda: self.copy.wait_send())

    def wait_recv(self):
        pl.when(self.receives)(lambda: self.copy.wait_recv())


def loop(lo, hi, body):
    def step(p, carry):
        body(p)
        return carry

    lax.fori_loop(lo, hi, step, 0)


def planes(lo, hi, group, dst, body):
    def some(first, count):
        values = [body(first + j) for j in range(count)]
        for j, (r, i) in enumerate(values):
            dst[0, first + j] = r
            dst[1, first + j] = i

    steps = (hi - lo) // group
    if steps == 1:
        some(lo, group)
    elif steps > 1:
        loop(0, steps, lambda t: some(lo + t * group, group))
    if (hi - lo) % group:
        some(lo + steps * group, (hi - lo) % group)


FINE, MIDDLE, COARSE = 2, 4, 6


def row_neighbours(x, lane_step):
    if lane_step == 4:
        return pltpu.roll(x, 1, 0) + pltpu.roll(x, x.shape[0] - 1, 0)
    if lane_step == 2:
        h = x.shape[0] // 2
        even, odd = x[:h], x[h:]
        return jnp.concatenate([odd + pltpu.roll(odd, 1, 0), even + pltpu.roll(even, h - 1, 0)])
    q = x.shape[0] // 4
    a, b, c, d = (x[j * q : (j + 1) * q] for j in range(4))
    return jnp.concatenate([c + pltpu.roll(d, 1, 0), c + d, a + b, b + pltpu.roll(a, q - 1, 0)])


def split_rows(rows):
    q = rows // 4
    return [((2 * c + b) * q, 2 * b + c) for c in range(2) for b in range(2)]


def around(ref, k, p, lane_step):
    x = ref[k, p]
    lanes = x.shape[1]
    total = ref[k, p - 1] + ref[k, p + 1]
    total = total + row_neighbours(x, lane_step)
    return total + (pltpu.roll(x, lane_step, 1) + pltpu.roll(x, lanes - lane_step, 1))


def first_sweep(lo, hi, group, dst, rhs, weight):
    planes(lo, hi, group, dst, lambda p: mul(weight[0, p], weight[1, p], rhs[0, p], rhs[1, p]))


def sweep(lo, hi, group, dst, old, rhs, weight, lane_step, h2):
    def body(p):
        nr = around(old, 0, p, lane_step)
        ni = around(old, 1, p, lane_step)
        if h2 != 1.0:
            nr, ni = nr * h2, ni * h2
        r, i = mul(weight[0, p], weight[1, p], rhs[0, p] + nr, rhs[1, p] + ni)
        return (1.0 - RELAX) * old[0, p] + r, (1.0 - RELAX) * old[1, p] + i

    planes(lo, hi, group, dst, body)


def lane_iota(shape):
    return lax.broadcasted_iota(jnp.int32, shape, 1)


def pair_lanes(x, step):
    lanes = x.shape[1]
    low = (lane_iota(x.shape) & step) == 0
    return x + jnp.where(low, pltpu.roll(x, lanes - step, 1), pltpu.roll(x, step, 1))


def pair_rows(x):
    h = x.shape[0] // 2
    return x[:h] + x[h:]


def spread_rows(x):
    return jnp.concatenate([x, x])


def pack_two(r, i):
    return jnp.where((lane_iota(r.shape) & 1) == 0, r, i)


def unpack_two(x):
    lanes = x.shape[1]
    even = (lane_iota(x.shape) & 1) == 0
    return jnp.where(even, x, pltpu.roll(x, 1, 1)), jnp.where(even, pltpu.roll(x, lanes - 1, 1), x)


def pack_four(r, i):
    rows = r.shape[0] // 2
    top = pack_two(r[:rows], i[:rows])
    low = pack_two(r[rows:], i[rows:])
    return jnp.where((lane_iota(top.shape) & 2) == 0, top, low)


def unpack_four(x):
    lanes = x.shape[1]
    first = (lane_iota(x.shape) & 2) == 0
    halves = []
    for y in unpack_two(x):
        halves.append(
            (jnp.where(first, y, pltpu.roll(y, 2, 1)), jnp.where(first, pltpu.roll(y, lanes - 2, 1), y))
        )
    return halves


def invert(r, i):
    bottom = 1.0 / (r * r + i * i)
    return RELAX * r * bottom, -RELAX * i * bottom


def precise(a, b, dims):
    return lax.dot_general(
        a, b, (dims, ((), ())), precision=lax.Precision.HIGHEST, preferred_element_type=F32
    )


def spectrum_of(r, i, ty, tx):
    gr = precise(ty, r, ((1,), (1,)))
    gi = precise(ty, i, ((1,), (1,)))
    inner = jnp.concatenate([gr[:HALF] - gi[HALF:], gr[HALF:] + gi[:HALF]], axis=0)
    outer = precise(inner, tx, ((1,), (0,)))
    turned = pltpu.roll(outer[HALF:], HALF, 1)
    left = lane_iota(turned.shape) < HALF
    return (outer[:HALF] + jnp.where(left, -turned, turned))[:HARM]


def tables(nx, ny):
    harmonics = np.arange(2 * ORD_HALF + 1) - ORD_HALF
    count = harmonics.size
    ty = np.zeros((2 * HALF, ny), np.float32)
    angle = 2.0 * np.pi * ((harmonics[:, None] * np.arange(ny)[None, :]) % ny) / ny
    ty[:count] = np.cos(angle)
    ty[HALF : HALF + count] = -np.sin(angle)
    tx = np.zeros((nx, 2 * HALF), np.float32)
    angle = 2.0 * np.pi * ((np.arange(nx)[:, None] * harmonics[None, :]) % nx) / nx
    scale = 1.0 / math.sqrt(nx * ny)
    tx[:, :count] = np.cos(angle) * scale
    tx[:, HALF : HALF + count] = -np.sin(angle) * scale
    tx = np.concatenate([tx[row::4] for _, row in split_rows(nx)])
    return ty, tx


def kernel(
    n, src_in, mat_in, ords_in, ty_in, tx_in, sol, res, pup,
    ords, ty, tx, in_sem, fx, gx, mx, w0, va, vb, d1, w1, f1, v1a, v1b, w2, f2, v2a, v2b, d2,
    pk1, pk2, raw, raw_mat, red, spec,
    fine_send, fine_recv, k1_send, k1_recv, k2_send, k2_recv,
    red_send, red_recv, spec_send, spec_recv,
):
    me = lax.axis_index("gz")
    own = mat_in.shape[0]
    depth = own
    half = own // 2
    mid1 = REACH1 * half
    sent = []

    def there(k):
        return me < n - k if k > 0 else me >= -k

    def other(k):
        return {"gz": lax.rem(me + k + n, n)}

    def start(source, target, ssem, rsem, k):
        copy = pltpu.make_async_remote_copy(
            src_ref=source, dst_ref=target, send_sem=ssem, recv_sem=rsem,
            device_id=other(k), device_id_type=pl.DeviceIdType.MESH,
        )
        message = Message(copy, there(k), there(-k))
        message.start()
        sent.append(message)
        return message

    barrier = pltpu.get_barrier_semaphore()

    def greet(k):
        pl.semaphore_signal(
            barrier, inc=1, device_id={"gz": lax.rem(me + k, n)},
            device_id_type=pl.DeviceIdType.MESH,
        )

    def clear(ref):
        ref[...] = jnp.zeros(ref.shape, ref.dtype)

    for d in range(1, REACH2 + 1):
        for k in (d, -d):

            @pl.when(jnp.logical_not(there(k)))
            def _():
                for which in range(3):
                    clear(pk2.at[which, REACH2 + k])
                    if d <= REACH1:
                        clear(pk1.at[which, REACH1 + k])
                if d == 1:
                    rim = pl.ds(depth + own if k > 0 else 0, depth)
                    clear(mx.at[rim])
                    clear(fx.at[:, rim])
                    clear(gx.at[:, rim])

    loop(1, n, greet)

    src = fx.at[:, pl.ds(depth, own)]
    mat = mx.at[pl.ds(depth, own)]
    fetches = [
        pltpu.make_async_copy(a, b, in_sem.at[k])
        for k, (a, b) in enumerate(
            ((mat_in, raw_mat), (src_in, raw), (ords_in, ords), (ty_in, ty), (tx_in, tx))
        )
    ]
    for fetch in fetches:
        fetch.start()
    quarter = mat_in.shape[1] // 4
    quarters = split_rows(mat_in.shape[1])
    fetches[0].wait()
    for p in range(own):
        for at, row in quarters:
            mat[p, at : at + quarter] = raw_mat[p, pl.ds(row, quarter, stride=4)]

    for p in range(half):
        a = pick(mat[2 * p], SHIFT_TABLE)
        b = pick(mat[2 * p + 1], SHIFT_TABLE)
        for k in range(2):
            d1[k, p] = 0.125 * pair_rows(pair_lanes(a[k] + b[k], 1))
        pk1[0, REACH1, p] = pack_two(d1[0, p], d1[1, p])
    for k in range(2):
        d2[k] = 0.125 * pair_rows(pair_lanes(d1[k, 0] + d1[k, 1], 2))
    pk2[0, REACH2] = pack_four(d2[0], d2[1])

    for fetch in fetches[1:]:
        fetch.wait()
    for p in range(own):
        for at, row in quarters:
            for k in range(2):
                src[k, p, at : at + quarter] = raw[k, p, pl.ds(row, quarter, stride=4)]
    pl.semaphore_wait(barrier, n - 1)

    def send_planes(source, base, target, slot, near, dims):
        up_from = half if near else 0
        up_to = half if near else 0
        down_from = 0 if near else half
        down_to = depth + own + (0 if near else half)
        copies = []
        for which, (k, a, b) in enumerate(((1, up_from, up_to), (-1, down_from, down_to))):
            s = pl.ds(base + a, half)
            t = pl.ds(b, half)
            one = source.at[:, s] if dims else source.at[s]
            two = target.at[:, t] if dims else target.at[t]
            copies.append(
                start(one, two, fine_send.at[slot + which], fine_recv.at[slot + which], k)
            )
        return copies

    def send_one(which, lo, hi):
        copies = {}
        for k in range(lo, hi + 1):
            for d in (k, -k):
                at = which * (2 * REACH1 + 1) + REACH1 - d
                part = pl.ds(0, half)
                if k == REACH1:
                    part = pl.ds(half - 1 if d > 0 else 0, 1)
                copies[-d] = start(
                    pk1.at[which, REACH1, part], pk1.at[which, REACH1 - d, part],
                    k1_send.at[at], k1_recv.at[at], d,
                )
        return copies

    def send_two(which):
        copies = {}
        for k in range(1, REACH2 + 1):
            for d in (k, -k):
                at = which * (2 * REACH2 + 1) + REACH2 - d
                copies[-d] = start(
                    pk2.at[which, REACH2], pk2.at[which, REACH2 - d],
                    k2_send.at[at], k2_recv.at[at], d,
                )
        return copies

    near_mat = send_planes(mx, depth, mx, 0, True, False)
    near_src = send_planes(fx, depth, fx, 2, True, True)
    shifts1 = send_one(0, 1, 1)
    shifts2 = {}

    def inside(plane, count):
        return jnp.where(jnp.logical_and(plane >= 0, plane < count), 1.0, 0.0).astype(F32)

    def weight0(p):
        m = inside(me * own + p - depth, n * own)
        r, i = pick(mx[p], WEIGHT_TABLE)
        return r * m, i * m

    def weight1(p):
        r, i = unpack_two(pk1[0, p // half, p % half])
        r, i = invert(r + 1.5, i)
        m = inside(me * half + p - mid1, n * half)
        return r * m, i * m

    def weight2(p):
        (rt, rb), (it, ib) = unpack_four(pk2[0, p])
        m = inside(me + p - REACH2, n)
        r, i = invert(jnp.concatenate([rt, rb]) + 0.375, jnp.concatenate([it, ib]))
        return r * m, i * m

    def take1(which):
        def body(p):
            return unpack_two(pk1[which, p // half, p % half])

        return body

    def take2(which):
        def body(p):
            (rt, rb), (it, ib) = unpack_four(pk2[which, p])
            return jnp.concatenate([rt, rb]), jnp.concatenate([it, ib])

        return body

    def cycle(which, f, near):
        begin, end = depth, depth + own
        if which == 1:
            for copy in near_mat:
                copy.wait_recv()
            planes(begin - 2, end + 2, FINE, w0, weight0)
        for copy in near:
            copy.wait_recv()
        first_sweep(begin - 2, end + 2, FINE, va, f, w0)
        sweep(begin - 1, end + 1, FINE, vb, va, f, w0, 1, 1.0)

        def down(q):
            total = [None, None]
            for s in range(2):
                p = depth + 2 * q + s
                c = pick(mx[p], DIAG_TABLE)
                dr, di = mul(c[0], c[1], vb[0, p], vb[1, p])
                for k, d in enumerate((dr, di)):
                    e = (f[k, p] - d) + around(vb, k, p, 1)
                    total[k] = e if s == 0 else total[k] + e
            parts = [
                0.125 * pair_rows(pair_lanes(t, 1)) for k, t in enumerate(total)
            ]
            f1[0, mid1 + q] = parts[0]
            f1[1, mid1 + q] = parts[1]
            pk1[which, REACH1, q] = pack_two(parts[0], parts[1])

        for q in range(half):
            down(q)
        ones = send_one(which, 1, 1)
        ones.update(send_one(which, 2, REACH1))
        if which == 1:
            shifts1.update(send_one(0, 2, REACH1))
            shifts2.update(send_two(0))

        if which == 1:
            for d in (-1, 1):
                shifts1[d].wait_recv()
            planes(mid1 - half, mid1 + 2 * half, MIDDLE, w1, weight1)

        for d in (-1, 1):
            ones[d].wait_recv()
        planes(mid1 - half, mid1, MIDDLE, f1, take1(which))
        planes(mid1 + half, mid1 + 2 * half, MIDDLE, f1, take1(which))
        first_sweep(mid1 - 2, mid1 + half + 2, MIDDLE, v1a, f1, w1)
        sweep(mid1 - 1, mid1 + half + 1, MIDDLE, v1b, v1a, f1, w1, 2, 0.25)

        parts = []
        total = [None, None]
        for q in range(half):
            p = mid1 + q
            dr, di = mul(d1[0, q] + 1.5, d1[1, q], v1b[0, p], v1b[1, p])
            for k, d in enumerate((dr, di)):
                e = (f1[k, p] - d) + 0.25 * around(v1b, k, p, 2)
                total[k] = e if q == 0 else total[k] + e
        parts = [0.125 * pair_rows(pair_lanes(t, 2)) for k, t in enumerate(total)]
        pk2[which, REACH2] = pack_four(parts[0], parts[1])
        twos = send_two(which)
        if which == 1:
            far_mat = send_planes(mx, depth, mx, 4, False, False)
        far = send_planes(f, depth, f, 4 + 2 * which, False, True)

        if which == 1:
            for d in range(2, REACH1 + 1):
                shifts1[d].wait_recv()
                shifts1[-d].wait_recv()
            planes(1, mid1 - half, MIDDLE, w1, weight1)
            planes(mid1 + 2 * half, 2 * mid1 + half - 1, MIDDLE, w1, weight1)
        for d in range(2, REACH1 + 1):
            ones[d].wait_recv()
            ones[-d].wait_recv()
        planes(1, mid1 - half, MIDDLE, f1, take1(which))
        planes(mid1 + 2 * half, 2 * mid1 + half - 1, MIDDLE, f1, take1(which))
        first_sweep(1, mid1 - 2, MIDDLE, v1a, f1, w1)
        first_sweep(mid1 + half + 2, 2 * mid1 + half - 1, MIDDLE, v1a, f1, w1)
        sweep(2, mid1 - 1, MIDDLE, v1b, v1a, f1, w1, 2, 0.25)
        sweep(mid1 + half + 1, 2 * mid1 + half - 2, MIDDLE, v1b, v1a, f1, w1, 2, 0.25)
        if which == 1:
            for d in range(1, REACH2 + 1):
                shifts2[d].wait_recv()
                shifts2[-d].wait_recv()
            planes(0, 2 * REACH2 + 1, COARSE, w2, weight2)

        for d in range(1, REACH2 + 1):
            twos[d].wait_recv()
            twos[-d].wait_recv()
        planes(0, 2 * REACH2 + 1, COARSE, f2, take2(which))
        first_sweep(0, 2 * REACH2 + 1, COARSE, v2a, f2, w2)
        sweep(1, 2 * REACH2, COARSE, v2b, v2a, f2, w2, 4, 0.0625)
        sweep(2, 2 * REACH2 - 1, COARSE, v2a, v2b, f2, w2, 4, 0.0625)
        sweep(3, 2 * REACH2 - 2, COARSE, v2b, v2a, f2, w2, 4, 0.0625)

        def raise1(c):
            p = (c - REACH2 + REACH1) * half
            for k in range(2):
                x = spread_rows(v2b[k, c])
                v1b[k, p] = v1b[k, p] + x
                v1b[k, p + 1] = v1b[k, p + 1] + x

        for c in range(REACH2 - 2, REACH2 + 3):
            raise1(c)
        sweep(mid1 - 3, mid1 + half + 3, MIDDLE, v1a, v1b, f1, w1, 2, 0.25)
        sweep(mid1 - 2, mid1 + half + 2, MIDDLE, v1b, v1a, f1, w1, 2, 0.25)

        if which == 1:
            for copy in far_mat:
                copy.wait_recv()
            planes(0, begin - 2, FINE, w0, weight0)
            planes(end + 2, end + depth, FINE, w0, weight0)
        for copy in far:
            copy.wait_recv()
        first_sweep(0, begin - 2, FINE, va, f, w0)
        first_sweep(end + 2, end + depth, FINE, va, f, w0)
        sweep(1, begin - 1, FINE, vb, va, f, w0, 1, 1.0)
        sweep(end + 1, end + depth - 1, FINE, vb, va, f, w0, 1, 1.0)

        def raise0(c):
            p = depth + 2 * (c - mid1)
            for k in range(2):
                x = spread_rows(v1b[k, c])
                vb[k, p] = vb[k, p] + x
                vb[k, p + 1] = vb[k, p + 1] + x

        for c in range(mid1 - 2, mid1 + half + 2):
            raise0(c)
        sweep(begin - 2, end + 2, FINE, va, vb, f, w0, 1, 1.0)
        sweep(begin - 1, end + 1, FINE, vb, va, f, w0, 1, 1.0)

    def image_of(p):
        c = pick(mx[p], IMAGE_TABLE)
        r, i = mul(c[0], c[1], vb[0, p], vb[1, p])
        return r - around(vb, 0, p, 1), i - around(vb, 1, p, 1)

    def fold(x):
        rows, lanes = x.shape
        return jnp.sum(x.reshape(rows // 8, 8, lanes), axis=0)

    def share(which, sums):
        rows = [jnp.sum(s, axis=0, keepdims=True) for s in sums]
        rows.append(jnp.zeros((8 - len(rows), rows[0].shape[1]), F32))
        red[which, me] = jnp.concatenate(rows, axis=0)

        def post(k):
            pltpu.make_async_remote_copy(
                src_ref=red.at[which, me], dst_ref=red.at[which, me],
                send_sem=red_send.at[which, k], recv_sem=red_recv.at[which, k],
                device_id={"gz": lax.rem(me + k, n)}, device_id_type=pl.DeviceIdType.MESH,
            ).start()

        loop(1, n, post)

    def collect(which):
        def await_one(k):
            one = pltpu.make_async_remote_copy(
                src_ref=red.at[which, me], dst_ref=red.at[which, lax.rem(me + n - k, n)],
                send_sem=red_send.at[which, k], recv_sem=red_recv.at[which, k],
                device_id={"gz": lax.rem(me + k, n)}, device_id_type=pl.DeviceIdType.MESH,
            )
            one.wait_recv()
            one.wait_send()

        loop(1, n, await_one)
        total = red[which, 0]
        for j in range(1, n):
            total = total + red[which, j]
        total = jnp.sum(total, axis=1, keepdims=True)
        return total[0:1], total[1:2], total[2:3]

    def spectrum(which):
        def post(k):
            pltpu.make_async_remote_copy(
                src_ref=spec.at[which], dst_ref=spec.at[which],
                send_sem=spec_send.at[which, k], recv_sem=spec_recv.at[which],
                device_id={"gz": lax.rem(me + k, n)}, device_id_type=pl.DeviceIdType.MESH,
            ).start()

        @pl.when(me == n - 1)
        def _():
            last = depth + own - 1
            spec[which] = spectrum_of(vb[0, last], vb[1, last], ty[...], tx[...])
            loop(1, n, post)

    def orders_of(which):
        def settle(k):
            pltpu.make_async_remote_copy(
                src_ref=spec.at[which], dst_ref=spec.at[which],
                send_sem=spec_send.at[which, k], recv_sem=spec_recv.at[which],
                device_id={"gz": lax.rem(me + k, n)}, device_id_type=pl.DeviceIdType.MESH,
            ).wait_send()

        @pl.when(me == n - 1)
        def _():
            loop(1, n, settle)

        @pl.when(me != n - 1)
        def _():
            pltpu.make_async_remote_copy(
                src_ref=spec.at[which], dst_ref=spec.at[which],
                send_sem=spec_send.at[which, 0], recv_sem=spec_recv.at[which],
                device_id={"gz": lax.rem(me + 1, n)}, device_id_type=pl.DeviceIdType.MESH,
            ).wait_recv()

        count = ords.shape[1]
        x = ords[0:1] + ORD_HALF
        y = ords[1:2] + ORD_HALF
        row = lax.broadcasted_iota(jnp.int32, (2 * HALF, count), 0)
        pick_y = lax.broadcasted_iota(jnp.int32, (HARM, count), 0) == y
        out = []
        for k in range(2):
            pick_x = jnp.where(row == x + k * HALF, 1.0, 0.0).astype(F32)
            chosen = precise(spec[which], pick_x, ((1,), (0,)))
            out.append(jnp.sum(jnp.where(pick_y, chosen, 0.0), axis=0, keepdims=True))
        return out

    cycle(1, fx, near_src)

    zero = jnp.zeros((8, fx.shape[3]), F32)
    sums = [zero, zero, zero]
    for p in range(own):
        r, i = image_of(depth + p)
        gx[0, depth + p] = r
        gx[1, depth + p] = i
        a, b = src[0, p], src[1, p]
        sums[0] = sums[0] + fold(a * a + b * b)
        sums[1] = sums[1] + fold(a * r + b * i)
        sums[2] = sums[2] + fold(a * i - b * r)
    near_img = send_planes(gx, depth, gx, 10, True, True)
    share(0, sums)

    def keep(p):
        sol[0, p] = vb[0, depth + p]
        sol[1, p] = vb[1, depth + p]

    loop(0, own, keep)
    spectrum(0)

    cycle(2, gx, near_img)

    rho, cr, ci = collect(0)
    scale = rho / (cr * cr + ci * ci)
    ar, ai = cr * scale, -(ci * scale)

    sums = [zero, zero, zero]
    for p in range(own):
        e = depth + p
        r, i = image_of(e)
        gr, gi = gx[0, e], gx[1, e]
        tr, ti = mul(ar, ai, gr, gi)
        hr, hi = src[0, p] - tr, src[1, p] - ti
        tr, ti = mul(ar, ai, r, i)
        lr, li = gr - tr, gi - ti
        va[0, e], va[1, e] = lr, li
        raw[0, p], raw[1, p] = hr, hi
        sums[0] = sums[0] + fold(lr * hr + li * hi)
        sums[1] = sums[1] + fold(lr * hi - li * hr)
        sums[2] = sums[2] + fold(lr * lr + li * li)
    share(1, sums)
    spectrum(1)
    sdr, sdi = orders_of(0)

    along_r, along_i, norm = collect(1)
    wr, wi = along_r / norm, along_i / norm

    def finish(p):
        e = depth + p
        dr, di = sol[0, p], sol[1, p]
        tr, ti = mul(ar, ai, vb[0, e], vb[1, e])
        cr_, ci_ = mul(wr, wi, dr - tr, di - ti)
        xr, xi = mul(ar, ai, dr, di)
        solved = (xr + cr_, xi + ci_)
        tr, ti = mul(wr, wi, va[0, e], va[1, e])
        left = (raw[0, p] - tr, raw[1, p] - ti)
        for k in range(2):
            for at, row in quarters:
                sol[k, p, pl.ds(row, quarter, stride=4)] = solved[k][at : at + quarter]
                res[k, p, pl.ds(row, quarter, stride=4)] = left[k][at : at + quarter]

    for p in range(own):
        finish(p)

    sqr, sqi = orders_of(1)
    tr, ti = mul(ar, ai, sqr, sqi)
    cr_, ci_ = mul(wr, wi, sdr - tr, sdi - ti)
    xr, xi = mul(ar, ai, sdr, sdi)
    pup[0:1] = xr + cr_
    pup[1:2] = xi + ci_

    for copy in sent:
        copy.wait_send()


def on_device(n, source_term, material, orders):
    own, nx, ny = material.shape
    half = own // 2
    ty, tx = tables(nx, ny)
    vm = pltpu.VMEM
    fine = vm((2, 3 * own, nx, ny), F32)
    planes1 = (2 * REACH1 + 1) * half
    one = vm((2, planes1, nx // 2, ny), F32)
    planes2 = 2 * REACH2 + 1
    two = vm((2, planes2, nx // 4, ny), F32)
    dma = pltpu.SemaphoreType.DMA
    ext1 = 3 * (2 * REACH1 + 1)
    ext2 = 3 * planes2
    whole = pl.BlockSpec(memory_space=pltpu.VMEM)
    return pl.pallas_call(
        functools.partial(kernel, n),
        out_shape=(
            jax.ShapeDtypeStruct(source_term.shape, F32),
            jax.ShapeDtypeStruct(source_term.shape, F32),
            jax.ShapeDtypeStruct(orders.shape, F32),
        ),
        in_specs=[pl.BlockSpec(memory_space=pl.ANY)] * 5,
        out_specs=(whole,) * 3,
        scratch_shapes=[
            vm(orders.shape, jnp.int32), vm(ty.shape, F32), vm(tx.shape, F32), dma((5,)),
            fine, fine, vm((3 * own, nx, ny), jnp.int32), fine, fine, fine,
            vm((2, half, nx // 2, ny), F32), one, one, one, one,
            two, two, two, two, vm((2, nx // 4, ny), F32),
            vm((3, 2 * REACH1 + 1, half, nx // 2, ny), F32),
            vm((3, planes2, nx // 8, ny), F32),
            vm((2, own, nx, ny), F32),
            vm((own, nx, ny), jnp.int32),
            vm((2, n, 8, ny), F32),
            vm((2, HARM, 2 * HALF), F32),
            dma((12,)), dma((12,)), dma((ext1,)), dma((ext1,)), dma((ext2,)), dma((ext2,)),
            dma((2, n)), dma((2, n)), dma((2, n)), dma((2,)),
        ],
        compiler_params=pltpu.CompilerParams(
            collective_id=0, has_side_effects=True, vmem_limit_bytes=62 * 1024 * 1024
        ),
    )(source_term, material, orders, jnp.asarray(ty), jnp.asarray(tx))


def solution(mesh):
    return jax.shard_map(
        functools.partial(on_device, mesh.shape["gz"]),
        mesh=mesh,
        in_specs=(
            P(None, ("clip", "gz"), None, None),
            P(("clip", "gz"), None, None),
            P(None, "gz"),
        ),
        out_specs=(
            P(None, ("clip", "gz"), None, None),
            P(None, ("clip", "gz"), None, None),
            P(None, ("clip", "gz")),
        ),
        check_vma=False,
    )
```

```python
import functools
import math

import jax
import jax.numpy as jnp
import numpy as np
from jax import lax
from jax.experimental import pallas as pl
from jax.experimental.pallas import tpu as pltpu
from jax.sharding import PartitionSpec as P

ORD_HALF = 22
HELM_TABLE = ((-0.5, 0.0), (1.0, -1.4), (-1.2, 0.0))
SHIFT_TABLE = ((-0.5, -0.25), (1.0, -0.25 * math.sqrt(11.84)), (-1.2, -0.6))
RELAX = 0.8
REACH1 = 3
REACH2 = 5
HALF = 64
HARM = 48
F32 = jnp.float32


def weight_of(shift):
    bottom = complex(6.0 + shift[0], shift[1])
    value = RELAX / bottom
    return (value.real, value.imag)


WEIGHT_TABLE = tuple(weight_of(entry) for entry in SHIFT_TABLE)
DIAG_TABLE = tuple((6.0 + entry[0], entry[1]) for entry in SHIFT_TABLE)
IMAGE_TABLE = tuple((6.0 + entry[0], entry[1]) for entry in HELM_TABLE)


def pick(material, table):
    one = material == 1
    two = material == 2
    return tuple(
        jnp.where(one, table[1][k], jnp.where(two, table[2][k], table[0][k])).astype(F32)
        for k in range(2)
    )


def mul(ar, ai, br, bi):
    return ar * br - ai * bi, ar * bi + ai * br


class Message:
    def __init__(self, copy, sends, receives):
        self.copy, self.sends, self.receives = copy, sends, receives

    def start(self):
        pl.when(self.sends)(lambda: self.copy.start())

    def wait_send(self):
        pl.when(self.sends)(lambda: self.copy.wait_send())

    def wait_recv(self):
        pl.when(self.receives)(lambda: self.copy.wait_recv())


def loop(lo, hi, body):
    def step(p, carry):
        body(p)
        return carry

    lax.fori_loop(lo, hi, step, 0)


def planes(lo, hi, group, dst, body):
    def some(first, count):
        values = [body(first + j) for j in range(count)]
        for j, (r, i) in enumerate(values):
            dst[0, first + j] = r
            dst[1, first + j] = i

    steps = (hi - lo) // group
    if steps == 1:
        some(lo, group)
    elif steps > 1:
        loop(0, steps, lambda t: some(lo + t * group, group))
    if (hi - lo) % group:
        some(lo + steps * group, (hi - lo) % group)


FINE, MIDDLE, COARSE = 2, 4, 6


def row_neighbours(x, lane_step):
    if lane_step == 4:
        return pltpu.roll(x, 1, 0) + pltpu.roll(x, x.shape[0] - 1, 0)
    if lane_step == 2:
        h = x.shape[0] // 2
        even, odd = x[:h], x[h:]
        return jnp.concatenate([odd + pltpu.roll(odd, 1, 0), even + pltpu.roll(even, h - 1, 0)])
    q = x.shape[0] // 4
    a, b, c, d = (x[j * q : (j + 1) * q] for j in range(4))
    return jnp.concatenate([c + pltpu.roll(d, 1, 0), c + d, a + b, b + pltpu.roll(a, q - 1, 0)])


def split_rows(rows):
    q = rows // 4
    return [((2 * c + b) * q, 2 * b + c) for c in range(2) for b in range(2)]


def around(ref, k, p, lane_step):
    x = ref[k, p]
    lanes = x.shape[1]
    total = ref[k, p - 1] + ref[k, p + 1]
    total = total + row_neighbours(x, lane_step)
    return total + (pltpu.roll(x, lane_step, 1) + pltpu.roll(x, lanes - lane_step, 1))


def first_sweep(lo, hi, group, dst, rhs, weight):
    planes(lo, hi, group, dst, lambda p: mul(weight[0, p], weight[1, p], rhs[0, p], rhs[1, p]))


def sweep(lo, hi, group, dst, old, rhs, weight, lane_step, h2):
    def body(p):
        nr = around(old, 0, p, lane_step)
        ni = around(old, 1, p, lane_step)
        if h2 != 1.0:
            nr, ni = nr * h2, ni * h2
        r, i = mul(weight[0, p], weight[1, p], rhs[0, p] + nr, rhs[1, p] + ni)
        return (1.0 - RELAX) * old[0, p] + r, (1.0 - RELAX) * old[1, p] + i

    planes(lo, hi, group, dst, body)


def lane_iota(shape):
    return lax.broadcasted_iota(jnp.int32, shape, 1)


def pair_lanes(x, step):
    lanes = x.shape[1]
    low = (lane_iota(x.shape) & step) == 0
    return x + jnp.where(low, pltpu.roll(x, lanes - step, 1), pltpu.roll(x, step, 1))


def pair_rows(x):
    h = x.shape[0] // 2
    return x[:h] + x[h:]


def spread_rows(x):
    return jnp.concatenate([x, x])


def pack_two(r, i):
    return jnp.where((lane_iota(r.shape) & 1) == 0, r, i)


def unpack_two(x):
    lanes = x.shape[1]
    even = (lane_iota(x.shape) & 1) == 0
    return jnp.where(even, x, pltpu.roll(x, 1, 1)), jnp.where(even, pltpu.roll(x, lanes - 1, 1), x)


def pack_four(r, i):
    rows = r.shape[0] // 2
    top = pack_two(r[:rows], i[:rows])
    low = pack_two(r[rows:], i[rows:])
    return jnp.where((lane_iota(top.shape) & 2) == 0, top, low)


def unpack_four(x):
    lanes = x.shape[1]
    first = (lane_iota(x.shape) & 2) == 0
    halves = []
    for y in unpack_two(x):
        halves.append(
            (jnp.where(first, y, pltpu.roll(y, 2, 1)), jnp.where(first, pltpu.roll(y, lanes - 2, 1), y))
        )
    return halves


def invert(r, i):
    bottom = 1.0 / (r * r + i * i)
    return RELAX * r * bottom, -RELAX * i * bottom


def precise(a, b, dims):
    return lax.dot_general(
        a, b, (dims, ((), ())), precision=lax.Precision.HIGHEST, preferred_element_type=F32
    )


def spectrum_of(r, i, ty, tx):
    gr = precise(ty, r, ((1,), (1,)))
    gi = precise(ty, i, ((1,), (1,)))
    inner = jnp.concatenate([gr[:HALF] - gi[HALF:], gr[HALF:] + gi[:HALF]], axis=0)
    outer = precise(inner, tx, ((1,), (0,)))
    turned = pltpu.roll(outer[HALF:], HALF, 1)
    left = lane_iota(turned.shape) < HALF
    return (outer[:HALF] + jnp.where(left, -turned, turned))[:HARM]


def tables(nx, ny):
    harmonics = np.arange(2 * ORD_HALF + 1) - ORD_HALF
    count = harmonics.size
    ty = np.zeros((2 * HALF, ny), np.float32)
    angle = 2.0 * np.pi * ((harmonics[:, None] * np.arange(ny)[None, :]) % ny) / ny
    ty[:count] = np.cos(angle)
    ty[HALF : HALF + count] = -np.sin(angle)
    tx = np.zeros((nx, 2 * HALF), np.float32)
    angle = 2.0 * np.pi * ((np.arange(nx)[:, None] * harmonics[None, :]) % nx) / nx
    scale = 1.0 / math.sqrt(nx * ny)
    tx[:, :count] = np.cos(angle) * scale
    tx[:, HALF : HALF + count] = -np.sin(angle) * scale
    tx = np.concatenate([tx[row::4] for _, row in split_rows(nx)])
    return ty, tx


def kernel(
    n, src_in, mat_in, ords_in, ty_in, tx_in, sol, res, pup,
    ords, ty, tx, in_sem, fx, gx, mx, w0, va, vb, d1, w1, f1, v1a, v1b, w2, f2, v2a, v2b, d2,
    pk1, pk2, raw, raw_mat, red, spec,
    fine_send, fine_recv, k1_send, k1_recv, k2_send, k2_recv,
    red_send, red_recv, spec_send, spec_recv,
):
    me = lax.axis_index("gz")
    own = mat_in.shape[0]
    depth = own
    half = own // 2
    mid1 = REACH1 * half
    sent = []

    def there(k):
        return me < n - k if k > 0 else me >= -k

    def other(k):
        return {"gz": lax.rem(me + k + n, n)}

    def start(source, target, ssem, rsem, k):
        copy = pltpu.make_async_remote_copy(
            src_ref=source, dst_ref=target, send_sem=ssem, recv_sem=rsem,
            device_id=other(k), device_id_type=pl.DeviceIdType.MESH,
        )
        message = Message(copy, there(k), there(-k))
        message.start()
        sent.append(message)
        return message

    barrier = pltpu.get_barrier_semaphore()

    def greet(k):
        pl.semaphore_signal(
            barrier, inc=1, device_id={"gz": lax.rem(me + k, n)},
            device_id_type=pl.DeviceIdType.MESH,
        )

    def clear(ref):
        ref[...] = jnp.zeros(ref.shape, ref.dtype)

    for d in range(1, REACH2 + 1):
        for k in (d, -d):

            @pl.when(jnp.logical_not(there(k)))
            def _():
                for which in range(3):
                    clear(pk2.at[which, REACH2 + k])
                    if d <= REACH1:
                        clear(pk1.at[which, REACH1 + k])
                if d == 1:
                    rim = pl.ds(depth + own if k > 0 else 0, depth)
                    clear(mx.at[rim])
                    clear(fx.at[:, rim])
                    clear(gx.at[:, rim])

    loop(1, n, greet)

    src = fx.at[:, pl.ds(depth, own)]
    mat = mx.at[pl.ds(depth, own)]
    fetches = [
        pltpu.make_async_copy(a, b, in_sem.at[k])
        for k, (a, b) in enumerate(
            ((mat_in, raw_mat), (src_in, raw), (ords_in, ords), (ty_in, ty), (tx_in, tx))
        )
    ]
    for fetch in fetches:
        fetch.start()
    quarter = mat_in.shape[1] // 4
    quarters = split_rows(mat_in.shape[1])
    fetches[0].wait()
    for p in range(own):
        for at, row in quarters:
            mat[p, at : at + quarter] = raw_mat[p, pl.ds(row, quarter, stride=4)]

    for p in range(half):
        a = pick(mat[2 * p], SHIFT_TABLE)
        b = pick(mat[2 * p + 1], SHIFT_TABLE)
        for k in range(2):
            d1[k, p] = 0.125 * pair_rows(pair_lanes(a[k] + b[k], 1))
        pk1[0, REACH1, p] = pack_two(d1[0, p], d1[1, p])
    for k in range(2):
        d2[k] = 0.125 * pair_rows(pair_lanes(d1[k, 0] + d1[k, 1], 2))
    pk2[0, REACH2] = pack_four(d2[0], d2[1])

    for fetch in fetches[1:]:
        fetch.wait()
    for p in range(own):
        for at, row in quarters:
            for k in range(2):
                src[k, p, at : at + quarter] = raw[k, p, pl.ds(row, quarter, stride=4)]
    pl.semaphore_wait(barrier, n - 1)

    def send_planes(source, base, target, slot, near, dims):
        up_from = half if near else 0
        up_to = half if near else 0
        down_from = 0 if near else half
        down_to = depth + own + (0 if near else half)
        copies = []
        for which, (k, a, b) in enumerate(((1, up_from, up_to), (-1, down_from, down_to))):
            s = pl.ds(base + a, half)
            t = pl.ds(b, half)
            one = source.at[:, s] if dims else source.at[s]
            two = target.at[:, t] if dims else target.at[t]
            copies.append(
                start(one, two, fine_send.at[slot + which], fine_recv.at[slot + which], k)
            )
        return copies

    def send_one(which, lo, hi):
        copies = {}
        for k in range(lo, hi + 1):
            for d in (k, -k):
                at = which * (2 * REACH1 + 1) + REACH1 - d
                part = pl.ds(0, half)
                if k == REACH1:
                    part = pl.ds(half - 1 if d > 0 else 0, 1)
                copies[-d] = start(
                    pk1.at[which, REACH1, part], pk1.at[which, REACH1 - d, part],
                    k1_send.at[at], k1_recv.at[at], d,
                )
        return copies

    def send_two(which):
        copies = {}
        for k in range(1, REACH2 + 1):
            for d in (k, -k):
                at = which * (2 * REACH2 + 1) + REACH2 - d
                copies[-d] = start(
                    pk2.at[which, REACH2], pk2.at[which, REACH2 - d],
                    k2_send.at[at], k2_recv.at[at], d,
                )
        return copies

    near_mat = send_planes(mx, depth, mx, 0, True, False)
    near_src = send_planes(fx, depth, fx, 2, True, True)
    shifts1 = send_one(0, 1, 1)
    shifts2 = {}

    def inside(plane, count):
        return jnp.where(jnp.logical_and(plane >= 0, plane < count), 1.0, 0.0).astype(F32)

    def weight0(p):
        m = inside(me * own + p - depth, n * own)
        r, i = pick(mx[p], WEIGHT_TABLE)
        return r * m, i * m

    def weight1(p):
        r, i = unpack_two(pk1[0, p // half, p % half])
        r, i = invert(r + 1.5, i)
        m = inside(me * half + p - mid1, n * half)
        return r * m, i * m

    def weight2(p):
        (rt, rb), (it, ib) = unpack_four(pk2[0, p])
        m = inside(me + p - REACH2, n)
        r, i = invert(jnp.concatenate([rt, rb]) + 0.375, jnp.concatenate([it, ib]))
        return r * m, i * m

    def take1(which):
        def body(p):
            return unpack_two(pk1[which, p // half, p % half])

        return body

    def take2(which):
        def body(p):
            (rt, rb), (it, ib) = unpack_four(pk2[which, p])
            return jnp.concatenate([rt, rb]), jnp.concatenate([it, ib])

        return body

    def cycle(which, f, near):
        begin, end = depth, depth + own
        if which == 1:
            planes(begin, end, FINE, w0, weight0)
        first_sweep(begin, end, FINE, va, f, w0)
        sweep(begin + 1, end - 1, FINE, vb, va, f, w0, 1, 1.0)
        if which == 1:
            for copy in near_mat:
                copy.wait_recv()
            planes(begin - 2, begin, FINE, w0, weight0)
            planes(end, end + 2, FINE, w0, weight0)
        for copy in near:
            copy.wait_recv()
        first_sweep(begin - 2, begin, FINE, va, f, w0)
        first_sweep(end, end + 2, FINE, va, f, w0)
        sweep(begin - 1, begin + 1, FINE, vb, va, f, w0, 1, 1.0)
        sweep(end - 1, end + 1, FINE, vb, va, f, w0, 1, 1.0)

        def down(q):
            total = [None, None]
            for s in range(2):
                p = depth + 2 * q + s
                c = pick(mx[p], DIAG_TABLE)
                dr, di = mul(c[0], c[1], vb[0, p], vb[1, p])
                for k, d in enumerate((dr, di)):
                    e = (f[k, p] - d) + around(vb, k, p, 1)
                    total[k] = e if s == 0 else total[k] + e
            parts = [
                0.125 * pair_rows(pair_lanes(t, 1)) for k, t in enumerate(total)
            ]
            f1[0, mid1 + q] = parts[0]
            f1[1, mid1 + q] = parts[1]
            pk1[which, REACH1, q] = pack_two(parts[0], parts[1])

        for q in range(half):
            down(q)
        ones = send_one(which, 1, 1)
        ones.update(send_one(which, 2, REACH1))
        if which == 1:
            shifts1.update(send_one(0, 2, REACH1))
            shifts2.update(send_two(0))

        if which == 1:
            for d in (-1, 1):
                shifts1[d].wait_recv()
            planes(mid1 - half, mid1 + 2 * half, MIDDLE, w1, weight1)

        for d in (-1, 1):
            ones[d].wait_recv()
        planes(mid1 - half, mid1, MIDDLE, f1, take1(which))
        planes(mid1 + half, mid1 + 2 * half, MIDDLE, f1, take1(which))
        first_sweep(mid1 - 2, mid1 + half + 2, MIDDLE, v1a, f1, w1)
        sweep(mid1 - 1, mid1 + half + 1, MIDDLE, v1b, v1a, f1, w1, 2, 0.25)

        parts = []
        total = [None, None]
        for q in range(half):
            p = mid1 + q
            dr, di = mul(d1[0, q] + 1.5, d1[1, q], v1b[0, p], v1b[1, p])
            for k, d in enumerate((dr, di)):
                e = (f1[k, p] - d) + 0.25 * around(v1b, k, p, 2)
                total[k] = e if q == 0 else total[k] + e
        parts = [0.125 * pair_rows(pair_lanes(t, 2)) for k, t in enumerate(total)]
        pk2[which, REACH2] = pack_four(parts[0], parts[1])
        twos = send_two(which)
        if which == 1:
            far_mat = send_planes(mx, depth, mx, 4, False, False)
        far = send_planes(f, depth, f, 4 + 2 * which, False, True)

        if which == 1:
            for d in range(2, REACH1 + 1):
                shifts1[d].wait_recv()
                shifts1[-d].wait_recv()
            planes(1, mid1 - half, MIDDLE, w1, weight1)
            planes(mid1 + 2 * half, 2 * mid1 + half - 1, MIDDLE, w1, weight1)
        for d in range(2, REACH1 + 1):
            ones[d].wait_recv()
            ones[-d].wait_recv()
        planes(1, mid1 - half, MIDDLE, f1, take1(which))
        planes(mid1 + 2 * half, 2 * mid1 + half - 1, MIDDLE, f1, take1(which))
        first_sweep(1, mid1 - 2, MIDDLE, v1a, f1, w1)
        first_sweep(mid1 + half + 2, 2 * mid1 + half - 1, MIDDLE, v1a, f1, w1)
        sweep(2, mid1 - 1, MIDDLE, v1b, v1a, f1, w1, 2, 0.25)
        sweep(mid1 + half + 1, 2 * mid1 + half - 2, MIDDLE, v1b, v1a, f1, w1, 2, 0.25)
        if which == 1:
            for d in range(1, REACH2 + 1):
                shifts2[d].wait_recv()
                shifts2[-d].wait_recv()
            planes(0, 2 * REACH2 + 1, COARSE, w2, weight2)

        for d in range(1, REACH2 + 1):
            twos[d].wait_recv()
            twos[-d].wait_recv()
        planes(0, 2 * REACH2 + 1, COARSE, f2, take2(which))
        first_sweep(0, 2 * REACH2 + 1, COARSE, v2a, f2, w2)
        sweep(1, 2 * REACH2, COARSE, v2b, v2a, f2, w2, 4, 0.0625)
        sweep(2, 2 * REACH2 - 1, COARSE, v2a, v2b, f2, w2, 4, 0.0625)
        sweep(3, 2 * REACH2 - 2, COARSE, v2b, v2a, f2, w2, 4, 0.0625)

        def raise1(c):
            p = (c - REACH2 + REACH1) * half
            for k in range(2):
                x = spread_rows(v2b[k, c])
                v1b[k, p] = v1b[k, p] + x
                v1b[k, p + 1] = v1b[k, p + 1] + x

        for c in range(REACH2 - 2, REACH2 + 3):
            raise1(c)
        sweep(mid1 - 3, mid1 + half + 3, MIDDLE, v1a, v1b, f1, w1, 2, 0.25)
        sweep(mid1 - 2, mid1 + half + 2, MIDDLE, v1b, v1a, f1, w1, 2, 0.25)

        if which == 1:
            for copy in far_mat:
                copy.wait_recv()
            planes(0, begin - 2, FINE, w0, weight0)
            planes(end + 2, end + depth, FINE, w0, weight0)
        for copy in far:
            copy.wait_recv()
        first_sweep(0, begin - 2, FINE, va, f, w0)
        first_sweep(end + 2, end + depth, FINE, va, f, w0)
        sweep(1, begin - 1, FINE, vb, va, f, w0, 1, 1.0)
        sweep(end + 1, end + depth - 1, FINE, vb, va, f, w0, 1, 1.0)

        def raise0(c):
            p = depth + 2 * (c - mid1)
            for k in range(2):
                x = spread_rows(v1b[k, c])
                vb[k, p] = vb[k, p] + x
                vb[k, p + 1] = vb[k, p + 1] + x

        for c in range(mid1 - 2, mid1 + half + 2):
            raise0(c)
        sweep(begin - 2, end + 2, FINE, va, vb, f, w0, 1, 1.0)
        sweep(begin - 1, end + 1, FINE, vb, va, f, w0, 1, 1.0)

    def image_of(p):
        c = pick(mx[p], IMAGE_TABLE)
        r, i = mul(c[0], c[1], vb[0, p], vb[1, p])
        return r - around(vb, 0, p, 1), i - around(vb, 1, p, 1)

    def fold(x):
        rows, lanes = x.shape
        return jnp.sum(x.reshape(rows // 8, 8, lanes), axis=0)

    def share(which, sums):
        rows = [jnp.sum(s, axis=0, keepdims=True) for s in sums]
        rows.append(jnp.zeros((8 - len(rows), rows[0].shape[1]), F32))
        red[which, me] = jnp.concatenate(rows, axis=0)

        def post(k):
            pltpu.make_async_remote_copy(
                src_ref=red.at[which, me], dst_ref=red.at[which, me],
                send_sem=red_send.at[which, k], recv_sem=red_recv.at[which, k],
                device_id={"gz": lax.rem(me + k, n)}, device_id_type=pl.DeviceIdType.MESH,
            ).start()

        loop(1, n, post)

    def collect(which):
        def await_one(k):
            one = pltpu.make_async_remote_copy(
                src_ref=red.at[which, me], dst_ref=red.at[which, lax.rem(me + n - k, n)],
                send_sem=red_send.at[which, k], recv_sem=red_recv.at[which, k],
                device_id={"gz": lax.rem(me + k, n)}, device_id_type=pl.DeviceIdType.MESH,
            )
            one.wait_recv()
            one.wait_send()

        loop(1, n, await_one)
        total = red[which, 0]
        for j in range(1, n):
            total = total + red[which, j]
        total = jnp.sum(total, axis=1, keepdims=True)
        return total[0:1], total[1:2], total[2:3]

    def spectrum(which):
        def post(k):
            pltpu.make_async_remote_copy(
                src_ref=spec.at[which], dst_ref=spec.at[which],
                send_sem=spec_send.at[which, k], recv_sem=spec_recv.at[which],
                device_id={"gz": lax.rem(me + k, n)}, device_id_type=pl.DeviceIdType.MESH,
            ).start()

        @pl.when(me == n - 1)
        def _():
            last = depth + own - 1
            spec[which] = spectrum_of(vb[0, last], vb[1, last], ty[...], tx[...])
            loop(1, n, post)

    def orders_of(which):
        def settle(k):
            pltpu.make_async_remote_copy(
                src_ref=spec.at[which], dst_ref=spec.at[which],
                send_sem=spec_send.at[which, k], recv_sem=spec_recv.at[which],
                device_id={"gz": lax.rem(me + k, n)}, device_id_type=pl.DeviceIdType.MESH,
            ).wait_send()

        @pl.when(me == n - 1)
        def _():
            loop(1, n, settle)

        @pl.when(me != n - 1)
        def _():
            pltpu.make_async_remote_copy(
                src_ref=spec.at[which], dst_ref=spec.at[which],
                send_sem=spec_send.at[which, 0], recv_sem=spec_recv.at[which],
                device_id={"gz": lax.rem(me + 1, n)}, device_id_type=pl.DeviceIdType.MESH,
            ).wait_recv()

        count = ords.shape[1]
        x = ords[0:1] + ORD_HALF
        y = ords[1:2] + ORD_HALF
        row = lax.broadcasted_iota(jnp.int32, (2 * HALF, count), 0)
        pick_y = lax.broadcasted_iota(jnp.int32, (HARM, count), 0) == y
        out = []
        for k in range(2):
            pick_x = jnp.where(row == x + k * HALF, 1.0, 0.0).astype(F32)
            chosen = precise(spec[which], pick_x, ((1,), (0,)))
            out.append(jnp.sum(jnp.where(pick_y, chosen, 0.0), axis=0, keepdims=True))
        return out

    cycle(1, fx, near_src)

    zero = jnp.zeros((8, fx.shape[3]), F32)
    sums = [zero, zero, zero]
    for p in range(own):
        r, i = image_of(depth + p)
        gx[0, depth + p] = r
        gx[1, depth + p] = i
        a, b = src[0, p], src[1, p]
        sums[0] = sums[0] + fold(a * a + b * b)
        sums[1] = sums[1] + fold(a * r + b * i)
        sums[2] = sums[2] + fold(a * i - b * r)
    near_img = send_planes(gx, depth, gx, 10, True, True)
    share(0, sums)

    def keep(p):
        sol[0, p] = vb[0, depth + p]
        sol[1, p] = vb[1, depth + p]

    loop(0, own, keep)
    spectrum(0)

    cycle(2, gx, near_img)

    rho, cr, ci = collect(0)
    scale = rho / (cr * cr + ci * ci)
    ar, ai = cr * scale, -(ci * scale)

    sums = [zero, zero, zero]
    for p in range(own):
        e = depth + p
        r, i = image_of(e)
        gr, gi = gx[0, e], gx[1, e]
        tr, ti = mul(ar, ai, gr, gi)
        hr, hi = src[0, p] - tr, src[1, p] - ti
        tr, ti = mul(ar, ai, r, i)
        lr, li = gr - tr, gi - ti
        va[0, e], va[1, e] = lr, li
        raw[0, p], raw[1, p] = hr, hi
        sums[0] = sums[0] + fold(lr * hr + li * hi)
        sums[1] = sums[1] + fold(lr * hi - li * hr)
        sums[2] = sums[2] + fold(lr * lr + li * li)
    share(1, sums)
    spectrum(1)
    sdr, sdi = orders_of(0)

    for copy in sent:
        copy.wait_send()

    along_r, along_i, norm = collect(1)
    wr, wi = along_r / norm, along_i / norm

    def finish(p):
        e = depth + p
        dr, di = sol[0, p], sol[1, p]
        tr, ti = mul(ar, ai, vb[0, e], vb[1, e])
        cr_, ci_ = mul(wr, wi, dr - tr, di - ti)
        xr, xi = mul(ar, ai, dr, di)
        solved = (xr + cr_, xi + ci_)
        tr, ti = mul(wr, wi, va[0, e], va[1, e])
        left = (raw[0, p] - tr, raw[1, p] - ti)
        for k in range(2):
            for at, row in quarters:
                sol[k, p, pl.ds(row, quarter, stride=4)] = solved[k][at : at + quarter]
                res[k, p, pl.ds(row, quarter, stride=4)] = left[k][at : at + quarter]

    for p in range(own):
        finish(p)

    sqr, sqi = orders_of(1)
    tr, ti = mul(ar, ai, sqr, sqi)
    cr_, ci_ = mul(wr, wi, sdr - tr, sdi - ti)
    xr, xi = mul(ar, ai, sdr, sdi)
    pup[0:1] = xr + cr_
    pup[1:2] = xi + ci_


def on_device(n, source_term, material, orders):
    own, nx, ny = material.shape
    half = own // 2
    ty, tx = tables(nx, ny)
    vm = pltpu.VMEM
    fine = vm((2, 3 * own, nx, ny), F32)
    planes1 = (2 * REACH1 + 1) * half
    one = vm((2, planes1, nx // 2, ny), F32)
    planes2 = 2 * REACH2 + 1
    two = vm((2, planes2, nx // 4, ny), F32)
    dma = pltpu.SemaphoreType.DMA
    ext1 = 3 * (2 * REACH1 + 1)
    ext2 = 3 * planes2
    whole = pl.BlockSpec(memory_space=pltpu.VMEM)
    return pl.pallas_call(
        functools.partial(kernel, n),
        out_shape=(
            jax.ShapeDtypeStruct(source_term.shape, F32),
            jax.ShapeDtypeStruct(source_term.shape, F32),
            jax.ShapeDtypeStruct(orders.shape, F32),
        ),
        in_specs=[pl.BlockSpec(memory_space=pl.ANY)] * 5,
        out_specs=(whole,) * 3,
        scratch_shapes=[
            vm(orders.shape, jnp.int32), vm(ty.shape, F32), vm(tx.shape, F32), dma((5,)),
            fine, fine, vm((3 * own, nx, ny), jnp.int32), fine, fine, fine,
            vm((2, half, nx // 2, ny), F32), one, one, one, one,
            two, two, two, two, vm((2, nx // 4, ny), F32),
            vm((3, 2 * REACH1 + 1, half, nx // 2, ny), F32),
            vm((3, planes2, nx // 8, ny), F32),
            vm((2, own, nx, ny), F32),
            vm((own, nx, ny), jnp.int32),
            vm((2, n, 8, ny), F32),
            vm((2, HARM, 2 * HALF), F32),
            dma((12,)), dma((12,)), dma((ext1,)), dma((ext1,)), dma((ext2,)), dma((ext2,)),
            dma((2, n)), dma((2, n)), dma((2, n)), dma((2,)),
        ],
        compiler_params=pltpu.CompilerParams(
            collective_id=0, has_side_effects=True, vmem_limit_bytes=62 * 1024 * 1024
        ),
    )(source_term, material, orders, jnp.asarray(ty), jnp.asarray(tx))


def solution(mesh):
    return jax.shard_map(
        functools.partial(on_device, mesh.shape["gz"]),
        mesh=mesh,
        in_specs=(
            P(None, ("clip", "gz"), None, None),
            P(("clip", "gz"), None, None),
            P(None, "gz"),
        ),
        out_specs=(
            P(None, ("clip", "gz"), None, None),
            P(None, ("clip", "gz"), None, None),
            P(None, ("clip", "gz")),
        ),
        check_vma=False,
    )
```

```python
import functools
import math

import jax
import jax.numpy as jnp
import numpy as np
from jax import lax
from jax.experimental import pallas as pl
from jax.experimental.pallas import tpu as pltpu
from jax.sharding import PartitionSpec as P

ORD_HALF = 22
HELM_TABLE = ((-0.5, 0.0), (1.0, -1.4), (-1.2, 0.0))
SHIFT_TABLE = ((-0.5, -0.25), (1.0, -0.25 * math.sqrt(11.84)), (-1.2, -0.6))
RELAX = 0.8
REACH1 = 3
REACH2 = 5
HALF = 64
HARM = 48
F32 = jnp.float32


def weight_of(shift):
    bottom = complex(6.0 + shift[0], shift[1])
    value = RELAX / bottom
    return (value.real, value.imag)


WEIGHT_TABLE = tuple(weight_of(entry) for entry in SHIFT_TABLE)
DIAG_TABLE = tuple((6.0 + entry[0], entry[1]) for entry in SHIFT_TABLE)
IMAGE_TABLE = tuple((6.0 + entry[0], entry[1]) for entry in HELM_TABLE)


def pick(material, table):
    one = material == 1
    two = material == 2
    return tuple(
        jnp.where(one, table[1][k], jnp.where(two, table[2][k], table[0][k])).astype(F32)
        for k in range(2)
    )


def mul(ar, ai, br, bi):
    return ar * br - ai * bi, ar * bi + ai * br


class Message:
    def __init__(self, copy, sends, receives):
        self.copy, self.sends, self.receives = copy, sends, receives

    def start(self):
        pl.when(self.sends)(lambda: self.copy.start())

    def wait_send(self):
        pl.when(self.sends)(lambda: self.copy.wait_send())

    def wait_recv(self):
        pl.when(self.receives)(lambda: self.copy.wait_recv())


def loop(lo, hi, body):
    def step(p, carry):
        body(p)
        return carry

    lax.fori_loop(lo, hi, step, 0)


def planes(lo, hi, group, dst, body):
    def some(first, count):
        values = [body(first + j) for j in range(count)]
        for j, (r, i) in enumerate(values):
            dst[0, first + j] = r
            dst[1, first + j] = i

    steps = (hi - lo) // group
    if steps == 1:
        some(lo, group)
    elif steps > 1:
        loop(0, steps, lambda t: some(lo + t * group, group))
    if (hi - lo) % group:
        some(lo + steps * group, (hi - lo) % group)


FINE, MIDDLE, COARSE = 4, 5, 11


def row_neighbours(x, lane_step):
    if lane_step == 4:
        return pltpu.roll(x, 1, 0) + pltpu.roll(x, x.shape[0] - 1, 0)
    if lane_step == 2:
        h = x.shape[0] // 2
        even, odd = x[:h], x[h:]
        return jnp.concatenate([odd + pltpu.roll(odd, 1, 0), even + pltpu.roll(even, h - 1, 0)])
    q = x.shape[0] // 4
    a, b, c, d = (x[j * q : (j + 1) * q] for j in range(4))
    return jnp.concatenate([c + pltpu.roll(d, 1, 0), c + d, a + b, b + pltpu.roll(a, q - 1, 0)])


def split_rows(rows):
    q = rows // 4
    return [((2 * c + b) * q, 2 * b + c) for c in range(2) for b in range(2)]


def around(ref, k, p, lane_step):
    x = ref[k, p]
    lanes = x.shape[1]
    total = ref[k, p - 1] + ref[k, p + 1]
    total = total + row_neighbours(x, lane_step)
    return total + (pltpu.roll(x, lane_step, 1) + pltpu.roll(x, lanes - lane_step, 1))


def first_sweep(lo, hi, group, dst, rhs, weight):
    planes(lo, hi, group, dst, lambda p: mul(weight[0, p], weight[1, p], rhs[0, p], rhs[1, p]))


def sweep(lo, hi, group, dst, old, rhs, weight, lane_step, h2):
    def body(p):
        nr = around(old, 0, p, lane_step)
        ni = around(old, 1, p, lane_step)
        if h2 != 1.0:
            nr, ni = nr * h2, ni * h2
        r, i = mul(weight[0, p], weight[1, p], rhs[0, p] + nr, rhs[1, p] + ni)
        return (1.0 - RELAX) * old[0, p] + r, (1.0 - RELAX) * old[1, p] + i

    planes(lo, hi, group, dst, body)


def lane_iota(shape):
    return lax.broadcasted_iota(jnp.int32, shape, 1)


def pair_lanes(x, step):
    lanes = x.shape[1]
    low = (lane_iota(x.shape) & step) == 0
    return x + jnp.where(low, pltpu.roll(x, lanes - step, 1), pltpu.roll(x, step, 1))


def pair_rows(x):
    h = x.shape[0] // 2
    return x[:h] + x[h:]


def spread_rows(x):
    return jnp.concatenate([x, x])


def pack_two(r, i):
    return jnp.where((lane_iota(r.shape) & 1) == 0, r, i)


def unpack_two(x):
    lanes = x.shape[1]
    even = (lane_iota(x.shape) & 1) == 0
    return jnp.where(even, x, pltpu.roll(x, 1, 1)), jnp.where(even, pltpu.roll(x, lanes - 1, 1), x)


def pack_four(r, i):
    rows = r.shape[0] // 2
    top = pack_two(r[:rows], i[:rows])
    low = pack_two(r[rows:], i[rows:])
    return jnp.where((lane_iota(top.shape) & 2) == 0, top, low)


def unpack_four(x):
    lanes = x.shape[1]
    first = (lane_iota(x.shape) & 2) == 0
    halves = []
    for y in unpack_two(x):
        halves.append(
            (jnp.where(first, y, pltpu.roll(y, 2, 1)), jnp.where(first, pltpu.roll(y, lanes - 2, 1), y))
        )
    return halves


def invert(r, i):
    bottom = 1.0 / (r * r + i * i)
    return RELAX * r * bottom, -RELAX * i * bottom


def precise(a, b, dims):
    return lax.dot_general(
        a, b, (dims, ((), ())), precision=lax.Precision.HIGHEST, preferred_element_type=F32
    )


def spectrum_of(r, i, ty, tx):
    gr = precise(ty, r, ((1,), (1,)))
    gi = precise(ty, i, ((1,), (1,)))
    inner = jnp.concatenate([gr[:HALF] - gi[HALF:], gr[HALF:] + gi[:HALF]], axis=0)
    outer = precise(inner, tx, ((1,), (0,)))
    turned = pltpu.roll(outer[HALF:], HALF, 1)
    left = lane_iota(turned.shape) < HALF
    return (outer[:HALF] + jnp.where(left, -turned, turned))[:HARM]


def tables(nx, ny):
    harmonics = np.arange(2 * ORD_HALF + 1) - ORD_HALF
    count = harmonics.size
    ty = np.zeros((2 * HALF, ny), np.float32)
    angle = 2.0 * np.pi * ((harmonics[:, None] * np.arange(ny)[None, :]) % ny) / ny
    ty[:count] = np.cos(angle)
    ty[HALF : HALF + count] = -np.sin(angle)
    tx = np.zeros((nx, 2 * HALF), np.float32)
    angle = 2.0 * np.pi * ((np.arange(nx)[:, None] * harmonics[None, :]) % nx) / nx
    scale = 1.0 / math.sqrt(nx * ny)
    tx[:, :count] = np.cos(angle) * scale
    tx[:, HALF : HALF + count] = -np.sin(angle) * scale
    tx = np.concatenate([tx[row::4] for _, row in split_rows(nx)])
    return ty, tx


def kernel(
    n, src_in, mat_in, ords_in, ty_in, tx_in, sol, res, pup,
    ords, ty, tx, in_sem, fx, gx, mx, w0, va, vb, d1, w1, f1, v1a, v1b, w2, f2, v2a, v2b, d2,
    pk1, pk2, raw, raw_mat, red, spec,
    fine_send, fine_recv, k1_send, k1_recv, k2_send, k2_recv,
    red_send, red_recv, spec_send, spec_recv,
):
    me = lax.axis_index("gz")
    own = mat_in.shape[0]
    depth = own
    half = own // 2
    mid1 = REACH1 * half
    sent = []

    def there(k):
        return me < n - k if k > 0 else me >= -k

    def other(k):
        return {"gz": lax.rem(me + k + n, n)}

    def start(source, target, ssem, rsem, k):
        copy = pltpu.make_async_remote_copy(
            src_ref=source, dst_ref=target, send_sem=ssem, recv_sem=rsem,
            device_id=other(k), device_id_type=pl.DeviceIdType.MESH,
        )
        message = Message(copy, there(k), there(-k))
        message.start()
        sent.append(message)
        return message

    barrier = pltpu.get_barrier_semaphore()

    def greet(k):
        pl.semaphore_signal(
            barrier, inc=1, device_id={"gz": lax.rem(me + k, n)},
            device_id_type=pl.DeviceIdType.MESH,
        )

    def clear(ref):
        ref[...] = jnp.zeros(ref.shape, ref.dtype)

    for d in range(1, REACH2 + 1):
        for k in (d, -d):

            @pl.when(jnp.logical_not(there(k)))
            def _():
                for which in range(3):
                    clear(pk2.at[which, REACH2 + k])
                    if d <= REACH1:
                        clear(pk1.at[which, REACH1 + k])
                if d == 1:
                    rim = pl.ds(depth + own if k > 0 else 0, depth)
                    clear(mx.at[rim])
                    clear(fx.at[:, rim])
                    clear(gx.at[:, rim])

    loop(1, n, greet)

    src = fx.at[:, pl.ds(depth, own)]
    mat = mx.at[pl.ds(depth, own)]
    fetches = [
        pltpu.make_async_copy(a, b, in_sem.at[k])
        for k, (a, b) in enumerate(
            ((mat_in, raw_mat), (src_in, raw), (ords_in, ords), (ty_in, ty), (tx_in, tx))
        )
    ]
    for fetch in fetches:
        fetch.start()
    quarter = mat_in.shape[1] // 4
    quarters = split_rows(mat_in.shape[1])
    fetches[0].wait()
    for p in range(own):
        for at, row in quarters:
            mat[p, at : at + quarter] = raw_mat[p, pl.ds(row, quarter, stride=4)]

    for p in range(half):
        a = pick(mat[2 * p], SHIFT_TABLE)
        b = pick(mat[2 * p + 1], SHIFT_TABLE)
        for k in range(2):
            d1[k, p] = 0.125 * pair_rows(pair_lanes(a[k] + b[k], 1))
        pk1[0, REACH1, p] = pack_two(d1[0, p], d1[1, p])
    for k in range(2):
        d2[k] = 0.125 * pair_rows(pair_lanes(d1[k, 0] + d1[k, 1], 2))
    pk2[0, REACH2] = pack_four(d2[0], d2[1])

    for fetch in fetches[1:]:
        fetch.wait()
    for p in range(own):
        for at, row in quarters:
            for k in range(2):
                src[k, p, at : at + quarter] = raw[k, p, pl.ds(row, quarter, stride=4)]
    pl.semaphore_wait(barrier, n - 1)

    def send_planes(source, base, target, slot, near, dims):
        up_from = half if near else 0
        up_to = half if near else 0
        down_from = 0 if near else half
        down_to = depth + own + (0 if near else half)
        copies = []
        for which, (k, a, b) in enumerate(((1, up_from, up_to), (-1, down_from, down_to))):
            s = pl.ds(base + a, half)
            t = pl.ds(b, half)
            one = source.at[:, s] if dims else source.at[s]
            two = target.at[:, t] if dims else target.at[t]
            copies.append(
                start(one, two, fine_send.at[slot + which], fine_recv.at[slot + which], k)
            )
        return copies

    def send_one(which, lo, hi):
        copies = {}
        for k in range(lo, hi + 1):
            for d in (k, -k):
                at = which * (2 * REACH1 + 1) + REACH1 - d
                part = pl.ds(0, half)
                if k == REACH1:
                    part = pl.ds(half - 1 if d > 0 else 0, 1)
                copies[-d] = start(
                    pk1.at[which, REACH1, part], pk1.at[which, REACH1 - d, part],
                    k1_send.at[at], k1_recv.at[at], d,
                )
        return copies

    def send_two(which):
        copies = {}
        for k in range(1, REACH2 + 1):
            for d in (k, -k):
                at = which * (2 * REACH2 + 1) + REACH2 - d
                copies[-d] = start(
                    pk2.at[which, REACH2], pk2.at[which, REACH2 - d],
                    k2_send.at[at], k2_recv.at[at], d,
                )
        return copies

    near_mat = send_planes(mx, depth, mx, 0, True, False)
    near_src = send_planes(fx, depth, fx, 2, True, True)
    shifts1 = send_one(0, 1, 1)
    shifts2 = {}

    def inside(plane, count):
        return jnp.where(jnp.logical_and(plane >= 0, plane < count), 1.0, 0.0).astype(F32)

    def weight0(p):
        m = inside(me * own + p - depth, n * own)
        r, i = pick(mx[p], WEIGHT_TABLE)
        return r * m, i * m

    def weight1(p):
        r, i = unpack_two(pk1[0, p // half, p % half])
        r, i = invert(r + 1.5, i)
        m = inside(me * half + p - mid1, n * half)
        return r * m, i * m

    def weight2(p):
        (rt, rb), (it, ib) = unpack_four(pk2[0, p])
        m = inside(me + p - REACH2, n)
        r, i = invert(jnp.concatenate([rt, rb]) + 0.375, jnp.concatenate([it, ib]))
        return r * m, i * m

    def take1(which):
        def body(p):
            return unpack_two(pk1[which, p // half, p % half])

        return body

    def take2(which):
        def body(p):
            (rt, rb), (it, ib) = unpack_four(pk2[which, p])
            return jnp.concatenate([rt, rb]), jnp.concatenate([it, ib])

        return body

    def cycle(which, f, near):
        begin, end = depth, depth + own
        if which == 1:
            planes(begin, end, FINE, w0, weight0)
        first_sweep(begin, end, FINE, va, f, w0)
        sweep(begin + 1, end - 1, FINE, vb, va, f, w0, 1, 1.0)
        if which == 1:
            for copy in near_mat:
                copy.wait_recv()
            planes(begin - 2, begin, FINE, w0, weight0)
            planes(end, end + 2, FINE, w0, weight0)
        for copy in near:
            copy.wait_recv()
        if which == 1:
            far_mat = send_planes(mx, depth, mx, 4, False, False)
        first_sweep(begin - 2, begin, FINE, va, f, w0)
        first_sweep(end, end + 2, FINE, va, f, w0)
        sweep(begin - 1, begin + 1, FINE, vb, va, f, w0, 1, 1.0)
        sweep(end - 1, end + 1, FINE, vb, va, f, w0, 1, 1.0)

        def down(q):
            total = [None, None]
            for s in range(2):
                p = depth + 2 * q + s
                c = pick(mx[p], DIAG_TABLE)
                dr, di = mul(c[0], c[1], vb[0, p], vb[1, p])
                for k, d in enumerate((dr, di)):
                    e = (f[k, p] - d) + around(vb, k, p, 1)
                    total[k] = e if s == 0 else total[k] + e
            parts = [
                0.125 * pair_rows(pair_lanes(t, 1)) for k, t in enumerate(total)
            ]
            f1[0, mid1 + q] = parts[0]
            f1[1, mid1 + q] = parts[1]
            pk1[which, REACH1, q] = pack_two(parts[0], parts[1])

        for q in range(half):
            down(q)
        ones = send_one(which, 1, 1)
        ones.update(send_one(which, 2, REACH1))
        if which == 1:
            shifts1.update(send_one(0, 2, REACH1))
            shifts2.update(send_two(0))

        if which == 1:
            for d in (-1, 1):
                shifts1[d].wait_recv()
            planes(mid1 - half, mid1 + 2 * half, MIDDLE, w1, weight1)

        for d in (-1, 1):
            ones[d].wait_recv()
        planes(mid1 - half, mid1, MIDDLE, f1, take1(which))
        planes(mid1 + half, mid1 + 2 * half, MIDDLE, f1, take1(which))
        first_sweep(mid1 - 2, mid1 + half + 2, MIDDLE, v1a, f1, w1)
        sweep(mid1 - 1, mid1 + half + 1, MIDDLE, v1b, v1a, f1, w1, 2, 0.25)

        parts = []
        total = [None, None]
        for q in range(half):
            p = mid1 + q
            dr, di = mul(d1[0, q] + 1.5, d1[1, q], v1b[0, p], v1b[1, p])
            for k, d in enumerate((dr, di)):
                e = (f1[k, p] - d) + 0.25 * around(v1b, k, p, 2)
                total[k] = e if q == 0 else total[k] + e
        parts = [0.125 * pair_rows(pair_lanes(t, 2)) for k, t in enumerate(total)]
        pk2[which, REACH2] = pack_four(parts[0], parts[1])
        twos = send_two(which)
        far = send_planes(f, depth, f, 4 + 2 * which, False, True)

        if which == 1:
            for d in range(2, REACH1 + 1):
                shifts1[d].wait_recv()
                shifts1[-d].wait_recv()
            planes(1, mid1 - half, MIDDLE, w1, weight1)
            planes(mid1 + 2 * half, 2 * mid1 + half - 1, MIDDLE, w1, weight1)
        for d in range(2, REACH1 + 1):
            ones[d].wait_recv()
            ones[-d].wait_recv()
        planes(1, mid1 - half, MIDDLE, f1, take1(which))
        planes(mid1 + 2 * half, 2 * mid1 + half - 1, MIDDLE, f1, take1(which))
        first_sweep(1, mid1 - 2, MIDDLE, v1a, f1, w1)
        first_sweep(mid1 + half + 2, 2 * mid1 + half - 1, MIDDLE, v1a, f1, w1)
        sweep(2, mid1 - 1, MIDDLE, v1b, v1a, f1, w1, 2, 0.25)
        sweep(mid1 + half + 1, 2 * mid1 + half - 2, MIDDLE, v1b, v1a, f1, w1, 2, 0.25)
        if which == 1:
            for d in range(1, REACH2 + 1):
                shifts2[d].wait_recv()
                shifts2[-d].wait_recv()
            planes(0, 2 * REACH2 + 1, COARSE, w2, weight2)

        for d in range(1, REACH2 + 1):
            twos[d].wait_recv()
            twos[-d].wait_recv()
        planes(0, 2 * REACH2 + 1, COARSE, f2, take2(which))
        first_sweep(0, 2 * REACH2 + 1, COARSE, v2a, f2, w2)
        sweep(1, 2 * REACH2, COARSE, v2b, v2a, f2, w2, 4, 0.0625)
        sweep(2, 2 * REACH2 - 1, COARSE, v2a, v2b, f2, w2, 4, 0.0625)
        sweep(3, 2 * REACH2 - 2, COARSE, v2b, v2a, f2, w2, 4, 0.0625)

        def raise1(c):
            p = (c - REACH2 + REACH1) * half
            for k in range(2):
                x = spread_rows(v2b[k, c])
                v1b[k, p] = v1b[k, p] + x
                v1b[k, p + 1] = v1b[k, p + 1] + x

        for c in range(REACH2 - 2, REACH2 + 3):
            raise1(c)
        sweep(mid1 - 3, mid1 + half + 3, MIDDLE, v1a, v1b, f1, w1, 2, 0.25)
        sweep(mid1 - 2, mid1 + half + 2, MIDDLE, v1b, v1a, f1, w1, 2, 0.25)

        if which == 1:
            for copy in far_mat:
                copy.wait_recv()
            planes(0, begin - 2, FINE, w0, weight0)
            planes(end + 2, end + depth, FINE, w0, weight0)
        for copy in far:
            copy.wait_recv()
        first_sweep(0, begin - 2, FINE, va, f, w0)
        first_sweep(end + 2, end + depth, FINE, va, f, w0)
        sweep(1, begin - 1, FINE, vb, va, f, w0, 1, 1.0)
        sweep(end + 1, end + depth - 1, FINE, vb, va, f, w0, 1, 1.0)

        def raise0(c):
            p = depth + 2 * (c - mid1)
            for k in range(2):
                x = spread_rows(v1b[k, c])
                vb[k, p] = vb[k, p] + x
                vb[k, p + 1] = vb[k, p + 1] + x

        for c in range(mid1 - 2, mid1 + half + 2):
            raise0(c)
        sweep(begin - 2, end + 2, FINE, va, vb, f, w0, 1, 1.0)
        sweep(begin - 1, end + 1, FINE, vb, va, f, w0, 1, 1.0)

    def image_of(p):
        c = pick(mx[p], IMAGE_TABLE)
        r, i = mul(c[0], c[1], vb[0, p], vb[1, p])
        return r - around(vb, 0, p, 1), i - around(vb, 1, p, 1)

    def fold(x):
        rows, lanes = x.shape
        return jnp.sum(x.reshape(rows // 8, 8, lanes), axis=0)

    def share(which, sums):
        rows = [jnp.sum(s, axis=0, keepdims=True) for s in sums]
        rows.append(jnp.zeros((8 - len(rows), rows[0].shape[1]), F32))
        red[which, me] = jnp.concatenate(rows, axis=0)

        def post(k):
            pltpu.make_async_remote_copy(
                src_ref=red.at[which, me], dst_ref=red.at[which, me],
                send_sem=red_send.at[which, k], recv_sem=red_recv.at[which, k],
                device_id={"gz": lax.rem(me + k, n)}, device_id_type=pl.DeviceIdType.MESH,
            ).start()

        loop(1, n, post)

    def collect(which):
        def await_one(k):
            one = pltpu.make_async_remote_copy(
                src_ref=red.at[which, me], dst_ref=red.at[which, lax.rem(me + n - k, n)],
                send_sem=red_send.at[which, k], recv_sem=red_recv.at[which, k],
                device_id={"gz": lax.rem(me + k, n)}, device_id_type=pl.DeviceIdType.MESH,
            )
            one.wait_recv()
            one.wait_send()

        loop(1, n, await_one)
        total = red[which, 0]
        for j in range(1, n):
            total = total + red[which, j]
        total = jnp.sum(total, axis=1, keepdims=True)
        return total[0:1], total[1:2], total[2:3]

    def spectrum(which):
        def post(k):
            pltpu.make_async_remote_copy(
                src_ref=spec.at[which], dst_ref=spec.at[which],
                send_sem=spec_send.at[which, k], recv_sem=spec_recv.at[which],
                device_id={"gz": lax.rem(me + k, n)}, device_id_type=pl.DeviceIdType.MESH,
            ).start()

        @pl.when(me == n - 1)
        def _():
            last = depth + own - 1
            spec[which] = spectrum_of(vb[0, last], vb[1, last], ty[...], tx[...])
            loop(1, n, post)

    def orders_of(which):
        def settle(k):
            pltpu.make_async_remote_copy(
                src_ref=spec.at[which], dst_ref=spec.at[which],
                send_sem=spec_send.at[which, k], recv_sem=spec_recv.at[which],
                device_id={"gz": lax.rem(me + k, n)}, device_id_type=pl.DeviceIdType.MESH,
            ).wait_send()

        @pl.when(me == n - 1)
        def _():
            loop(1, n, settle)

        @pl.when(me != n - 1)
        def _():
            pltpu.make_async_remote_copy(
                src_ref=spec.at[which], dst_ref=spec.at[which],
                send_sem=spec_send.at[which, 0], recv_sem=spec_recv.at[which],
                device_id={"gz": lax.rem(me + 1, n)}, device_id_type=pl.DeviceIdType.MESH,
            ).wait_recv()

        count = ords.shape[1]
        x = ords[0:1] + ORD_HALF
        y = ords[1:2] + ORD_HALF
        row = lax.broadcasted_iota(jnp.int32, (2 * HALF, count), 0)
        pick_y = lax.broadcasted_iota(jnp.int32, (HARM, count), 0) == y
        out = []
        for k in range(2):
            pick_x = jnp.where(row == x + k * HALF, 1.0, 0.0).astype(F32)
            chosen = precise(spec[which], pick_x, ((1,), (0,)))
            out.append(jnp.sum(jnp.where(pick_y, chosen, 0.0), axis=0, keepdims=True))
        return out

    cycle(1, fx, near_src)

    zero = jnp.zeros((8, fx.shape[3]), F32)
    sums = [zero, zero, zero]
    for p in range(own):
        r, i = image_of(depth + p)
        gx[0, depth + p] = r
        gx[1, depth + p] = i
        a, b = src[0, p], src[1, p]
        sums[0] = sums[0] + fold(a * a + b * b)
        sums[1] = sums[1] + fold(a * r + b * i)
        sums[2] = sums[2] + fold(a * i - b * r)
    near_img = send_planes(gx, depth, gx, 10, True, True)
    share(0, sums)

    def keep(p):
        sol[0, p] = vb[0, depth + p]
        sol[1, p] = vb[1, depth + p]

    loop(0, own, keep)
    spectrum(0)

    cycle(2, gx, near_img)

    rho, cr, ci = collect(0)
    scale = rho / (cr * cr + ci * ci)
    ar, ai = cr * scale, -(ci * scale)

    sums = [zero, zero, zero]
    for p in range(own):
        e = depth + p
        r, i = image_of(e)
        gr, gi = gx[0, e], gx[1, e]
        tr, ti = mul(ar, ai, gr, gi)
        hr, hi = src[0, p] - tr, src[1, p] - ti
        tr, ti = mul(ar, ai, r, i)
        lr, li = gr - tr, gi - ti
        va[0, e], va[1, e] = lr, li
        raw[0, p], raw[1, p] = hr, hi
        sums[0] = sums[0] + fold(lr * hr + li * hi)
        sums[1] = sums[1] + fold(lr * hi - li * hr)
        sums[2] = sums[2] + fold(lr * lr + li * li)
    share(1, sums)
    spectrum(1)
    sdr, sdi = orders_of(0)

    for copy in sent:
        copy.wait_send()

    along_r, along_i, norm = collect(1)
    wr, wi = along_r / norm, along_i / norm

    def finish(p):
        e = depth + p
        dr, di = sol[0, p], sol[1, p]
        tr, ti = mul(ar, ai, vb[0, e], vb[1, e])
        cr_, ci_ = mul(wr, wi, dr - tr, di - ti)
        xr, xi = mul(ar, ai, dr, di)
        solved = (xr + cr_, xi + ci_)
        tr, ti = mul(wr, wi, va[0, e], va[1, e])
        left = (raw[0, p] - tr, raw[1, p] - ti)
        for k in range(2):
            for at, row in quarters:
                sol[k, p, pl.ds(row, quarter, stride=4)] = solved[k][at : at + quarter]
                res[k, p, pl.ds(row, quarter, stride=4)] = left[k][at : at + quarter]

    for p in range(own):
        finish(p)

    sqr, sqi = orders_of(1)
    tr, ti = mul(ar, ai, sqr, sqi)
    cr_, ci_ = mul(wr, wi, sdr - tr, sdi - ti)
    xr, xi = mul(ar, ai, sdr, sdi)
    pup[0:1] = xr + cr_
    pup[1:2] = xi + ci_


def on_device(n, source_term, material, orders):
    own, nx, ny = material.shape
    half = own // 2
    ty, tx = tables(nx, ny)
    vm = pltpu.VMEM
    fine = vm((2, 3 * own, nx, ny), F32)
    planes1 = (2 * REACH1 + 1) * half
    one = vm((2, planes1, nx // 2, ny), F32)
    planes2 = 2 * REACH2 + 1
    two = vm((2, planes2, nx // 4, ny), F32)
    dma = pltpu.SemaphoreType.DMA
    ext1 = 3 * (2 * REACH1 + 1)
    ext2 = 3 * planes2
    whole = pl.BlockSpec(memory_space=pltpu.VMEM)
    return pl.pallas_call(
        functools.partial(kernel, n),
        out_shape=(
            jax.ShapeDtypeStruct(source_term.shape, F32),
            jax.ShapeDtypeStruct(source_term.shape, F32),
            jax.ShapeDtypeStruct(orders.shape, F32),
        ),
        in_specs=[pl.BlockSpec(memory_space=pl.ANY)] * 5,
        out_specs=(whole,) * 3,
        scratch_shapes=[
            vm(orders.shape, jnp.int32), vm(ty.shape, F32), vm(tx.shape, F32), dma((5,)),
            fine, fine, vm((3 * own, nx, ny), jnp.int32), fine, fine, fine,
            vm((2, half, nx // 2, ny), F32), one, one, one, one,
            two, two, two, two, vm((2, nx // 4, ny), F32),
            vm((3, 2 * REACH1 + 1, half, nx // 2, ny), F32),
            vm((3, planes2, nx // 8, ny), F32),
            vm((2, own, nx, ny), F32),
            vm((own, nx, ny), jnp.int32),
            vm((2, n, 8, ny), F32),
            vm((2, HARM, 2 * HALF), F32),
            dma((12,)), dma((12,)), dma((ext1,)), dma((ext1,)), dma((ext2,)), dma((ext2,)),
            dma((2, n)), dma((2, n)), dma((2, n)), dma((2,)),
        ],
        compiler_params=pltpu.CompilerParams(
            collective_id=0, has_side_effects=True, vmem_limit_bytes=62 * 1024 * 1024
        ),
    )(source_term, material, orders, jnp.asarray(ty), jnp.asarray(tx))


def solution(mesh):
    return jax.shard_map(
        functools.partial(on_device, mesh.shape["gz"]),
        mesh=mesh,
        in_specs=(
            P(None, ("clip", "gz"), None, None),
            P(("clip", "gz"), None, None),
            P(None, "gz"),
        ),
        out_specs=(
            P(None, ("clip", "gz"), None, None),
            P(None, ("clip", "gz"), None, None),
            P(None, ("clip", "gz")),
        ),
        check_vma=False,
    )
```

```python
import functools
import math

import jax
import jax.numpy as jnp
import numpy as np
from jax import lax
from jax.experimental import pallas as pl
from jax.experimental.pallas import tpu as pltpu
from jax.sharding import PartitionSpec as P

ORD_HALF = 22
HELM_TABLE = ((-0.5, 0.0), (1.0, -1.4), (-1.2, 0.0))
SHIFT_TABLE = ((-0.5, -0.25), (1.0, -0.25 * math.sqrt(11.84)), (-1.2, -0.6))
RELAX = 0.8
REACH1 = 3
REACH2 = 5
HALF = 64
HARM = 48
F32 = jnp.float32


def weight_of(shift):
    bottom = complex(6.0 + shift[0], shift[1])
    value = RELAX / bottom
    return (value.real, value.imag)


WEIGHT_TABLE = tuple(weight_of(entry) for entry in SHIFT_TABLE)
DIAG_TABLE = tuple((6.0 + entry[0], entry[1]) for entry in SHIFT_TABLE)
IMAGE_TABLE = tuple((6.0 + entry[0], entry[1]) for entry in HELM_TABLE)


def pick(material, table):
    one = material == 1
    two = material == 2
    return tuple(
        jnp.where(one, table[1][k], jnp.where(two, table[2][k], table[0][k])).astype(F32)
        for k in range(2)
    )


def mul(ar, ai, br, bi):
    return ar * br - ai * bi, ar * bi + ai * br


class Message:
    def __init__(self, copy, sends, receives):
        self.copy, self.sends, self.receives = copy, sends, receives

    def start(self):
        pl.when(self.sends)(lambda: self.copy.start())

    def wait_send(self):
        pl.when(self.sends)(lambda: self.copy.wait_send())

    def wait_recv(self):
        pl.when(self.receives)(lambda: self.copy.wait_recv())


def loop(lo, hi, body):
    def step(p, carry):
        body(p)
        return carry

    lax.fori_loop(lo, hi, step, 0)


def planes(lo, hi, group, dst, body):
    def some(first, count):
        values = [body(first + j) for j in range(count)]
        for j, (r, i) in enumerate(values):
            dst[0, first + j] = r
            dst[1, first + j] = i

    steps = (hi - lo) // group
    if steps == 1:
        some(lo, group)
    elif steps > 1:
        loop(0, steps, lambda t: some(lo + t * group, group))
    if (hi - lo) % group:
        some(lo + steps * group, (hi - lo) % group)


FINE, MIDDLE, COARSE = 2, 4, 6


def row_neighbours(x, lane_step):
    if lane_step == 4:
        return pltpu.roll(x, 1, 0) + pltpu.roll(x, x.shape[0] - 1, 0)
    if lane_step == 2:
        h = x.shape[0] // 2
        even, odd = x[:h], x[h:]
        return jnp.concatenate([odd + pltpu.roll(odd, 1, 0), even + pltpu.roll(even, h - 1, 0)])
    q = x.shape[0] // 4
    a, b, c, d = (x[j * q : (j + 1) * q] for j in range(4))
    return jnp.concatenate([c + pltpu.roll(d, 1, 0), c + d, a + b, b + pltpu.roll(a, q - 1, 0)])


def split_rows(rows):
    q = rows // 4
    return [((2 * c + b) * q, 2 * b + c) for c in range(2) for b in range(2)]


def around(ref, k, p, lane_step):
    x = ref[k, p]
    lanes = x.shape[1]
    total = ref[k, p - 1] + ref[k, p + 1]
    total = total + row_neighbours(x, lane_step)
    return total + (pltpu.roll(x, lane_step, 1) + pltpu.roll(x, lanes - lane_step, 1))


def first_sweep(lo, hi, group, dst, rhs, weight):
    planes(lo, hi, group, dst, lambda p: mul(weight[0, p], weight[1, p], rhs[0, p], rhs[1, p]))


def sweep(lo, hi, group, dst, old, rhs, weight, lane_step, h2):
    def body(p):
        nr = around(old, 0, p, lane_step)
        ni = around(old, 1, p, lane_step)
        if h2 != 1.0:
            nr, ni = nr * h2, ni * h2
        r, i = mul(weight[0, p], weight[1, p], rhs[0, p] + nr, rhs[1, p] + ni)
        return (1.0 - RELAX) * old[0, p] + r, (1.0 - RELAX) * old[1, p] + i

    planes(lo, hi, group, dst, body)


def lane_iota(shape):
    return lax.broadcasted_iota(jnp.int32, shape, 1)


def pair_lanes(x, step):
    lanes = x.shape[1]
    low = (lane_iota(x.shape) & step) == 0
    return x + jnp.where(low, pltpu.roll(x, lanes - step, 1), pltpu.roll(x, step, 1))


def pair_rows(x):
    h = x.shape[0] // 2
    return x[:h] + x[h:]


def spread_rows(x):
    return jnp.concatenate([x, x])


def pack_two(r, i):
    return jnp.where((lane_iota(r.shape) & 1) == 0, r, i)


def unpack_two(x):
    lanes = x.shape[1]
    even = (lane_iota(x.shape) & 1) == 0
    return jnp.where(even, x, pltpu.roll(x, 1, 1)), jnp.where(even, pltpu.roll(x, lanes - 1, 1), x)


def pack_four(r, i):
    rows = r.shape[0] // 2
    top = pack_two(r[:rows], i[:rows])
    low = pack_two(r[rows:], i[rows:])
    return jnp.where((lane_iota(top.shape) & 2) == 0, top, low)


def unpack_four(x):
    lanes = x.shape[1]
    first = (lane_iota(x.shape) & 2) == 0
    halves = []
    for y in unpack_two(x):
        halves.append(
            (jnp.where(first, y, pltpu.roll(y, 2, 1)), jnp.where(first, pltpu.roll(y, lanes - 2, 1), y))
        )
    return halves


def invert(r, i):
    bottom = 1.0 / (r * r + i * i)
    return RELAX * r * bottom, -RELAX * i * bottom


def precise(a, b, dims):
    return lax.dot_general(
        a, b, (dims, ((), ())), precision=lax.Precision.HIGHEST, preferred_element_type=F32
    )


def spectrum_of(r, i, ty, tx):
    gr = precise(ty, r, ((1,), (1,)))
    gi = precise(ty, i, ((1,), (1,)))
    inner = jnp.concatenate([gr[:HALF] - gi[HALF:], gr[HALF:] + gi[:HALF]], axis=0)
    outer = precise(inner, tx, ((1,), (0,)))
    turned = pltpu.roll(outer[HALF:], HALF, 1)
    left = lane_iota(turned.shape) < HALF
    return (outer[:HALF] + jnp.where(left, -turned, turned))[:HARM]


def tables(nx, ny):
    harmonics = np.arange(2 * ORD_HALF + 1) - ORD_HALF
    count = harmonics.size
    ty = np.zeros((2 * HALF, ny), np.float32)
    angle = 2.0 * np.pi * ((harmonics[:, None] * np.arange(ny)[None, :]) % ny) / ny
    ty[:count] = np.cos(angle)
    ty[HALF : HALF + count] = -np.sin(angle)
    tx = np.zeros((nx, 2 * HALF), np.float32)
    angle = 2.0 * np.pi * ((np.arange(nx)[:, None] * harmonics[None, :]) % nx) / nx
    scale = 1.0 / math.sqrt(nx * ny)
    tx[:, :count] = np.cos(angle) * scale
    tx[:, HALF : HALF + count] = -np.sin(angle) * scale
    tx = np.concatenate([tx[row::4] for _, row in split_rows(nx)])
    return ty, tx


def kernel(
    n, src_in, mat_in, ords_in, ty_in, tx_in, sol, res, pup,
    ords, ty, tx, in_sem, fx, gx, mx, w0, va, vb, d1, w1, f1, v1a, v1b, w2, f2, v2a, v2b, d2,
    pk1, pk2, raw, raw_mat, red, spec,
    fine_send, fine_recv, k1_send, k1_recv, k2_send, k2_recv,
    red_send, red_recv, spec_send, spec_recv,
):
    me = lax.axis_index("gz")
    own = mat_in.shape[0]
    depth = own
    half = own // 2
    mid1 = REACH1 * half
    sent = []

    def there(k):
        return me < n - k if k > 0 else me >= -k

    def other(k):
        return {"gz": lax.rem(me + k + n, n)}

    def start(source, target, ssem, rsem, k):
        copy = pltpu.make_async_remote_copy(
            src_ref=source, dst_ref=target, send_sem=ssem, recv_sem=rsem,
            device_id=other(k), device_id_type=pl.DeviceIdType.MESH,
        )
        message = Message(copy, there(k), there(-k))
        message.start()
        sent.append(message)
        return message

    barrier = pltpu.get_barrier_semaphore()

    def greet(k):
        pl.semaphore_signal(
            barrier, inc=1, device_id={"gz": lax.rem(me + k, n)},
            device_id_type=pl.DeviceIdType.MESH,
        )

    def clear(ref):
        ref[...] = jnp.zeros(ref.shape, ref.dtype)

    for d in range(1, REACH2 + 1):
        for k in (d, -d):

            @pl.when(jnp.logical_not(there(k)))
            def _():
                for which in range(3):
                    clear(pk2.at[which, REACH2 + k])
                    if d <= REACH1:
                        clear(pk1.at[which, REACH1 + k])
                if d == 1:
                    rim = pl.ds(depth + own if k > 0 else 0, depth)
                    clear(mx.at[rim])
                    clear(fx.at[:, rim])
                    clear(gx.at[:, rim])

    loop(1, n, greet)

    src = fx.at[:, pl.ds(depth, own)]
    mat = mx.at[pl.ds(depth, own)]
    fetches = [
        pltpu.make_async_copy(a, b, in_sem.at[k])
        for k, (a, b) in enumerate(
            ((mat_in, raw_mat), (src_in, raw), (ords_in, ords), (ty_in, ty), (tx_in, tx))
        )
    ]
    for fetch in fetches:
        fetch.start()
    quarter = mat_in.shape[1] // 4
    quarters = split_rows(mat_in.shape[1])
    fetches[0].wait()
    for p in range(own):
        for at, row in quarters:
            mat[p, at : at + quarter] = raw_mat[p, pl.ds(row, quarter, stride=4)]

    for p in range(half):
        a = pick(mat[2 * p], SHIFT_TABLE)
        b = pick(mat[2 * p + 1], SHIFT_TABLE)
        for k in range(2):
            d1[k, p] = 0.125 * pair_rows(pair_lanes(a[k] + b[k], 1))
        pk1[0, REACH1, p] = pack_two(d1[0, p], d1[1, p])
    for k in range(2):
        d2[k] = 0.125 * pair_rows(pair_lanes(d1[k, 0] + d1[k, 1], 2))
    pk2[0, REACH2] = pack_four(d2[0], d2[1])

    for fetch in fetches[1:]:
        fetch.wait()
    for p in range(own):
        for at, row in quarters:
            for k in range(2):
                src[k, p, at : at + quarter] = raw[k, p, pl.ds(row, quarter, stride=4)]
    pl.semaphore_wait(barrier, n - 1)

    def send_planes(source, base, target, slot, near, dims, sides=(0, 1)):
        up_from = half if near else 0
        up_to = half if near else 0
        down_from = 0 if near else half
        down_to = depth + own + (0 if near else half)
        copies = []
        for which, (k, a, b) in enumerate(((1, up_from, up_to), (-1, down_from, down_to))):
            if which not in sides:
                continue
            s = pl.ds(base + a, half)
            t = pl.ds(b, half)
            one = source.at[:, s] if dims else source.at[s]
            two = target.at[:, t] if dims else target.at[t]
            copies.append(
                start(one, two, fine_send.at[slot + which], fine_recv.at[slot + which], k)
            )
        return copies

    def send_one(which, lo, hi):
        copies = {}
        for k in range(lo, hi + 1):
            for d in (k, -k):
                at = which * (2 * REACH1 + 1) + REACH1 - d
                part = pl.ds(0, half)
                if k == REACH1:
                    part = pl.ds(half - 1 if d > 0 else 0, 1)
                copies[-d] = start(
                    pk1.at[which, REACH1, part], pk1.at[which, REACH1 - d, part],
                    k1_send.at[at], k1_recv.at[at], d,
                )
        return copies

    def send_two(which):
        copies = {}
        for k in range(1, REACH2 + 1):
            for d in (k, -k):
                at = which * (2 * REACH2 + 1) + REACH2 - d
                copies[-d] = start(
                    pk2.at[which, REACH2], pk2.at[which, REACH2 - d],
                    k2_send.at[at], k2_recv.at[at], d,
                )
        return copies

    near_mat = send_planes(mx, depth, mx, 0, True, False)
    near_src = send_planes(fx, depth, fx, 2, True, True)
    shifts1 = send_one(0, 1, 1)
    shifts2 = {}

    def inside(plane, count):
        return jnp.where(jnp.logical_and(plane >= 0, plane < count), 1.0, 0.0).astype(F32)

    def weight0(p):
        m = inside(me * own + p - depth, n * own)
        r, i = pick(mx[p], WEIGHT_TABLE)
        return r * m, i * m

    def weight1(p):
        r, i = unpack_two(pk1[0, p // half, p % half])
        r, i = invert(r + 1.5, i)
        m = inside(me * half + p - mid1, n * half)
        return r * m, i * m

    def weight2(p):
        (rt, rb), (it, ib) = unpack_four(pk2[0, p])
        m = inside(me + p - REACH2, n)
        r, i = invert(jnp.concatenate([rt, rb]) + 0.375, jnp.concatenate([it, ib]))
        return r * m, i * m

    def take1(which):
        def body(p):
            return unpack_two(pk1[which, p // half, p % half])

        return body

    def take2(which):
        def body(p):
            (rt, rb), (it, ib) = unpack_four(pk2[which, p])
            return jnp.concatenate([rt, rb]), jnp.concatenate([it, ib])

        return body

    def cycle(which, f, near):
        begin, end = depth, depth + own
        if which == 1:
            planes(begin, end, FINE, w0, weight0)
        first_sweep(begin, end, FINE, va, f, w0)
        sweep(begin + 1, end - 1, FINE, vb, va, f, w0, 1, 1.0)
        if which == 1:
            for copy in near_mat:
                copy.wait_recv()
            planes(begin - 2, begin, FINE, w0, weight0)
            planes(end, end + 2, FINE, w0, weight0)
        for copy in near:
            copy.wait_recv()
        first_sweep(begin - 2, begin, FINE, va, f, w0)
        first_sweep(end, end + 2, FINE, va, f, w0)
        sweep(begin - 1, begin + 1, FINE, vb, va, f, w0, 1, 1.0)
        sweep(end - 1, end + 1, FINE, vb, va, f, w0, 1, 1.0)

        def down(q):
            total = [None, None]
            for s in range(2):
                p = depth + 2 * q + s
                c = pick(mx[p], DIAG_TABLE)
                dr, di = mul(c[0], c[1], vb[0, p], vb[1, p])
                for k, d in enumerate((dr, di)):
                    e = (f[k, p] - d) + around(vb, k, p, 1)
                    total[k] = e if s == 0 else total[k] + e
            parts = [
                0.125 * pair_rows(pair_lanes(t, 1)) for k, t in enumerate(total)
            ]
            f1[0, mid1 + q] = parts[0]
            f1[1, mid1 + q] = parts[1]
            pk1[which, REACH1, q] = pack_two(parts[0], parts[1])

        for q in range(half):
            down(q)
        ones = send_one(which, 1, 1)
        ones.update(send_one(which, 2, REACH1))
        if which == 1:
            shifts1.update(send_one(0, 2, REACH1))
            shifts2.update(send_two(0))

        if which == 1:
            for d in (-1, 1):
                shifts1[d].wait_recv()
            planes(mid1 - half, mid1 + 2 * half, MIDDLE, w1, weight1)

        for d in (-1, 1):
            ones[d].wait_recv()
        planes(mid1 - half, mid1, MIDDLE, f1, take1(which))
        planes(mid1 + half, mid1 + 2 * half, MIDDLE, f1, take1(which))
        first_sweep(mid1 - 2, mid1 + half + 2, MIDDLE, v1a, f1, w1)
        sweep(mid1 - 1, mid1 + half + 1, MIDDLE, v1b, v1a, f1, w1, 2, 0.25)

        parts = []
        total = [None, None]
        for q in range(half):
            p = mid1 + q
            dr, di = mul(d1[0, q] + 1.5, d1[1, q], v1b[0, p], v1b[1, p])
            for k, d in enumerate((dr, di)):
                e = (f1[k, p] - d) + 0.25 * around(v1b, k, p, 2)
                total[k] = e if q == 0 else total[k] + e
        parts = [0.125 * pair_rows(pair_lanes(t, 2)) for k, t in enumerate(total)]
        pk2[which, REACH2] = pack_four(parts[0], parts[1])
        twos = send_two(which)
        if which == 1:
            far_mat = send_planes(mx, depth, mx, 4, False, False)
        far = send_planes(f, depth, f, 4 + 2 * which, False, True)

        if which == 1:
            for d in range(2, REACH1 + 1):
                shifts1[d].wait_recv()
                shifts1[-d].wait_recv()
            planes(1, mid1 - half, MIDDLE, w1, weight1)
            planes(mid1 + 2 * half, 2 * mid1 + half - 1, MIDDLE, w1, weight1)
        for d in range(2, REACH1 + 1):
            ones[d].wait_recv()
            ones[-d].wait_recv()
        planes(1, mid1 - half, MIDDLE, f1, take1(which))
        planes(mid1 + 2 * half, 2 * mid1 + half - 1, MIDDLE, f1, take1(which))
        first_sweep(1, mid1 - 2, MIDDLE, v1a, f1, w1)
        first_sweep(mid1 + half + 2, 2 * mid1 + half - 1, MIDDLE, v1a, f1, w1)
        sweep(2, mid1 - 1, MIDDLE, v1b, v1a, f1, w1, 2, 0.25)
        sweep(mid1 + half + 1, 2 * mid1 + half - 2, MIDDLE, v1b, v1a, f1, w1, 2, 0.25)
        if which == 1:
            for d in range(1, REACH2 + 1):
                shifts2[d].wait_recv()
                shifts2[-d].wait_recv()
            planes(0, 2 * REACH2 + 1, COARSE, w2, weight2)

        for d in range(1, REACH2 + 1):
            twos[d].wait_recv()
            twos[-d].wait_recv()
        planes(0, 2 * REACH2 + 1, COARSE, f2, take2(which))
        first_sweep(0, 2 * REACH2 + 1, COARSE, v2a, f2, w2)
        sweep(1, 2 * REACH2, COARSE, v2b, v2a, f2, w2, 4, 0.0625)
        sweep(2, 2 * REACH2 - 1, COARSE, v2a, v2b, f2, w2, 4, 0.0625)
        sweep(3, 2 * REACH2 - 2, COARSE, v2b, v2a, f2, w2, 4, 0.0625)

        def raise1(c):
            p = (c - REACH2 + REACH1) * half
            for k in range(2):
                x = spread_rows(v2b[k, c])
                v1b[k, p] = v1b[k, p] + x
                v1b[k, p + 1] = v1b[k, p + 1] + x

        for c in range(REACH2 - 2, REACH2 + 3):
            raise1(c)
        sweep(mid1 - 3, mid1 + half + 3, MIDDLE, v1a, v1b, f1, w1, 2, 0.25)
        sweep(mid1 - 2, mid1 + half + 2, MIDDLE, v1b, v1a, f1, w1, 2, 0.25)

        if which == 1:
            for copy in far_mat:
                copy.wait_recv()
            planes(0, begin - 2, FINE, w0, weight0)
            planes(end + 2, end + depth, FINE, w0, weight0)
        for copy in far:
            copy.wait_recv()
        first_sweep(0, begin - 2, FINE, va, f, w0)
        first_sweep(end + 2, end + depth, FINE, va, f, w0)
        sweep(1, begin - 1, FINE, vb, va, f, w0, 1, 1.0)
        sweep(end + 1, end + depth - 1, FINE, vb, va, f, w0, 1, 1.0)

        def raise0(c):
            p = depth + 2 * (c - mid1)
            for k in range(2):
                x = spread_rows(v1b[k, c])
                vb[k, p] = vb[k, p] + x
                vb[k, p + 1] = vb[k, p + 1] + x

        for c in range(mid1 - 2, mid1 + half + 2):
            raise0(c)
        sweep(begin - 2, end + 2, FINE, va, vb, f, w0, 1, 1.0)
        sweep(begin - 1, end + 1, FINE, vb, va, f, w0, 1, 1.0)

    def image_of(p):
        c = pick(mx[p], IMAGE_TABLE)
        r, i = mul(c[0], c[1], vb[0, p], vb[1, p])
        return r - around(vb, 0, p, 1), i - around(vb, 1, p, 1)

    def fold(x):
        rows, lanes = x.shape
        return jnp.sum(x.reshape(rows // 8, 8, lanes), axis=0)

    def share(which, sums):
        rows = [jnp.sum(s, axis=0, keepdims=True) for s in sums]
        rows.append(jnp.zeros((4 - len(rows), rows[0].shape[1]), F32))
        red[which, me] = jnp.concatenate(rows, axis=0)

        def post(k):
            pltpu.make_async_remote_copy(
                src_ref=red.at[which, me], dst_ref=red.at[which, me],
                send_sem=red_send.at[which, k], recv_sem=red_recv.at[which, k],
                device_id={"gz": lax.rem(me + k, n)}, device_id_type=pl.DeviceIdType.MESH,
            ).start()

        loop(1, n, post)

    def collect(which):
        def await_one(k):
            one = pltpu.make_async_remote_copy(
                src_ref=red.at[which, me], dst_ref=red.at[which, lax.rem(me + n - k, n)],
                send_sem=red_send.at[which, k], recv_sem=red_recv.at[which, k],
                device_id={"gz": lax.rem(me + k, n)}, device_id_type=pl.DeviceIdType.MESH,
            )
            one.wait_recv()
            one.wait_send()

        loop(1, n, await_one)
        total = red[which, 0]
        for j in range(1, n):
            total = total + red[which, j]
        total = jnp.sum(total, axis=1, keepdims=True)
        return total[0:1], total[1:2], total[2:3]

    def spectrum(which):
        def post(k):
            pltpu.make_async_remote_copy(
                src_ref=spec.at[which], dst_ref=spec.at[which],
                send_sem=spec_send.at[which, k], recv_sem=spec_recv.at[which],
                device_id={"gz": lax.rem(me + k, n)}, device_id_type=pl.DeviceIdType.MESH,
            ).start()

        @pl.when(me == n - 1)
        def _():
            last = depth + own - 1
            spec[which] = spectrum_of(vb[0, last], vb[1, last], ty[...], tx[...])
            loop(1, n, post)

    def orders_of(which):
        def settle(k):
            pltpu.make_async_remote_copy(
                src_ref=spec.at[which], dst_ref=spec.at[which],
                send_sem=spec_send.at[which, k], recv_sem=spec_recv.at[which],
                device_id={"gz": lax.rem(me + k, n)}, device_id_type=pl.DeviceIdType.MESH,
            ).wait_send()

        @pl.when(me == n - 1)
        def _():
            loop(1, n, settle)

        @pl.when(me != n - 1)
        def _():
            pltpu.make_async_remote_copy(
                src_ref=spec.at[which], dst_ref=spec.at[which],
                send_sem=spec_send.at[which, 0], recv_sem=spec_recv.at[which],
                device_id={"gz": lax.rem(me + 1, n)}, device_id_type=pl.DeviceIdType.MESH,
            ).wait_recv()

        count = ords.shape[1]
        x = ords[0:1] + ORD_HALF
        y = ords[1:2] + ORD_HALF
        row = lax.broadcasted_iota(jnp.int32, (2 * HALF, count), 0)
        pick_y = lax.broadcasted_iota(jnp.int32, (HARM, count), 0) == y
        out = []
        for k in range(2):
            pick_x = jnp.where(row == x + k * HALF, 1.0, 0.0).astype(F32)
            chosen = precise(spec[which], pick_x, ((1,), (0,)))
            out.append(jnp.sum(jnp.where(pick_y, chosen, 0.0), axis=0, keepdims=True))
        return out

    cycle(1, fx, near_src)

    zero = jnp.zeros((8, fx.shape[3]), F32)
    sums = [zero, zero, zero]
    for p in range(own):
        r, i = image_of(depth + p)
        gx[0, depth + p] = r
        gx[1, depth + p] = i
        a, b = src[0, p], src[1, p]
        sums[0] = sums[0] + fold(a * a + b * b)
        sums[1] = sums[1] + fold(a * r + b * i)
        sums[2] = sums[2] + fold(a * i - b * r)
        if p == half - 1:
            near_img = send_planes(gx, depth, gx, 10, True, True, (1,))
    near_img += send_planes(gx, depth, gx, 10, True, True, (0,))
    share(0, sums)

    def keep(p):
        sol[0, p] = vb[0, depth + p]
        sol[1, p] = vb[1, depth + p]

    loop(0, own, keep)
    spectrum(0)

    cycle(2, gx, near_img)

    rho, cr, ci = collect(0)
    scale = rho / (cr * cr + ci * ci)
    ar, ai = cr * scale, -(ci * scale)

    sums = [zero, zero, zero]
    for p in range(own):
        e = depth + p
        r, i = image_of(e)
        gr, gi = gx[0, e], gx[1, e]
        tr, ti = mul(ar, ai, gr, gi)
        hr, hi = src[0, p] - tr, src[1, p] - ti
        tr, ti = mul(ar, ai, r, i)
        lr, li = gr - tr, gi - ti
        va[0, e], va[1, e] = lr, li
        raw[0, p], raw[1, p] = hr, hi
        sums[0] = sums[0] + fold(lr * hr + li * hi)
        sums[1] = sums[1] + fold(lr * hi - li * hr)
        sums[2] = sums[2] + fold(lr * lr + li * li)
    share(1, sums)
    spectrum(1)
    sdr, sdi = orders_of(0)

    for copy in sent:
        copy.wait_send()

    along_r, along_i, norm = collect(1)
    wr, wi = along_r / norm, along_i / norm

    def finish(p):
        e = depth + p
        dr, di = sol[0, p], sol[1, p]
        tr, ti = mul(ar, ai, vb[0, e], vb[1, e])
        cr_, ci_ = mul(wr, wi, dr - tr, di - ti)
        xr, xi = mul(ar, ai, dr, di)
        solved = (xr + cr_, xi + ci_)
        tr, ti = mul(wr, wi, va[0, e], va[1, e])
        left = (raw[0, p] - tr, raw[1, p] - ti)
        for k in range(2):
            for at, row in quarters:
                sol[k, p, pl.ds(row, quarter, stride=4)] = solved[k][at : at + quarter]
                res[k, p, pl.ds(row, quarter, stride=4)] = left[k][at : at + quarter]

    for p in range(own):
        finish(p)

    sqr, sqi = orders_of(1)
    tr, ti = mul(ar, ai, sqr, sqi)
    cr_, ci_ = mul(wr, wi, sdr - tr, sdi - ti)
    xr, xi = mul(ar, ai, sdr, sdi)
    pup[0:1] = xr + cr_
    pup[1:2] = xi + ci_


def on_device(n, source_term, material, orders):
    own, nx, ny = material.shape
    half = own // 2
    ty, tx = tables(nx, ny)
    vm = pltpu.VMEM
    fine = vm((2, 3 * own, nx, ny), F32)
    planes1 = (2 * REACH1 + 1) * half
    one = vm((2, planes1, nx // 2, ny), F32)
    planes2 = 2 * REACH2 + 1
    two = vm((2, planes2, nx // 4, ny), F32)
    dma = pltpu.SemaphoreType.DMA
    ext1 = 3 * (2 * REACH1 + 1)
    ext2 = 3 * planes2
    whole = pl.BlockSpec(memory_space=pltpu.VMEM)
    return pl.pallas_call(
        functools.partial(kernel, n),
        out_shape=(
            jax.ShapeDtypeStruct(source_term.shape, F32),
            jax.ShapeDtypeStruct(source_term.shape, F32),
            jax.ShapeDtypeStruct(orders.shape, F32),
        ),
        in_specs=[pl.BlockSpec(memory_space=pl.ANY)] * 5,
        out_specs=(whole,) * 3,
        scratch_shapes=[
            vm(orders.shape, jnp.int32), vm(ty.shape, F32), vm(tx.shape, F32), dma((5,)),
            fine, fine, vm((3 * own, nx, ny), jnp.int32), fine, fine, fine,
            vm((2, half, nx // 2, ny), F32), one, one, one, one,
            two, two, two, two, vm((2, nx // 4, ny), F32),
            vm((3, 2 * REACH1 + 1, half, nx // 2, ny), F32),
            vm((3, planes2, nx // 8, ny), F32),
            vm((2, own, nx, ny), F32),
            vm((own, nx, ny), jnp.int32),
            vm((2, n, 4, ny), F32),
            vm((2, HARM, 2 * HALF), F32),
            dma((12,)), dma((12,)), dma((ext1,)), dma((ext1,)), dma((ext2,)), dma((ext2,)),
            dma((2, n)), dma((2, n)), dma((2, n)), dma((2,)),
        ],
        compiler_params=pltpu.CompilerParams(
            collective_id=0, has_side_effects=True, vmem_limit_bytes=62 * 1024 * 1024
        ),
    )(source_term, material, orders, jnp.asarray(ty), jnp.asarray(tx))


def solution(mesh):
    return jax.shard_map(
        functools.partial(on_device, mesh.shape["gz"]),
        mesh=mesh,
        in_specs=(
            P(None, ("clip", "gz"), None, None),
            P(("clip", "gz"), None, None),
            P(None, "gz"),
        ),
        out_specs=(
            P(None, ("clip", "gz"), None, None),
            P(None, ("clip", "gz"), None, None),
            P(None, ("clip", "gz")),
        ),
        check_vma=False,
    )
```

```python
import functools
import math

import jax
import jax.numpy as jnp
import numpy as np
from jax import lax
from jax.experimental import pallas as pl
from jax.experimental.pallas import tpu as pltpu
from jax.sharding import PartitionSpec as P

ORD_HALF = 22
HELM_TABLE = ((-0.5, 0.0), (1.0, -1.4), (-1.2, 0.0))
SHIFT_TABLE = ((-0.5, -0.25), (1.0, -0.25 * math.sqrt(11.84)), (-1.2, -0.6))
RELAX = 0.8
REACH1 = 3
REACH2 = 5
HALF = 64
HARM = 48
F32 = jnp.float32


def weight_of(shift):
    bottom = complex(6.0 + shift[0], shift[1])
    value = RELAX / bottom
    return (value.real, value.imag)


WEIGHT_TABLE = tuple(weight_of(entry) for entry in SHIFT_TABLE)
DIAG_TABLE = tuple((6.0 + entry[0], entry[1]) for entry in SHIFT_TABLE)
IMAGE_TABLE = tuple((6.0 + entry[0], entry[1]) for entry in HELM_TABLE)


def pick(material, table):
    one = material == 1
    two = material == 2
    return tuple(
        jnp.where(one, table[1][k], jnp.where(two, table[2][k], table[0][k])).astype(F32)
        for k in range(2)
    )


def mul(ar, ai, br, bi):
    return ar * br - ai * bi, ar * bi + ai * br


class Message:
    def __init__(self, copy, sends, receives):
        self.copy, self.sends, self.receives = copy, sends, receives

    def start(self):
        pl.when(self.sends)(lambda: self.copy.start())

    def wait_send(self):
        pl.when(self.sends)(lambda: self.copy.wait_send())

    def wait_recv(self):
        pl.when(self.receives)(lambda: self.copy.wait_recv())


def loop(lo, hi, body):
    def step(p, carry):
        body(p)
        return carry

    lax.fori_loop(lo, hi, step, 0)


def planes(lo, hi, group, dst, body):
    def some(first, count):
        values = [body(first + j) for j in range(count)]
        for j, (r, i) in enumerate(values):
            dst[0, first + j] = r
            dst[1, first + j] = i

    steps = (hi - lo) // group
    if steps == 1:
        some(lo, group)
    elif steps > 1:
        loop(0, steps, lambda t: some(lo + t * group, group))
    if (hi - lo) % group:
        some(lo + steps * group, (hi - lo) % group)


FINE, MIDDLE, COARSE = 2, 4, 6


def row_neighbours(x, lane_step):
    if lane_step == 4:
        return pltpu.roll(x, 1, 0) + pltpu.roll(x, x.shape[0] - 1, 0)
    if lane_step == 2:
        h = x.shape[0] // 2
        even, odd = x[:h], x[h:]
        return jnp.concatenate([odd + pltpu.roll(odd, 1, 0), even + pltpu.roll(even, h - 1, 0)])
    q = x.shape[0] // 4
    a, b, c, d = (x[j * q : (j + 1) * q] for j in range(4))
    return jnp.concatenate([c + pltpu.roll(d, 1, 0), c + d, a + b, b + pltpu.roll(a, q - 1, 0)])


def split_rows(rows):
    q = rows // 4
    return [((2 * c + b) * q, 2 * b + c) for c in range(2) for b in range(2)]


def around(ref, k, p, lane_step):
    x = ref[k, p]
    lanes = x.shape[1]
    total = ref[k, p - 1] + ref[k, p + 1]
    total = total + row_neighbours(x, lane_step)
    return total + (pltpu.roll(x, lane_step, 1) + pltpu.roll(x, lanes - lane_step, 1))


def first_sweep(lo, hi, group, dst, rhs, weight):
    planes(lo, hi, group, dst, lambda p: mul(weight[0, p], weight[1, p], rhs[0, p], rhs[1, p]))


def sweep(lo, hi, group, dst, old, rhs, weight, lane_step, h2):
    def body(p):
        nr = around(old, 0, p, lane_step)
        ni = around(old, 1, p, lane_step)
        if h2 != 1.0:
            nr, ni = nr * h2, ni * h2
        r, i = mul(weight[0, p], weight[1, p], rhs[0, p] + nr, rhs[1, p] + ni)
        return (1.0 - RELAX) * old[0, p] + r, (1.0 - RELAX) * old[1, p] + i

    planes(lo, hi, group, dst, body)


def lane_iota(shape):
    return lax.broadcasted_iota(jnp.int32, shape, 1)


def pair_lanes(x, step):
    lanes = x.shape[1]
    low = (lane_iota(x.shape) & step) == 0
    return x + jnp.where(low, pltpu.roll(x, lanes - step, 1), pltpu.roll(x, step, 1))


def pair_rows(x):
    h = x.shape[0] // 2
    return x[:h] + x[h:]


def spread_rows(x):
    return jnp.concatenate([x, x])


def pack_two(r, i):
    return jnp.where((lane_iota(r.shape) & 1) == 0, r, i)


def unpack_two(x):
    lanes = x.shape[1]
    even = (lane_iota(x.shape) & 1) == 0
    return jnp.where(even, x, pltpu.roll(x, 1, 1)), jnp.where(even, pltpu.roll(x, lanes - 1, 1), x)


def pack_four(r, i):
    rows = r.shape[0] // 2
    top = pack_two(r[:rows], i[:rows])
    low = pack_two(r[rows:], i[rows:])
    return jnp.where((lane_iota(top.shape) & 2) == 0, top, low)


def unpack_four(x):
    lanes = x.shape[1]
    first = (lane_iota(x.shape) & 2) == 0
    halves = []
    for y in unpack_two(x):
        halves.append(
            (jnp.where(first, y, pltpu.roll(y, 2, 1)), jnp.where(first, pltpu.roll(y, lanes - 2, 1), y))
        )
    return halves


def invert(r, i):
    bottom = 1.0 / (r * r + i * i)
    return RELAX * r * bottom, -RELAX * i * bottom


def precise(a, b, dims):
    return lax.dot_general(
        a, b, (dims, ((), ())), precision=lax.Precision.HIGHEST, preferred_element_type=F32
    )


def spectrum_of(r, i, ty, tx):
    gr = precise(ty, r, ((1,), (1,)))
    gi = precise(ty, i, ((1,), (1,)))
    inner = jnp.concatenate([gr[:HALF] - gi[HALF:], gr[HALF:] + gi[:HALF]], axis=0)
    outer = precise(inner, tx, ((1,), (0,)))
    turned = pltpu.roll(outer[HALF:], HALF, 1)
    left = lane_iota(turned.shape) < HALF
    return (outer[:HALF] + jnp.where(left, -turned, turned))[:HARM]


def tables(nx, ny):
    harmonics = np.arange(2 * ORD_HALF + 1) - ORD_HALF
    count = harmonics.size
    ty = np.zeros((2 * HALF, ny), np.float32)
    angle = 2.0 * np.pi * ((harmonics[:, None] * np.arange(ny)[None, :]) % ny) / ny
    ty[:count] = np.cos(angle)
    ty[HALF : HALF + count] = -np.sin(angle)
    tx = np.zeros((nx, 2 * HALF), np.float32)
    angle = 2.0 * np.pi * ((np.arange(nx)[:, None] * harmonics[None, :]) % nx) / nx
    scale = 1.0 / math.sqrt(nx * ny)
    tx[:, :count] = np.cos(angle) * scale
    tx[:, HALF : HALF + count] = -np.sin(angle) * scale
    tx = np.concatenate([tx[row::4] for _, row in split_rows(nx)])
    return ty, tx


def kernel(
    n, src_in, mat_in, ords_in, ty_in, tx_in, sol, res, pup,
    ords, ty, tx, in_sem, fx, gx, mx, w0, va, vb, d1, w1, f1, v1a, v1b, w2, f2, v2a, v2b, d2,
    pk1, pk2, raw, raw_mat, red, spec,
    fine_send, fine_recv, k1_send, k1_recv, k2_send, k2_recv,
    red_send, red_recv, spec_send, spec_recv,
):
    me = lax.axis_index("gz")
    own = mat_in.shape[0]
    depth = own
    half = own // 2
    mid1 = REACH1 * half
    sent = []

    def there(k):
        return me < n - k if k > 0 else me >= -k

    def other(k):
        return {"gz": lax.rem(me + k + n, n)}

    def start(source, target, ssem, rsem, k):
        copy = pltpu.make_async_remote_copy(
            src_ref=source, dst_ref=target, send_sem=ssem, recv_sem=rsem,
            device_id=other(k), device_id_type=pl.DeviceIdType.MESH,
        )
        message = Message(copy, there(k), there(-k))
        message.start()
        sent.append(message)
        return message

    barrier = pltpu.get_barrier_semaphore()

    def greet(k):
        pl.semaphore_signal(
            barrier, inc=1, device_id={"gz": lax.rem(me + k, n)},
            device_id_type=pl.DeviceIdType.MESH,
        )

    def clear(ref):
        ref[...] = jnp.zeros(ref.shape, ref.dtype)

    for d in range(1, REACH2 + 1):
        for k in (d, -d):

            @pl.when(jnp.logical_not(there(k)))
            def _():
                for which in range(3):
                    clear(pk2.at[which, REACH2 + k])
                    if d <= REACH1:
                        clear(pk1.at[which, REACH1 + k])
                if d == 1:
                    rim = pl.ds(depth + own if k > 0 else 0, depth)
                    clear(mx.at[rim])
                    clear(fx.at[:, rim])
                    clear(gx.at[:, rim])

    loop(1, n, greet)

    src = fx.at[:, pl.ds(depth, own)]
    mat = mx.at[pl.ds(depth, own)]
    fetches = [
        pltpu.make_async_copy(a, b, in_sem.at[k])
        for k, (a, b) in enumerate(
            ((mat_in, raw_mat), (src_in, raw), (ords_in, ords), (ty_in, ty), (tx_in, tx))
        )
    ]
    for fetch in fetches:
        fetch.start()
    quarter = mat_in.shape[1] // 4
    quarters = split_rows(mat_in.shape[1])
    fetches[0].wait()
    for p in range(own):
        for at, row in quarters:
            mat[p, at : at + quarter] = raw_mat[p, pl.ds(row, quarter, stride=4)]

    for p in range(half):
        a = pick(mat[2 * p], SHIFT_TABLE)
        b = pick(mat[2 * p + 1], SHIFT_TABLE)
        for k in range(2):
            d1[k, p] = 0.125 * pair_rows(pair_lanes(a[k] + b[k], 1))
        pk1[0, REACH1, p] = pack_two(d1[0, p], d1[1, p])
    for k in range(2):
        d2[k] = 0.125 * pair_rows(pair_lanes(d1[k, 0] + d1[k, 1], 2))
    pk2[0, REACH2] = pack_four(d2[0], d2[1])

    for fetch in fetches[1:]:
        fetch.wait()
    for p in range(own):
        for at, row in quarters:
            for k in range(2):
                src[k, p, at : at + quarter] = raw[k, p, pl.ds(row, quarter, stride=4)]
    pl.semaphore_wait(barrier, n - 1)

    def send_planes(source, base, target, slot, near, dims, sides=(0, 1)):
        up_from = half if near else 0
        up_to = half if near else 0
        down_from = 0 if near else half
        down_to = depth + own + (0 if near else half)
        copies = []
        for which, (k, a, b) in enumerate(((1, up_from, up_to), (-1, down_from, down_to))):
            if which not in sides:
                continue
            s = pl.ds(base + a, half)
            t = pl.ds(b, half)
            one = source.at[:, s] if dims else source.at[s]
            two = target.at[:, t] if dims else target.at[t]
            copies.append(
                start(one, two, fine_send.at[slot + which], fine_recv.at[slot + which], k)
            )
        return copies

    def send_one(which, lo, hi):
        copies = {}
        for k in range(lo, hi + 1):
            for d in (k, -k):
                at = which * (2 * REACH1 + 1) + REACH1 - d
                part = pl.ds(0, half)
                if k == REACH1:
                    part = pl.ds(half - 1 if d > 0 else 0, 1)
                copies[-d] = start(
                    pk1.at[which, REACH1, part], pk1.at[which, REACH1 - d, part],
                    k1_send.at[at], k1_recv.at[at], d,
                )
        return copies

    def send_two(which):
        copies = {}
        for k in range(1, REACH2 + 1):
            for d in (k, -k):
                at = which * (2 * REACH2 + 1) + REACH2 - d
                copies[-d] = start(
                    pk2.at[which, REACH2], pk2.at[which, REACH2 - d],
                    k2_send.at[at], k2_recv.at[at], d,
                )
        return copies

    near_mat = send_planes(mx, depth, mx, 0, True, False)
    near_src = send_planes(fx, depth, fx, 2, True, True)
    shifts1 = send_one(0, 1, 1)
    shifts2 = {}

    def inside(plane, count):
        return jnp.where(jnp.logical_and(plane >= 0, plane < count), 1.0, 0.0).astype(F32)

    def weight0(p):
        m = inside(me * own + p - depth, n * own)
        r, i = pick(mx[p], WEIGHT_TABLE)
        return r * m, i * m

    def weight1(p):
        r, i = unpack_two(pk1[0, p // half, p % half])
        r, i = invert(r + 1.5, i)
        m = inside(me * half + p - mid1, n * half)
        return r * m, i * m

    def weight2(p):
        (rt, rb), (it, ib) = unpack_four(pk2[0, p])
        m = inside(me + p - REACH2, n)
        r, i = invert(jnp.concatenate([rt, rb]) + 0.375, jnp.concatenate([it, ib]))
        return r * m, i * m

    def take1(which):
        def body(p):
            return unpack_two(pk1[which, p // half, p % half])

        return body

    def take2(which):
        def body(p):
            (rt, rb), (it, ib) = unpack_four(pk2[which, p])
            return jnp.concatenate([rt, rb]), jnp.concatenate([it, ib])

        return body

    def cycle(which, f, near):
        begin, end = depth, depth + own
        if which == 1:
            planes(begin, end, FINE, w0, weight0)
        first_sweep(begin, end, FINE, va, f, w0)
        sweep(begin + 1, end - 1, FINE, vb, va, f, w0, 1, 1.0)
        if which == 1:
            for copy in near_mat:
                copy.wait_recv()
            planes(begin - 2, begin, FINE, w0, weight0)
            planes(end, end + 2, FINE, w0, weight0)
        for copy in near:
            copy.wait_recv()
        first_sweep(begin - 2, begin, FINE, va, f, w0)
        first_sweep(end, end + 2, FINE, va, f, w0)
        sweep(begin - 1, begin + 1, FINE, vb, va, f, w0, 1, 1.0)
        sweep(end - 1, end + 1, FINE, vb, va, f, w0, 1, 1.0)

        def down(q):
            total = [None, None]
            for s in range(2):
                p = depth + 2 * q + s
                c = pick(mx[p], DIAG_TABLE)
                dr, di = mul(c[0], c[1], vb[0, p], vb[1, p])
                for k, d in enumerate((dr, di)):
                    e = (f[k, p] - d) + around(vb, k, p, 1)
                    total[k] = e if s == 0 else total[k] + e
            parts = [
                0.125 * pair_rows(pair_lanes(t, 1)) for k, t in enumerate(total)
            ]
            f1[0, mid1 + q] = parts[0]
            f1[1, mid1 + q] = parts[1]
            pk1[which, REACH1, q] = pack_two(parts[0], parts[1])

        for q in range(half):
            down(q)
        ones = send_one(which, 1, 1)
        ones.update(send_one(which, 2, REACH1))
        if which == 1:
            shifts1.update(send_one(0, 2, REACH1))
            shifts2.update(send_two(0))

        if which == 1:
            for d in (-1, 1):
                shifts1[d].wait_recv()
            planes(mid1 - half, mid1 + 2 * half, MIDDLE, w1, weight1)

        for d in (-1, 1):
            ones[d].wait_recv()
        planes(mid1 - half, mid1, MIDDLE, f1, take1(which))
        planes(mid1 + half, mid1 + 2 * half, MIDDLE, f1, take1(which))
        first_sweep(mid1 - 2, mid1 + half + 2, MIDDLE, v1a, f1, w1)
        sweep(mid1 - 1, mid1 + half + 1, MIDDLE, v1b, v1a, f1, w1, 2, 0.25)

        parts = []
        total = [None, None]
        for q in range(half):
            p = mid1 + q
            dr, di = mul(d1[0, q] + 1.5, d1[1, q], v1b[0, p], v1b[1, p])
            for k, d in enumerate((dr, di)):
                e = (f1[k, p] - d) + 0.25 * around(v1b, k, p, 2)
                total[k] = e if q == 0 else total[k] + e
        parts = [0.125 * pair_rows(pair_lanes(t, 2)) for k, t in enumerate(total)]
        pk2[which, REACH2] = pack_four(parts[0], parts[1])
        twos = send_two(which)
        if which == 1:
            far_mat = send_planes(mx, depth, mx, 4, False, False)
        far = send_planes(f, depth, f, 4 + 2 * which, False, True)

        if which == 1:
            for d in range(2, REACH1 + 1):
                shifts1[d].wait_recv()
                shifts1[-d].wait_recv()
            planes(1, mid1 - half, MIDDLE, w1, weight1)
            planes(mid1 + 2 * half, 2 * mid1 + half - 1, MIDDLE, w1, weight1)
        for d in range(2, REACH1 + 1):
            ones[d].wait_recv()
            ones[-d].wait_recv()
        planes(1, mid1 - half, MIDDLE, f1, take1(which))
        planes(mid1 + 2 * half, 2 * mid1 + half - 1, MIDDLE, f1, take1(which))
        first_sweep(1, mid1 - 2, MIDDLE, v1a, f1, w1)
        first_sweep(mid1 + half + 2, 2 * mid1 + half - 1, MIDDLE, v1a, f1, w1)
        sweep(2, mid1 - 1, MIDDLE, v1b, v1a, f1, w1, 2, 0.25)
        sweep(mid1 + half + 1, 2 * mid1 + half - 2, MIDDLE, v1b, v1a, f1, w1, 2, 0.25)
        if which == 1:
            for d in range(1, REACH2 + 1):
                shifts2[d].wait_recv()
                shifts2[-d].wait_recv()
            planes(0, 2 * REACH2 + 1, COARSE, w2, weight2)

        for d in range(1, REACH2 + 1):
            twos[d].wait_recv()
            twos[-d].wait_recv()
        planes(0, 2 * REACH2 + 1, COARSE, f2, take2(which))
        first_sweep(0, 2 * REACH2 + 1, COARSE, v2a, f2, w2)
        sweep(1, 2 * REACH2, COARSE, v2b, v2a, f2, w2, 4, 0.0625)
        sweep(2, 2 * REACH2 - 1, COARSE, v2a, v2b, f2, w2, 4, 0.0625)
        sweep(3, 2 * REACH2 - 2, COARSE, v2b, v2a, f2, w2, 4, 0.0625)

        def raise1(c):
            p = (c - REACH2 + REACH1) * half
            for k in range(2):
                x = spread_rows(v2b[k, c])
                v1b[k, p] = v1b[k, p] + x
                v1b[k, p + 1] = v1b[k, p + 1] + x

        for c in range(REACH2 - 2, REACH2 + 3):
            raise1(c)
        sweep(mid1 - 3, mid1 + half + 3, MIDDLE, v1a, v1b, f1, w1, 2, 0.25)
        sweep(mid1 - 2, mid1 + half + 2, MIDDLE, v1b, v1a, f1, w1, 2, 0.25)

        if which == 1:
            for copy in far_mat:
                copy.wait_recv()
            planes(0, begin - 2, FINE, w0, weight0)
            planes(end + 2, end + depth, FINE, w0, weight0)
        for copy in far:
            copy.wait_recv()
        first_sweep(0, begin - 2, FINE, va, f, w0)
        first_sweep(end + 2, end + depth, FINE, va, f, w0)
        sweep(1, begin - 1, FINE, vb, va, f, w0, 1, 1.0)
        sweep(end + 1, end + depth - 1, FINE, vb, va, f, w0, 1, 1.0)

        def raise0(c):
            p = depth + 2 * (c - mid1)
            for k in range(2):
                x = spread_rows(v1b[k, c])
                vb[k, p] = vb[k, p] + x
                vb[k, p + 1] = vb[k, p + 1] + x

        for c in range(mid1 - 2, mid1 + half + 2):
            raise0(c)
        sweep(begin - 2, end + 2, FINE, va, vb, f, w0, 1, 1.0)
        sweep(begin - 1, end + 1, FINE, vb, va, f, w0, 1, 1.0)

    def image_of(p):
        c = pick(mx[p], IMAGE_TABLE)
        r, i = mul(c[0], c[1], vb[0, p], vb[1, p])
        return r - around(vb, 0, p, 1), i - around(vb, 1, p, 1)

    def fold(x):
        rows, lanes = x.shape
        return jnp.sum(x.reshape(rows // 8, 8, lanes), axis=0)

    def share(which, sums):
        rows = [jnp.sum(s, axis=0, keepdims=True) for s in sums]
        rows.append(jnp.zeros((4 - len(rows), rows[0].shape[1]), F32))
        red[which, me] = jnp.concatenate(rows, axis=0)

        def post(k):
            pltpu.make_async_remote_copy(
                src_ref=red.at[which, me], dst_ref=red.at[which, me],
                send_sem=red_send.at[which, k], recv_sem=red_recv.at[which, k],
                device_id={"gz": lax.rem(me + k, n)}, device_id_type=pl.DeviceIdType.MESH,
            ).start()

        loop(1, n, post)

    def collect(which):
        def await_one(k):
            one = pltpu.make_async_remote_copy(
                src_ref=red.at[which, me], dst_ref=red.at[which, lax.rem(me + n - k, n)],
                send_sem=red_send.at[which, k], recv_sem=red_recv.at[which, k],
                device_id={"gz": lax.rem(me + k, n)}, device_id_type=pl.DeviceIdType.MESH,
            )
            one.wait_recv()
            one.wait_send()

        loop(1, n, await_one)
        total = red[which, 0]
        for j in range(1, n):
            total = total + red[which, j]
        total = jnp.sum(total, axis=1, keepdims=True)
        return total[0:1], total[1:2], total[2:3]

    def spectrum(which):
        def post(k):
            pltpu.make_async_remote_copy(
                src_ref=spec.at[which], dst_ref=spec.at[which],
                send_sem=spec_send.at[which, k], recv_sem=spec_recv.at[which],
                device_id={"gz": lax.rem(me + k, n)}, device_id_type=pl.DeviceIdType.MESH,
            ).start()

        @pl.when(me == n - 1)
        def _():
            last = depth + own - 1
            spec[which] = spectrum_of(vb[0, last], vb[1, last], ty[...], tx[...])
            loop(1, n, post)

    def orders_of(which):
        def settle(k):
            pltpu.make_async_remote_copy(
                src_ref=spec.at[which], dst_ref=spec.at[which],
                send_sem=spec_send.at[which, k], recv_sem=spec_recv.at[which],
                device_id={"gz": lax.rem(me + k, n)}, device_id_type=pl.DeviceIdType.MESH,
            ).wait_send()

        @pl.when(me == n - 1)
        def _():
            loop(1, n, settle)

        @pl.when(me != n - 1)
        def _():
            pltpu.make_async_remote_copy(
                src_ref=spec.at[which], dst_ref=spec.at[which],
                send_sem=spec_send.at[which, 0], recv_sem=spec_recv.at[which],
                device_id={"gz": lax.rem(me + 1, n)}, device_id_type=pl.DeviceIdType.MESH,
            ).wait_recv()

        count = ords.shape[1]
        x = ords[0:1] + ORD_HALF
        y = ords[1:2] + ORD_HALF
        row = lax.broadcasted_iota(jnp.int32, (2 * HALF, count), 0)
        pick_y = lax.broadcasted_iota(jnp.int32, (HARM, count), 0) == y
        out = []
        for k in range(2):
            pick_x = jnp.where(row == x + k * HALF, 1.0, 0.0).astype(F32)
            chosen = precise(spec[which], pick_x, ((1,), (0,)))
            out.append(jnp.sum(jnp.where(pick_y, chosen, 0.0), axis=0, keepdims=True))
        return out

    cycle(1, fx, near_src)

    zero = jnp.zeros((8, fx.shape[3]), F32)
    sums = [zero, zero, zero]
    for p in range(own):
        r, i = image_of(depth + p)
        gx[0, depth + p] = r
        gx[1, depth + p] = i
        a, b = src[0, p], src[1, p]
        sums[0] = sums[0] + fold(a * a + b * b)
        sums[1] = sums[1] + fold(a * r + b * i)
        sums[2] = sums[2] + fold(a * i - b * r)
        if p == half - 1:
            near_img = send_planes(gx, depth, gx, 10, True, True, (1,))
    near_img += send_planes(gx, depth, gx, 10, True, True, (0,))
    share(0, sums)

    def keep(p):
        sol[0, p] = vb[0, depth + p]
        sol[1, p] = vb[1, depth + p]

    loop(0, own, keep)
    spectrum(0)

    cycle(2, gx, near_img)
    spectrum(1)

    rho, cr, ci = collect(0)
    scale = rho / (cr * cr + ci * ci)
    ar, ai = cr * scale, -(ci * scale)

    sums = [zero, zero, zero]
    for p in range(own):
        e = depth + p
        r, i = image_of(e)
        gr, gi = gx[0, e], gx[1, e]
        tr, ti = mul(ar, ai, gr, gi)
        hr, hi = src[0, p] - tr, src[1, p] - ti
        tr, ti = mul(ar, ai, r, i)
        lr, li = gr - tr, gi - ti
        va[0, e], va[1, e] = lr, li
        raw[0, p], raw[1, p] = hr, hi
        sums[0] = sums[0] + fold(lr * hr + li * hi)
        sums[1] = sums[1] + fold(lr * hi - li * hr)
        sums[2] = sums[2] + fold(lr * lr + li * li)
    share(1, sums)
    sdr, sdi = orders_of(0)

    for copy in sent:
        copy.wait_send()

    along_r, along_i, norm = collect(1)
    wr, wi = along_r / norm, along_i / norm

    def finish(p):
        e = depth + p
        dr, di = sol[0, p], sol[1, p]
        tr, ti = mul(ar, ai, vb[0, e], vb[1, e])
        cr_, ci_ = mul(wr, wi, dr - tr, di - ti)
        xr, xi = mul(ar, ai, dr, di)
        solved = (xr + cr_, xi + ci_)
        tr, ti = mul(wr, wi, va[0, e], va[1, e])
        left = (raw[0, p] - tr, raw[1, p] - ti)
        for k in range(2):
            for at, row in quarters:
                sol[k, p, pl.ds(row, quarter, stride=4)] = solved[k][at : at + quarter]
                res[k, p, pl.ds(row, quarter, stride=4)] = left[k][at : at + quarter]

    for p in range(own):
        finish(p)

    sqr, sqi = orders_of(1)
    tr, ti = mul(ar, ai, sqr, sqi)
    cr_, ci_ = mul(wr, wi, sdr - tr, sdi - ti)
    xr, xi = mul(ar, ai, sdr, sdi)
    pup[0:1] = xr + cr_
    pup[1:2] = xi + ci_


def on_device(n, source_term, material, orders):
    own, nx, ny = material.shape
    half = own // 2
    ty, tx = tables(nx, ny)
    vm = pltpu.VMEM
    fine = vm((2, 3 * own, nx, ny), F32)
    planes1 = (2 * REACH1 + 1) * half
    one = vm((2, planes1, nx // 2, ny), F32)
    planes2 = 2 * REACH2 + 1
    two = vm((2, planes2, nx // 4, ny), F32)
    dma = pltpu.SemaphoreType.DMA
    ext1 = 3 * (2 * REACH1 + 1)
    ext2 = 3 * planes2
    whole = pl.BlockSpec(memory_space=pltpu.VMEM)
    return pl.pallas_call(
        functools.partial(kernel, n),
        out_shape=(
            jax.ShapeDtypeStruct(source_term.shape, F32),
            jax.ShapeDtypeStruct(source_term.shape, F32),
            jax.ShapeDtypeStruct(orders.shape, F32),
        ),
        in_specs=[pl.BlockSpec(memory_space=pl.ANY)] * 5,
        out_specs=(whole,) * 3,
        scratch_shapes=[
            vm(orders.shape, jnp.int32), vm(ty.shape, F32), vm(tx.shape, F32), dma((5,)),
            fine, fine, vm((3 * own, nx, ny), jnp.int32), fine, fine, fine,
            vm((2, half, nx // 2, ny), F32), one, one, one, one,
            two, two, two, two, vm((2, nx // 4, ny), F32),
            vm((3, 2 * REACH1 + 1, half, nx // 2, ny), F32),
            vm((3, planes2, nx // 8, ny), F32),
            vm((2, own, nx, ny), F32),
            vm((own, nx, ny), jnp.int32),
            vm((2, n, 4, ny), F32),
            vm((2, HARM, 2 * HALF), F32),
            dma((12,)), dma((12,)), dma((ext1,)), dma((ext1,)), dma((ext2,)), dma((ext2,)),
            dma((2, n)), dma((2, n)), dma((2, n)), dma((2,)),
        ],
        compiler_params=pltpu.CompilerParams(
            collective_id=0, has_side_effects=True, vmem_limit_bytes=62 * 1024 * 1024
        ),
    )(source_term, material, orders, jnp.asarray(ty), jnp.asarray(tx))


def solution(mesh):
    return jax.shard_map(
        functools.partial(on_device, mesh.shape["gz"]),
        mesh=mesh,
        in_specs=(
            P(None, ("clip", "gz"), None, None),
            P(("clip", "gz"), None, None),
            P(None, "gz"),
        ),
        out_specs=(
            P(None, ("clip", "gz"), None, None),
            P(None, ("clip", "gz"), None, None),
            P(None, ("clip", "gz")),
        ),
        check_vma=False,
    )
```
